32 devices in a mesh: dp: 4 (over z), blk: 4 (over y, x), head: 2 (over core).
Axes of the slice: x: 2, y: 2, z: 4, core: 2. Of those that a mesh axis runs over, the one named last changes fastest.
Arguments:
- layer_input: bfloat16 [4, 2048, 768], P(None, ('dp', 'blk')), may hold values from -6 to 6
- sequence_lengths: int32 [4, 4, 3], P(None, 'dp'), may hold values from 0 to 512, as said below
- alibi_slopes: float32 [12], P('head'), may hold values from 0.0009765625 to 0.12
- project_weight: bfloat16 [768, 3, 768], P('dp', None, 'head'), may hold values from -0.21875 to 0.21875
- project_bias: float32 [2, 768], P(None, 'head'), may hold values from -1.75 to 1.75
- output_weight: bfloat16 [768, 768], P('head', 'dp'), may hold values from -0.875 to 0.875
- output_bias: float32 [768], replicated, may hold values from -1.75 to 1.75
- first_gain: float32 [768], replicated, may hold values from 0.25 to 1.75
- first_shift: float32 [768], replicated, may hold values from -1.75 to 1.75
- expand_weight: bfloat16 [768, 2, 3072], P('dp', None, 'head'), may hold values from -0.21875 to 0.21875
- expand_bias: float32 [2, 3072], P(None, 'head'), may hold values from -1.75 to 1.75
- down_weight: bfloat16 [3072, 768], P('head', 'dp'), may hold values from -0.15625 to 0.15625
- down_bias: float32 [768], replicated, may hold values from -1.75 to 1.75
- second_gain: float32 [768], replicated, may hold values from 0.25 to 1.75
- second_shift: float32 [768], replicated, may hold values from -1.75 to 1.75
- layer_cotangent: bfloat16 [4, 2048, 768], P(None, ('dp', 'blk')), may hold values from -6 to 6
Outputs:
- layer_output: bfloat16 [4, 2048, 768], P(None, ('dp', 'blk'))
- input_gradient: float32 [4, 2048, 768], P(None, ('dp', 'blk'))
- project_weight_gradient: float32 [768, 3, 768], P('dp', None, 'head')
- project_bias_gradient: float32 [2, 768], P(None, 'head')
- output_weight_gradient: float32 [768, 768], P('head', 'dp')
- output_bias_gradient: float32 [768], replicated
- first_gain_gradient: float32 [768], replicated
- first_shift_gradient: float32 [768], replicated
- expand_weight_gradient: float32 [768, 2, 3072], P('dp', None, 'head')
- expand_bias_gradient: float32 [2, 3072], P(None, 'head')
- down_weight_gradient: float32 [3072, 768], P('head', 'dp')
- down_bias_gradient: float32 [768], replicated
- second_gain_gradient: float32 [768], replicated
- second_shift_gradient: float32 [768], replicated
The draws below stay inside these ranges and needn't reach their ends.
Inputs may be any that keep to these rules, and one draw needn't show every extreme that they name: `sequence_lengths`: for each micro-batch and group, the three slots hold the lengths of one to three sequences laid end to end from the group's first token; used lengths are 128 or more and sum to 512; unused slots are 0 and follow the used ones; in every group some micro-batch holds a single sequence of 512 tokens.
All inputs are finite; a program needn't handle non-finite values.
Results may differ from the reference program's by a relative error of at most 0.025.
Values may be sent and summed in bfloat16 or wider, within the bound.
A program may use at most 128 MiB of HBM per device.

```python
import math
import jax
import jax.numpy as jnp
from jax import lax

D = 768
H = 12
HD = 64
FF = 3072
MB = 4
GROUP = 512
SEQ_MIN = 128
TOKENS = 2048
N_DP = 4


def draw_sequence_lengths(key, part):
    key = jax.random.fold_in(key, 7)
    count_key, first_key, second_key, whole_key = jax.random.split(key, 4)
    grid = (MB, N_DP)
    counts = jax.random.randint(count_key, grid, 1, 4)
    first = jax.random.randint(first_key, grid, SEQ_MIN, GROUP - 2 * SEQ_MIN + 1)
    second = jax.random.randint(second_key, grid, first + SEQ_MIN, GROUP - SEQ_MIN + 1)
    chosen = jax.random.randint(whole_key, (N_DP,), 0, MB)
    single = jnp.arange(MB)[:, None] == chosen[None, :]
    counts = jnp.where(single, 1, counts)
    leading = jnp.where(counts == 1, GROUP, first)
    middle = jnp.where(counts == 1, 0, jnp.where(counts == 2, GROUP - first, second - first))
    trailing = jnp.where(counts == 3, GROUP - second, 0)
    return jnp.stack([leading, middle, trailing], axis=-1).astype(jnp.int32)


def block_levels(stream_key, dims, cuts, least, high):
    def one(axis_at, blocks):
        heights = jax.random.uniform(jax.random.fold_in(jax.random.fold_in(stream_key, 6), axis_at), (blocks,), jnp.float32, least / len(cuts), high / len(cuts))
        return jnp.repeat(jnp.exp(heights), dims[axis_at] // blocks).reshape((-1,) + (1,) * (len(dims) - axis_at - 1))

    loudness = one(*cuts[0])
    for cut in cuts[1:]:
        loudness = loudness * one(*cut)
    return loudness


def centred(own_key, dims, scale, limit, cuts=(), kind=jnp.bfloat16):
    values = jax.random.normal(own_key, dims, jnp.float32) * scale
    if len(cuts) > 0:
        values = block_levels(own_key, dims, cuts, -0.22, 0.18) * values
    return jnp.clip(values, min=-limit, max=limit).astype(kind)


def setup_inputs(seed: int = 0) -> dict:
    key_of = jax.random.split(jax.random.key(seed), 17)
    layer_input = centred(key_of[0], (MB, TOKENS, D), 1.0, 6.0, ((1, 16),))
    sequence_lengths = draw_sequence_lengths(jax.random.fold_in(key_of[16], 71), 0)
    alibi_slopes = jnp.clip(jnp.exp(math.log(0.12) - 4.8112082 * jax.random.uniform(key_of[2], (H,), jnp.float32) ** block_levels(key_of[2], (H,), ((0, 2),), -0.2, 0.2)), 0.0009765625, 0.12)
    project_weight = centred(key_of[3], (D, 3, H * HD), D ** -0.5, 0.21875, ((0, 4), (2, 2)))
    project_bias = centred(key_of[4], (2, H * HD), 0.3, 1.75, ((1, 2),), jnp.float32)
    output_weight = centred(key_of[5], (H * HD, D), (H * HD // 16) ** -0.5, 0.875, ((0, 2), (1, 4)))
    output_bias = centred(key_of[6], (D,), 0.3, 1.75, (), jnp.float32)
    first_gain = jnp.clip(1.0 + 0.15 * jax.random.normal(key_of[7], (D,), jnp.float32), 0.25, 1.75)
    first_shift = centred(key_of[8], (D,), 0.3, 1.75, (), jnp.float32)
    expand_weight = centred(key_of[9], (D, 2, FF), D ** -0.5, 0.21875, ((0, 4), (2, 2)))
    expand_bias = centred(key_of[10], (2, FF), 0.3, 1.75, ((1, 2),), jnp.float32)
    down_weight = centred(key_of[11], (FF, D), (FF // 2) ** -0.5, 0.15625, ((0, 2), (1, 4)))
    down_bias = centred(key_of[12], (D,), 0.3, 1.75, (), jnp.float32)
    second_gain = jnp.clip(1.0 + 0.15 * jax.random.normal(key_of[13], (D,), jnp.float32), 0.25, 1.75)
    second_shift = centred(key_of[14], (D,), 0.3, 1.75, (), jnp.float32)
    layer_cotangent = centred(key_of[15], (MB, TOKENS, D), 1.0, 6.0, ((1, 16),))
    return {"layer_input": layer_input, "sequence_lengths": sequence_lengths, "alibi_slopes": alibi_slopes, "project_weight": project_weight, "project_bias": project_bias, "output_weight": output_weight, "output_bias": output_bias, "first_gain": first_gain, "first_shift": first_shift, "expand_weight": expand_weight, "expand_bias": expand_bias, "down_weight": down_weight, "down_bias": down_bias, "second_gain": second_gain, "second_shift": second_shift, "layer_cotangent": layer_cotangent}


EPSILON = 1e-12
MASKED = -1e+30
HIGHEST = lax.Precision.HIGHEST

@jax.custom_vjp
def low(v):
    return lax.optimization_barrier(v.astype(jnp.bfloat16)).astype(jnp.float32)

@jax.custom_vjp
def low_back(v):
    return v

def low_keep(v):
    return (low(v), None)

def low_pass(kept, grad):
    return (grad,)

def back_keep(v):
    return (v, None)

def back_low(kept, grad):
    return (low(grad),)
low.defvjp(low_keep, low_pass)
low_back.defvjp(back_keep, back_low)

def normalize(rows, gain, shift):
    mean = lax.optimization_barrier(jnp.mean(rows, axis=-1, keepdims=True))
    centered = rows - mean
    spread = lax.optimization_barrier(jnp.mean(centered * centered, axis=-1, keepdims=True))
    return centered * lax.rsqrt(spread + EPSILON) * gain + shift

def attend(query, keys, values, slopes, seq_ids):
    block = min(512, GROUP)
    count = GROUP // block
    positions = jnp.arange(GROUP, dtype=jnp.int32)

    def one_block(start):
        rows = lax.dynamic_slice_in_dim(query, start, block, 0)
        row_pos = start + jnp.arange(block, dtype=jnp.int32)
        row_seq = lax.dynamic_slice_in_dim(seq_ids, start, block, 0)
        scores = jnp.einsum('qhd,khd->hqk', rows, keys, precision=HIGHEST) * HD ** (-0.5)
        distance = jnp.abs(row_pos[:, None] - positions[None, :]).astype(jnp.float32)
        scores = low_back(scores - slopes[:, None, None] * distance[None])
        same = (row_seq[:, None] == seq_ids[None, :])[None]
        scores = jnp.where(same, scores, MASKED)
        weights = low(jax.nn.softmax(scores, axis=-1))
        return jnp.einsum('hqk,khd->qhd', weights, values, precision=HIGHEST)
    starts = jnp.arange(count, dtype=jnp.int32) * block
    return lax.map(jax.checkpoint(one_block), starts).reshape(GROUP, H, HD)

def layer_forward(inputs, params, slopes, lengths):
    project_weight, project_bias, output_weight, output_bias, first_gain, first_shift, expand_weight, expand_bias, down_weight, down_bias, second_gain, second_shift = params
    width = H * HD

    def one_group(operands):
        rows, group_lengths = operands
        positions = jnp.arange(GROUP, dtype=jnp.int32)
        seq_ids = (positions >= group_lengths[0]).astype(jnp.int32) + (positions >= group_lengths[0] + group_lengths[1]).astype(jnp.int32)
        mixed = jnp.dot(rows, project_weight.reshape(D, 3 * width), precision=HIGHEST)
        query = low(low_back(mixed[:, :width] + project_bias[0]))
        keys = low(low_back(mixed[:, width:2 * width]))
        values = low(low_back(mixed[:, 2 * width:] + project_bias[1]))
        context = attend(query.reshape(GROUP, H, HD), keys.reshape(GROUP, H, HD), values.reshape(GROUP, H, HD), slopes, seq_ids)
        context = low(low_back(context.reshape(GROUP, width)))
        branch = low_back(jnp.dot(context, output_weight, precision=HIGHEST) + output_bias)
        first = normalize(rows + branch, first_gain, first_shift)
        expanded = jnp.dot(low(first), expand_weight.reshape(D, 2 * FF), precision=HIGHEST) + expand_bias.reshape(2 * FF)
        gate_part = low_back(expanded[:, :FF])
        up_part = low_back(expanded[:, FF:])
        hidden = low(jax.nn.gelu(gate_part, approximate=False) * up_part)
        feed = low_back(jnp.dot(hidden, down_weight, precision=HIGHEST) + down_bias)
        return normalize(first + feed, second_gain, second_shift)
    groups = inputs.reshape(MB * N_DP, GROUP, D)
    group_lengths = lengths.reshape(MB * N_DP, 3)
    result = lax.map(jax.checkpoint(one_group), (groups, group_lengths))
    return result.reshape(MB, N_DP * GROUP, D)

def reference(layer_input, sequence_lengths, alibi_slopes, project_weight, project_bias, output_weight, output_bias, first_gain, first_shift, expand_weight, expand_bias, down_weight, down_bias, second_gain, second_shift, layer_cotangent):
    params = (project_weight, project_bias, output_weight, output_bias, first_gain, first_shift, expand_weight, expand_bias, down_weight, down_bias, second_gain, second_shift)
    floats = tuple((item.astype(jnp.float32) for item in params))
    slopes = alibi_slopes.astype(jnp.float32)

    def forward(inputs, *weights):
        return layer_forward(inputs, weights, slopes, sequence_lengths)
    result, pull = jax.vjp(forward, layer_input.astype(jnp.float32), *floats)
    grads = pull(layer_cotangent.astype(jnp.float32))
    return (result.astype(jnp.bfloat16), grads[0], grads[1], grads[2], grads[3], grads[4], grads[5], grads[6], grads[7], grads[8], grads[9], grads[10], grads[11], grads[12])
```

```python
import math

import jax
import jax.numpy as jnp
from jax import lax
from jax.experimental import pallas as pl
from jax.experimental.pallas import tpu as pltpu
from jax.sharding import PartitionSpec as P

EPSILON = 1e-12
MASKED = -1e30


def shifted(value, axis, steps):
    count = lax.axis_size(axis)
    pairs = [(source, (source + steps) % count) for source in range(count)]
    return lax.ppermute(value, axis, pairs)


def normalize(rows, gain, shift):
    mean = jnp.mean(rows, axis=-1, keepdims=True)
    centered = rows - mean
    spread = jnp.mean(centered * centered, axis=-1, keepdims=True)
    return centered * lax.rsqrt(spread + EPSILON) * gain + shift


def gelu_product(gate_part, up_part):
    return jax.nn.gelu(gate_part, approximate=False) * up_part


def sequence_ids(lengths, positions):
    first = lengths[:, 0:1]
    second = first + lengths[:, 1:2]
    later = (positions[None, :] >= first).astype(jnp.int32)
    return later + (positions[None, :] >= second).astype(jnp.int32)


def block_scores(query, keys, slopes, query_pos, key_pos, query_seq, key_seq):
    scale = query.shape[-1] ** (-0.5)
    raw = jnp.einsum("mqhd,mkhd->mhqk", query, keys, preferred_element_type=jnp.float32)
    distance = jnp.abs(query_pos[:, None] - key_pos[None, :]).astype(jnp.float32)
    scores = raw * scale - slopes[None, :, None, None] * distance[None, None]
    same = (query_seq[:, :, None] == key_seq[:, None, :])[:, None]
    return (jnp.where(same, scores, MASKED), same)


def forward_update(state, query, keys, values, slopes, query_pos, key_pos, query_seq, key_seq):
    top, total, accum = state
    scores, same = block_scores(query, keys, slopes, query_pos, key_pos, query_seq, key_seq)
    new_top = jnp.maximum(top, jnp.max(scores, axis=-1))
    weights = jnp.where(same, jnp.exp(scores - new_top[..., None]), 0.0)
    factor = jnp.exp(top - new_top)
    total = total * factor + jnp.sum(weights, axis=-1)
    update = jnp.einsum(
        "mhqk,mkhd->mqhd", weights.astype(jnp.bfloat16), values, preferred_element_type=jnp.float32
    )
    accum = accum * jnp.transpose(factor, (0, 2, 1))[..., None] + update
    return (new_top, total, accum)


def over_blocks(function, state, arrays, start):
    count_rows = arrays[0].shape[1]
    block = math.gcd(count_rows, 512)
    if block == count_rows:
        return function(state, arrays, start)

    def step(index, carry):
        offset = index * block
        blocks = tuple((lax.dynamic_slice_in_dim(item, offset, block, 1) for item in arrays))
        return function(carry, blocks, start + offset)

    return lax.fori_loop(0, count_rows // block, step, state)


def general(
    layer_input,
    sequence_lengths,
    alibi_slopes,
    project_weight,
    project_bias,
    output_weight,
    output_bias,
    first_gain,
    first_shift,
    expand_weight,
    expand_bias,
    down_weight,
    down_bias,
    second_gain,
    second_shift,
    layer_cotangent,
):
    batches, tokens, width = layer_input.shape
    heads = alibi_slopes.shape[0]
    local_width = project_weight.shape[2]
    head_size = local_width // heads
    units = expand_weight.shape[2]
    rows_all = batches * tokens
    scale = head_size ** (-0.5)
    project_full, output_full, expand_full, down_full = (
        lax.all_gather(project_weight, "dp", axis=0, tiled=True),
        lax.all_gather(output_weight, "dp", axis=1, tiled=True),
        lax.all_gather(expand_weight, "dp", axis=0, tiled=True),
        lax.all_gather(down_weight, "dp", axis=1, tiled=True),
    )
    lengths = sequence_lengths.reshape(batches, 3)
    cycle_index = lax.axis_index("blk")
    cycle_size = lax.axis_size("blk")
    own_pos = cycle_index * tokens + jnp.arange(tokens, dtype=jnp.int32)
    own_seq = sequence_ids(lengths, own_pos)

    def split_heads(item):
        return item.reshape(item.shape[0], item.shape[1], heads, head_size)

    flat_input = layer_input.reshape(rows_all, width)
    mixed = jnp.dot(
        flat_input, project_full.reshape(width, 3 * local_width), preferred_element_type=jnp.float32
    )
    query = (
        (mixed[:, :local_width] + project_bias[0])
        .astype(jnp.bfloat16)
        .reshape(batches, tokens, local_width)
    )
    keys = (
        mixed[:, local_width : 2 * local_width]
        .astype(jnp.bfloat16)
        .reshape(batches, tokens, local_width)
    )
    values = (
        (mixed[:, 2 * local_width :] + project_bias[1])
        .astype(jnp.bfloat16)
        .reshape(batches, tokens, local_width)
    )
    query_heads = split_heads(query)
    initial = (
        jnp.full((batches, heads, tokens), MASKED, jnp.float32),
        jnp.zeros((batches, heads, tokens), jnp.float32),
        jnp.zeros((batches, tokens, heads, head_size), jnp.float32),
    )

    def inner(carry, blocks, block_start):
        key_pos = block_start + jnp.arange(blocks[0].shape[1], dtype=jnp.int32)
        key_seq = sequence_ids(lengths, key_pos)
        return forward_update(
            carry,
            query_heads,
            split_heads(blocks[0]),
            split_heads(blocks[1]),
            alibi_slopes,
            own_pos,
            key_pos,
            own_seq,
            key_seq,
        )

    top, total, accum = over_blocks(
        inner,
        initial,
        (
            lax.all_gather(keys, "blk", axis=1, tiled=True),
            lax.all_gather(values, "blk", axis=1, tiled=True),
        ),
        jnp.int32(0),
    )
    context = accum / jnp.transpose(total, (0, 2, 1))[..., None]
    log_total = top + jnp.log(total)
    context_low = context.astype(jnp.bfloat16).reshape(rows_all, local_width)
    branch_part = jnp.dot(context_low, output_full, preferred_element_type=jnp.float32)
    branch = lax.psum(branch_part.astype(jnp.bfloat16), "head").astype(jnp.float32) + output_bias
    first_in = flat_input.astype(jnp.float32) + branch
    first_out, first_pull = jax.vjp(normalize, first_in, first_gain, first_shift)
    first_low = first_out.astype(jnp.bfloat16)
    expanded = jnp.dot(
        first_low, expand_full.reshape(width, 2 * units), preferred_element_type=jnp.float32
    )
    expanded = expanded + expand_bias.reshape(2 * units)
    hidden_act, gelu_pull = jax.vjp(gelu_product, expanded[:, :units], expanded[:, units:])
    hidden_low = hidden_act.astype(jnp.bfloat16)
    feed_part = jnp.dot(hidden_low, down_full, preferred_element_type=jnp.float32)
    feed = lax.psum(feed_part.astype(jnp.bfloat16), "head").astype(jnp.float32) + down_bias
    second_in = first_out + feed
    result, second_pull = jax.vjp(normalize, second_in, second_gain, second_shift)
    layer_output = result.astype(jnp.bfloat16).reshape(batches, tokens, width)
    grad_result = layer_cotangent.reshape(rows_all, width).astype(jnp.float32)
    grad_second, second_gain_grad, second_shift_grad = second_pull(grad_result)
    grad_feed = grad_second.astype(jnp.bfloat16)
    down_bias_grad = jnp.sum(grad_feed.astype(jnp.float32), axis=0)
    down_part = jnp.einsum("rf,rd->fd", hidden_low, grad_feed, preferred_element_type=jnp.float32)
    grad_hidden = jnp.einsum("rd,fd->rf", grad_feed, down_full, preferred_element_type=jnp.float32)
    grad_gate, grad_up = gelu_pull(grad_hidden)
    grad_expanded = jnp.concatenate([grad_gate, grad_up], axis=1).astype(jnp.bfloat16)
    expand_bias_grad = jnp.sum(grad_expanded.astype(jnp.float32), axis=0).reshape(2, units)
    expand_part = jnp.einsum(
        "rd,rf->df", first_low, grad_expanded, preferred_element_type=jnp.float32
    ).reshape(width, 2, units)
    first_back = jnp.einsum(
        "rf,df->rd",
        grad_expanded,
        expand_full.reshape(width, 2 * units),
        preferred_element_type=jnp.float32,
    )
    grad_first = grad_second + lax.psum(first_back.astype(jnp.bfloat16), "head").astype(jnp.float32)
    grad_first_in, first_gain_grad, first_shift_grad = first_pull(grad_first)
    grad_branch = grad_first_in.astype(jnp.bfloat16)
    output_bias_grad = jnp.sum(grad_branch.astype(jnp.float32), axis=0)
    output_part = jnp.einsum(
        "rc,rd->cd", context_low, grad_branch, preferred_element_type=jnp.float32
    )
    grad_context = jnp.einsum(
        "rd,cd->rc", grad_branch, output_full, preferred_element_type=jnp.float32
    )
    grad_context = grad_context.astype(jnp.bfloat16).reshape(batches, tokens, local_width)
    grad_heads = split_heads(grad_context)
    delta_rows = jnp.sum(grad_heads.astype(jnp.float32) * context, axis=-1)
    delta_heads = jnp.transpose(delta_rows, (0, 2, 1))
    zeros_heads = jnp.zeros((batches, tokens, heads, head_size), jnp.float32)
    zeros_flat = jnp.zeros((batches, tokens, local_width), jnp.float32)

    def cycle_step(carry, anchor):
        keys_now, values_now, grad_keys_now, grad_values_now, grad_query = carry
        key_pos = anchor * tokens + jnp.arange(tokens, dtype=jnp.int32)
        key_seq = sequence_ids(lengths, key_pos)
        keys_block = split_heads(keys_now)
        values_block = split_heads(values_now)
        scores, same = block_scores(
            query_heads, keys_block, alibi_slopes, own_pos, key_pos, own_seq, key_seq
        )
        weights = jnp.where(same, jnp.exp(scores - log_total[..., None]), 0.0)
        grad_prob = jnp.einsum(
            "mqhd,mkhd->mhqk", grad_heads, values_block, preferred_element_type=jnp.float32
        )
        grad_score = (weights * (grad_prob - delta_heads[..., None])).astype(jnp.bfloat16)
        grad_query = (
            grad_query
            + jnp.einsum(
                "mhqk,mkhd->mqhd", grad_score, keys_block, preferred_element_type=jnp.float32
            )
            * scale
        )
        key_term = (
            jnp.einsum(
                "mhqk,mqhd->mkhd", grad_score, query_heads, preferred_element_type=jnp.float32
            )
            * scale
        )
        value_term = jnp.einsum(
            "mhqk,mqhd->mkhd",
            weights.astype(jnp.bfloat16),
            grad_heads,
            preferred_element_type=jnp.float32,
        )
        grad_keys_now = grad_keys_now + key_term.reshape(grad_keys_now.shape)
        grad_values_now = grad_values_now + value_term.reshape(grad_values_now.shape)
        return (keys_now, values_now, grad_keys_now, grad_values_now, grad_query)

    def cycle_turn(index, carry):
        anchor = (cycle_index - index) % cycle_size
        updated = cycle_step(carry, anchor)
        moved = (
            shifted(updated[0], "blk", 1),
            shifted(updated[1], "blk", 1),
            shifted(updated[2].astype(jnp.bfloat16), "blk", 1).astype(jnp.float32),
            shifted(updated[3].astype(jnp.bfloat16), "blk", 1).astype(jnp.float32),
        )
        return (
            moved[0],
            moved[1],
            moved[2].astype(jnp.float32),
            moved[3].astype(jnp.float32),
            updated[4],
        )

    carry = lax.fori_loop(
        0, cycle_size - 1, cycle_turn, (keys, values, zeros_flat, zeros_flat, zeros_heads)
    )
    final = cycle_step(carry, (cycle_index + 1) % cycle_size)
    returned = (
        shifted(final[2].astype(jnp.bfloat16), "blk", 1).astype(jnp.float32),
        shifted(final[3].astype(jnp.bfloat16), "blk", 1).astype(jnp.float32),
    )
    grad_keys = returned[0].astype(jnp.float32)
    grad_values = returned[1].astype(jnp.float32)
    grad_query = final[4].reshape(batches, tokens, local_width)
    grad_mixed = jnp.concatenate(
        [
            grad_query.reshape(rows_all, local_width),
            grad_keys.reshape(rows_all, local_width),
            grad_values.reshape(rows_all, local_width),
        ],
        axis=1,
    ).astype(jnp.bfloat16)
    project_bias_grad = jnp.stack(
        [
            jnp.sum(grad_mixed[:, :local_width].astype(jnp.float32), axis=0),
            jnp.sum(grad_mixed[:, 2 * local_width :].astype(jnp.float32), axis=0),
        ]
    )
    project_part = jnp.einsum(
        "rd,rc->dc", flat_input, grad_mixed, preferred_element_type=jnp.float32
    ).reshape(width, 3, local_width)
    input_back = jnp.einsum(
        "rc,dc->rd",
        grad_mixed,
        project_full.reshape(width, 3 * local_width),
        preferred_element_type=jnp.float32,
    )
    input_gradient = grad_first_in + lax.psum(input_back.astype(jnp.bfloat16), "head").astype(
        jnp.float32
    )
    shards = (
        lax.psum_scatter(
            project_part.astype(jnp.bfloat16), "dp", scatter_dimension=0, tiled=True
        ).astype(jnp.float32),
        lax.psum_scatter(
            output_part.astype(jnp.bfloat16), "dp", scatter_dimension=1, tiled=True
        ).astype(jnp.float32),
        lax.psum_scatter(
            expand_part.astype(jnp.bfloat16), "dp", scatter_dimension=0, tiled=True
        ).astype(jnp.float32),
        lax.psum_scatter(
            down_part.astype(jnp.bfloat16), "dp", scatter_dimension=1, tiled=True
        ).astype(jnp.float32),
    )
    totals = (
        lax.psum(shards[0].astype(jnp.bfloat16), "blk").astype(jnp.float32),
        lax.psum(shards[1].astype(jnp.bfloat16), "blk").astype(jnp.float32),
        lax.psum(shards[2].astype(jnp.bfloat16), "blk").astype(jnp.float32),
        lax.psum(shards[3].astype(jnp.bfloat16), "blk").astype(jnp.float32),
    )
    small = lax.psum(
        (
            project_bias_grad,
            output_bias_grad,
            first_gain_grad,
            first_shift_grad,
            expand_bias_grad,
            down_bias_grad,
            second_gain_grad,
            second_shift_grad,
        ),
        ("dp", "blk"),
    )
    return (
        layer_output,
        input_gradient.reshape(batches, tokens, width),
        totals[0],
        small[0],
        totals[1],
        small[1],
        small[2],
        small[3],
        totals[2],
        small[4],
        totals[3],
        small[5],
        small[6],
        small[7],
    )


MESH = pl.DeviceIdType.MESH
BF = jnp.bfloat16
F32 = jnp.float32
FAR = 1e33
VMEM_BYTES = 63 << 20


def dot(a, b):
    return lax.dot_general(a, b, (((1,), (0,)), ((), ())), preferred_element_type=F32)


def dot_nt(a, b):
    return lax.dot_general(a, b, (((1,), (1,)), ((), ())), preferred_element_type=F32)


def dot_tn(a, b):
    return lax.dot_general(a, b, (((0,), (0,)), ((), ())), preferred_element_type=F32)


def column_sum(rows):
    return jnp.sum(rows, axis=0, keepdims=True)


def row_mean(rows):
    return jnp.mean(rows, axis=-1, keepdims=True)


def standardize(rows):
    centered = rows - row_mean(rows)
    inverse = lax.rsqrt(row_mean(centered * centered) + EPSILON)
    return centered * inverse, inverse


def standardize_back(grad, normal, inverse):
    return inverse * (grad - row_mean(grad) - normal * row_mean(grad * normal))


def layer_kernel(
    x_ref, cot_ref, wa_ref, wf_ref, pack_ref, len_ref,
    out_ref, ig_ref, ga_ref, gf_ref, sm_ref,
    x_full, first_full, feed_full, branch_full,
    w_attn, w_gu, w_down, packs,
    part, r1x, r1y, r2,
    q_s, k_s, v_s, g_s, p_s, ctx_s, ctx_cat, dqkv, ds_s, dq_s, far_s,
    act_s, upd_s, hid_s, dgu_s, eb_acc,
    first_own, n1_s, a1_s, gr2_s, gr1_s,
    dwf, dwf_in, zf_in, dwa, dwa_in, zf_a, fin_a,
    sm_acc, sm_in, slope_s,
    ag_ss, ag_rs, rs_ss, rs_rs, pk_sem, wa_ss, wa_rs, wf_ss, wf_rs, wl_sem, wc_ss, wc_rs,
    gc_ss, gc_rs, gz_ss, gz_rs, gp_ss, gp_rs, sm_ss, sm_rs, io_ss, io_rs,
):
    z, b, c = lax.axis_index("dp"), lax.axis_index("blk"), lax.axis_index("head")
    half, odd = b // 2, b % 2
    xor = jnp.bitwise_xor
    other = 1 - c
    sib = (z, b, other)
    xdev, ydev, ddev = ((z, xor(b, k), c) for k in (1, 2, 3))
    bx, by, bd = xor(b, 1), xor(b, 2), xor(b, 3)
    T = x_ref.shape[1]
    D = x_ref.shape[2]
    H2 = D // 2
    ROWS = 4 * T
    DZ = wa_ref.shape[1]
    UB = wf_ref.shape[2] // 4

    def remote(src, dst, ss, rs, dev):
        return pltpu.make_async_remote_copy(
            src_ref=src, dst_ref=dst, send_sem=ss, recv_sem=rs, device_id=dev, device_id_type=MESH
        )

    def chunk(index, size):
        return pl.ds(pl.multiple_of(index * size, size), size)

    partners = [(z, xor(b, k), cc) for k in (1, 2, 3) for cc in (c, other)] + [sib]
    partners += [(xor(z, k), b, cc) for k in (1, 2, 3) for cc in (c, other)]
    barrier = pltpu.get_barrier_semaphore()
    for dev in partners:
        pl.semaphore_signal(barrier, inc=1, device_id=dev, device_id_type=MESH)
    pl.semaphore_wait(barrier, len(partners))

    class Gather:
        def __init__(self, full, phase, m):
            ss, rs = ag_ss.at[phase, m], ag_rs.at[phase, m]
            own, sx, sy = m * 4 + b, m * 4 + bx, m * 4 + by
            lo, hi = pl.ds(0, H2), pl.ds(H2, H2)
            self.cx = remote(full.at[own], full.at[own], ss.at[0], rs.at[0], xdev)
            self.cy = remote(full.at[own], full.at[own], ss.at[1], rs.at[1], ydev)
            self.fx = remote(full.at[sx, :, lo], full.at[sx, :, lo], ss.at[2], rs.at[2], ydev)
            self.fy = remote(full.at[sy, :, hi], full.at[sy, :, hi], ss.at[3], rs.at[3], xdev)

        def start(self):
            self.cx.start()
            self.cy.start()

        def mid(self):
            self.cx.wait_recv()
            self.fx.start()
            self.cy.wait_recv()
            self.fy.start()

        def end(self):
            self.fx.wait_recv()
            self.fy.wait_recv()

        def drain(self):
            for copy in (self.cx, self.cy, self.fx, self.fy):
                copy.wait_send()

    class Scatter:
        def __init__(self, phase, m):
            ss, rs = rs_ss.at[phase, m], rs_rs.at[phase, m]
            buf = part.at[phase % 2]
            lo, hi = pl.ds(0, H2), pl.ds(H2, H2)
            self.phase, self.m, self.buf = phase, m, buf
            own, sx, sy, sd = m * 4 + b, m * 4 + bx, m * 4 + by, m * 4 + bd
            self.own, self.sx, self.sy = own, sx, sy
            ix, iy, i2 = r1x.at[phase, m], r1y.at[phase, m], r2.at[phase, m]
            self.ix, self.iy, self.i2 = ix, iy, i2
            self.xd = remote(buf.at[sd, :, lo], ix.at[1], ss.at[0], rs.at[0], xdev)
            self.yd = remote(buf.at[sd, :, hi], iy.at[1], ss.at[1], rs.at[1], ydev)
            self.xo = remote(buf.at[sx, :, lo], ix.at[0], ss.at[2], rs.at[2], xdev)
            self.yo = remote(buf.at[sy, :, hi], iy.at[0], ss.at[3], rs.at[3], ydev)
            self.y2 = remote(buf.at[sy, :, lo], i2.at[0], ss.at[4], rs.at[4], ydev)
            self.x2 = remote(buf.at[sx, :, hi], i2.at[1], ss.at[5], rs.at[5], xdev)

        def start(self):
            for copy in (self.xd, self.yd, self.xo, self.yo):
                copy.start()

        def mid(self):
            buf = self.buf
            self.xd.wait_recv()
            buf[self.sy, :, :H2] = (
                buf[self.sy, :, :H2].astype(F32) + self.ix[1].astype(F32)
            ).astype(BF)
            self.y2.start()
            self.yd.wait_recv()
            buf[self.sx, :, H2:] = (
                buf[self.sx, :, H2:].astype(F32) + self.iy[1].astype(F32)
            ).astype(BF)
            self.x2.start()

        def end(self):
            for copy in (self.xo, self.yo, self.y2, self.x2):
                copy.wait_recv()
            mine = self.buf[self.own].astype(F32)
            low = mine[:, :H2] + self.ix[0].astype(F32) + self.i2[0].astype(F32)
            high = mine[:, H2:] + self.iy[0].astype(F32) + self.i2[1].astype(F32)
            return jnp.concatenate([low, high], axis=1)

        def drain(self):
            for copy in (self.xd, self.yd, self.xo, self.yo, self.y2, self.x2):
                copy.wait_send()

    gather_x = [Gather(x_full, 0, m) for m in (0, 1)]
    gather_first = [Gather(first_full, 1, m) for m in (0, 1)]
    gather_feed = [Gather(feed_full, 2, m) for m in (0, 1)]
    gather_branch = [Gather(branch_full, 3, m) for m in (0, 1)]
    sum_branch = [Scatter(0, m) for m in (0, 1)]
    sum_feed = [Scatter(1, m) for m in (0, 1)]
    sum_first = [Scatter(2, m) for m in (0, 1)]
    sum_input = [Scatter(3, m) for m in (0, 1)]

    for m in (0, 1):
        x_full[m * 4 + b] = x_ref[2 * c + m]
    gather_x[0].start()

    mine_z = chunk(z, DZ)
    attn_copies = []
    for kind in range(4):
        src = wa_ref.at[kind, :, pl.ds(pl.multiple_of(odd * 128, 128), 256)]
        dst = w_attn.at[mine_z, pl.ds(kind * 256, 256)]
        row = [
            remote(src, dst, wa_ss.at[dz, kind], wa_rs.at[dz, kind], (xor(z, dz), b, kind // 2))
            for dz in (1, 2, 3)
        ]
        cross = remote(src, dst, wa_ss.at[0, kind], wa_rs.at[0, kind], sib)
        local = pltpu.make_async_copy(src, dst, wl_sem.at[kind])
        attn_copies.append((row, cross, local))
    pack_copy = remote(pack_ref, packs.at[c], pk_sem.at[0], pk_sem.at[1], sib)
    pack_copy.start()
    packs[c] = pack_ref[...]

    @pl.when(c == half)
    def _():
        for kind in range(4):
            row, cross, local = attn_copies[kind]
            for copy in row:
                copy.start()
            for core in (0, 1):
                if kind // 2 == core:

                    @pl.when(c == core)
                    def _():
                        local.start()

                    @pl.when(c != core)
                    def _():
                        cross.start()

    gather_x[1].start()

    ffn_copies = []
    for kind in range(3):
        src = wf_ref.at[kind, :, chunk(b, UB)]
        if kind < 2:
            dst = w_gu.at[c, mine_z, pl.ds(kind * UB, UB)]
        else:
            dst = w_down.at[mine_z, chunk(c, UB)]
        row = [
            remote(src, dst, wf_ss.at[dz, kind], wf_rs.at[dz, kind], (xor(z, dz), b, c))
            for dz in (1, 2, 3)
        ]
        local = pltpu.make_async_copy(src, dst, wl_sem.at[4 + kind])
        ffn_copies.append((row, local))
        for copy in row:
            copy.start()
        local.start()

    positions = lax.broadcasted_iota(jnp.int32, (ROWS, ROWS), 0)
    key_positions = lax.broadcasted_iota(jnp.int32, (ROWS, ROWS), 1)
    for m in (0, 1):
        start_one = len_ref[(2 * c + m) * 3]
        start_two = start_one + len_ref[(2 * c + m) * 3 + 1]
        for rb in range(4):
            rows = lax.broadcasted_iota(jnp.int32, (T, ROWS), 0) + rb * T
            cols = lax.broadcasted_iota(jnp.int32, (T, ROWS), 1)
            seq_r = (rows >= start_one).astype(jnp.int32) + (rows >= start_two).astype(jnp.int32)
            seq_c = (cols >= start_one).astype(jnp.int32) + (cols >= start_two).astype(jnp.int32)
            distance = jnp.abs(rows - cols).astype(F32)
            far_s[m, pl.ds(rb * T, T), :] = jnp.where(seq_r == seq_c, distance, FAR)
    sm_acc[...] = jnp.zeros_like(sm_acc)
    eb_acc[...] = jnp.zeros_like(eb_acc)

    gather_x[0].mid()
    gather_x[1].mid()
    pack_copy.wait_recv()

    def small(row):
        return packs[c, pl.ds(row, 1), pl.ds(0, D)]

    for kind in range(4):
        row, cross, local = attn_copies[kind]

        @pl.when(c == kind // 2)
        def _():
            for copy in row:
                copy.wait_recv()

            @pl.when(c == half)
            def _():
                local.wait()

            @pl.when(c != half)
            def _():
                cross.wait_recv()

    pair = w_attn.at[:, chunk(c, 512)]
    attn_share = remote(pair, pair, wc_ss.at[0], wc_rs.at[0], sib)
    attn_share.start()
    attn_share.wait_recv()

    def pick(cols):
        return [
            jnp.where(odd == 0, cols[:, i * 64 : i * 64 + 64], cols[:, i * 64 + 64 : i * 64 + 128])
            for i in range(3)
        ]

    def place(heads):
        zero = jnp.zeros_like(heads[0])
        return jnp.concatenate(
            [
                jnp.where(odd == 0, heads[0], zero),
                jnp.where(odd == 0, heads[1], heads[0]),
                jnp.where(odd == 0, heads[2], heads[1]),
                jnp.where(odd == 0, zero, heads[2]),
            ],
            axis=1,
        )

    bias_cols = pl.ds(pl.multiple_of(odd * 128, 128), 256)

    def project(m):
        query_bias = packs[half, 2:3, bias_cols]
        value_bias = packs[half, 3:4, bias_cols]

        def rows_of(t, _):
            rows = x_full[pl.ds(m * 4 + t * 2, 2)].reshape(2 * T, D)
            at = pl.ds(pl.multiple_of(t * 2 * T, 2 * T), 2 * T)
            mixed = dot(rows, w_attn[:, 0:768])
            query = (mixed[:, 0:256] + query_bias).astype(BF) * jnp.asarray(0.125, BF)
            keys = mixed[:, 256:512].astype(BF)
            values = (mixed[:, 512:768] + value_bias).astype(BF)
            for i, item in enumerate(pick(query)):
                q_s[m * 3 + i, at, :] = item
            for i, item in enumerate(pick(keys)):
                k_s[m * 3 + i, at, :] = item
            for i, item in enumerate(pick(values)):
                v_s[m * 3 + i, at, :] = item
            return 0

        lax.fori_loop(0, 2, rows_of, 0)

    for i in range(3):
        low, high = packs[half, 10 + i : 11 + i, 0:128], packs[half, 13 + i : 14 + i, 0:128]
        slope_s[i] = jnp.broadcast_to(jnp.where(odd == 0, low, high), (8, 128))

    def slope_of(i):
        return slope_s[i][0:1, 0:1]

    def attend(m):
        def one(index, _):
            i, rb = index // 4, index % 4
            at = chunk(rb, T)
            h = m * 3 + i
            scores = dot_nt(q_s[h, at, :], k_s[h])
            scores = scores - slope_of(i) * far_s[m, at, :]
            top = jnp.max(scores, axis=-1, keepdims=True)
            weights = jnp.exp(scores - top)
            total = jnp.sum(weights, axis=-1, keepdims=True)
            probs = (weights * (1.0 / total)).astype(BF)
            p_s[h, at, :] = probs
            ctx_s[h, at, :] = dot(probs, v_s[h])
            return 0

        lax.fori_loop(0, 12, one, 0)

    def put_part(buf, m, t, rows):
        buf[pl.ds(m * 4 + 2 * t, 2)] = rows.astype(BF).reshape(2, T, D)

    def branch(m):
        def rows_of(t, _):
            at = pl.ds(pl.multiple_of(t * 2 * T, 2 * T), 2 * T)
            cat = place([ctx_s[m * 3 + i, at, :].astype(BF) for i in range(3)])
            ctx_cat[m, at, :] = cat
            put_part(sum_branch[m].buf, m, t, dot_nt(cat, w_attn[:, 768:1024]))
            return 0

        lax.fori_loop(0, 2, rows_of, 0)

    def first_norm(m):
        rows = x_ref[2 * c + m].astype(F32) + sum_branch[m].end() + small(4)
        normal, inverse = standardize(rows)
        first = normal * small(5) + small(6)
        n1_s[m], a1_s[m] = normal, inverse
        first_own[m] = first
        first_full[m * 4 + b] = first.astype(BF)

    def feed_forward(m):
        def rows_of(t, _):
            at = pl.ds(pl.multiple_of(m * ROWS + t * 2 * T, 2 * T), 2 * T)
            rows = first_full[pl.ds(m * 4 + t * 2, 2)].reshape(2 * T, D)
            for g in (0, 1):
                cols = pl.ds(g * UB, UB)
                bias = packs[g, 0:2, chunk(b, UB)]
                both = dot(rows, w_gu[g])
                gate = both[:, :UB] + bias[0:1]
                up = both[:, UB:] + bias[1:2]
                cdf = 0.5 + 0.5 * lax.erf(gate * 0.7071067811865476)
                act = gate * cdf
                slope = cdf + gate * (jnp.exp(-0.5 * gate * gate) * 0.3989422804014327)
                hid_s[at, cols] = (act * up).astype(BF)
                act_s[at, cols] = act.astype(BF)
                upd_s[at, cols] = (up * slope).astype(BF)
            put_part(sum_feed[m].buf, m, t, dot_nt(hid_s[at, :], w_down[...]))
            return 0

        lax.fori_loop(0, 2, rows_of, 0)

    def add_small(row, rows):
        sm_acc[row : row + 1, :] += column_sum(rows)

    def second_norm(m):
        rows = first_own[m] + sum_feed[m].end() + small(7)
        normal, inverse = standardize(rows)
        out_ref[2 * c + m] = (normal * small(8) + small(9)).astype(BF)
        grad = cot_ref[2 * c + m].astype(F32)
        add_small(4, grad * normal)
        add_small(5, grad)
        back = standardize_back(grad * small(8), normal, inverse)
        gr2_s[m] = back
        low = back.astype(BF)
        feed_full[m * 4 + b] = low
        add_small(3, low.astype(F32))

    def feed_backward(m):
        def rows_of(t, _):
            at = pl.ds(pl.multiple_of(m * ROWS + t * 2 * T, 2 * T), 2 * T)
            rows = feed_full[pl.ds(m * 4 + t * 2, 2)].reshape(2 * T, D)
            hidden = dot(rows, w_down[...])
            dgate = (hidden * upd_s[at, :].astype(F32)).astype(BF)
            dup = (hidden * act_s[at, :].astype(F32)).astype(BF)
            for g in (0, 1):
                cols = slice(g * UB, g * UB + UB)
                dgu_s[g, at, 0:UB] = dgate[:, cols]
                dgu_s[g, at, UB : 2 * UB] = dup[:, cols]
                eb_acc[2 * g : 2 * g + 1, :] += column_sum(dgate[:, cols].astype(F32))
                eb_acc[2 * g + 1 : 2 * g + 2, :] += column_sum(dup[:, cols].astype(F32))
            back = dot_nt(dgu_s[0, at, :], w_gu[0]) + dot_nt(dgu_s[1, at, :], w_gu[1])
            put_part(sum_first[m].buf, m, t, back)
            return 0

        lax.fori_loop(0, 2, rows_of, 0)

    def feed_weights():
        def cols_of(t, _):
            at = chunk(t, 256)
            rows = first_full[:, :, at].reshape(2 * ROWS, 256)
            for g in (0, 1):
                dwf[g, at, 0 : 2 * UB] = dot_tn(rows, dgu_s[g]).astype(BF)
            rows = feed_full[:, :, at].reshape(2 * ROWS, 256)
            down = dot_tn(rows, hid_s[...]).astype(BF)
            for g in (0, 1):
                dwf[g, at, 2 * UB : 3 * UB] = down[:, g * UB : g * UB + UB]
            return 0

        lax.fori_loop(0, D // 256, cols_of, 0)

    def first_back(m):
        grad = gr2_s[m] + sum_first[m].end()
        normal = n1_s[m]
        add_small(1, grad * normal)
        add_small(2, grad)
        back = standardize_back(grad * small(5), normal, a1_s[m])
        gr1_s[m] = back
        low = back.astype(BF)
        branch_full[m * 4 + b] = low
        add_small(0, low.astype(F32))

    def context_back(m):
        def rows_of(t, _):
            at = pl.ds(pl.multiple_of(t * 2 * T, 2 * T), 2 * T)
            rows = branch_full[pl.ds(m * 4 + t * 2, 2)].reshape(2 * T, D)
            grads = dot(rows, w_attn[:, 768:1024]).astype(BF)
            for i, item in enumerate(pick(grads)):
                g_s[m * 3 + i, at, :] = item
            return 0

        lax.fori_loop(0, 2, rows_of, 0)

    def attend_back(m):
        def one(i, _):
            h = m * 3 + i
            query, keys, values, grads = q_s[h], k_s[h], v_s[h], g_s[h]

            def block(rb, _):
                at = chunk(rb, T)
                rows = g_s[h, at, :]
                delta = jnp.sum(rows.astype(F32) * ctx_s[h, at, :], axis=-1, keepdims=True)
                probs = p_s[h, at, :].astype(F32)
                score = (probs * (dot_nt(rows, v_s[h]) - delta)).astype(BF)
                ds_s[at, :] = score
                dq_s[0, i, at, :] = (dot(score, k_s[h]) * 0.125).astype(BF)
                return 0

            lax.fori_loop(0, 4, block, 0)
            dq_s[1, i] = dot_tn(query, ds_s[...]).T.astype(BF)
            dq_s[2, i] = dot_tn(grads, p_s[h]).T.astype(BF)
            return 0

        lax.fori_loop(0, 3, one, 0)
        for kind in range(3):
            cat = place([dq_s[kind, i] for i in range(3)])
            dqkv[m, :, kind * 256 : kind * 256 + 256] = cat
            if kind != 1:
                lanes = pl.ds(pl.multiple_of(half * H2 + odd * 128, 128), 256)
                row = 14 + kind // 2
                sm_acc[row : row + 1, lanes] += column_sum(cat.astype(F32))

    def input_back(m):
        def rows_of(t, _):
            at = pl.ds(pl.multiple_of(t * 2 * T, 2 * T), 2 * T)
            put_part(sum_input[m].buf, m, t, dot_nt(dqkv[m, at, :], w_attn[:, 0:768]))
            return 0

        lax.fori_loop(0, 2, rows_of, 0)

    def attend_weights():
        def cols_of(t, _):
            at = chunk(t, 256)
            rows = x_full[:, :, at].reshape(2 * ROWS, 256)
            grads = dot_tn(rows, dqkv[...].reshape(2 * ROWS, 768)).astype(BF)
            dwa[0, at, :] = grads[:, 0:512]
            dwa[1, at, 0:256] = grads[:, 512:768]
            rows = branch_full[:, :, at].reshape(2 * ROWS, 256)
            dwa[1, at, 256:512] = dot_tn(rows, ctx_cat[...].reshape(2 * ROWS, 256)).astype(BF)
            return 0

        lax.fori_loop(0, D // 256, cols_of, 0)

    class Reduce:
        def __init__(self, index, buf, incoming, zin):
            self.buf, self.incoming, self.zin = buf, incoming, zin
            self.swap = remote(buf.at[other], incoming, gc_ss.at[index], gc_rs.at[index], sib)
            self.push = [
                remote(
                    buf.at[c, chunk(xor(z, dz), DZ), :],
                    zin.at[dz - 1],
                    gz_ss.at[index, dz - 1],
                    gz_rs.at[index, dz - 1],
                    (xor(z, dz), b, c),
                )
                for dz in (1, 2, 3)
            ]

        def join(self):
            self.swap.wait_recv()

            def rows_of(t, _):
                at = chunk(t, DZ)
                mine = self.buf[c, at, :].astype(F32)
                self.buf[c, at, :] = (mine + self.incoming[at, :].astype(F32)).astype(BF)
                return 0

            lax.fori_loop(0, D // DZ, rows_of, 0)
            for copy in self.push:
                copy.start()

        def total(self):
            for copy in self.push:
                copy.wait_recv()
            value = self.buf[c, chunk(z, DZ), :].astype(F32)
            for dz in (0, 1, 2):
                value = value + self.zin[dz].astype(F32)
            return value.astype(BF)

        def drain(self):
            self.swap.wait_send()
            for copy in self.push:
                copy.wait_send()

    reduce_feed = Reduce(0, dwf, dwf_in, zf_in)
    reduce_attn = Reduce(1, dwa, dwa_in, zf_a)

    gather_x[0].end()
    project(0)
    attend(0)
    branch(0)
    sum_branch[0].start()
    gather_x[1].end()
    project(1)
    sum_branch[0].mid()
    attend(1)
    branch(1)
    sum_branch[1].start()
    first_norm(0)
    gather_first[0].start()
    for row, local in ffn_copies:
        for copy in row:
            copy.wait_recv()
        local.wait()
    share_gu = remote(w_gu.at[c], w_gu.at[c], wc_ss.at[1], wc_rs.at[1], sib)
    lanes = w_down.at[:, chunk(c, UB)]
    share_down = remote(lanes, lanes, wc_ss.at[2], wc_rs.at[2], sib)
    share_gu.start()
    share_down.start()
    sum_branch[1].mid()
    gather_first[0].mid()
    first_norm(1)
    gather_first[1].start()
    share_gu.wait_recv()
    share_down.wait_recv()
    gather_first[0].end()
    feed_forward(0)
    sum_feed[0].start()
    gather_first[1].mid()
    gather_first[1].end()
    sum_feed[0].mid()
    feed_forward(1)
    sum_feed[1].start()
    second_norm(0)
    gather_feed[0].start()
    sum_feed[1].mid()
    gather_feed[0].mid()
    second_norm(1)
    gather_feed[1].start()
    out_copies = [
        remote(out_ref.at[2 * c + m], out_ref.at[2 * c + m], io_ss.at[0, m], io_rs.at[0, m], sib)
        for m in (0, 1)
    ]
    for copy in out_copies:
        copy.start()
    gather_feed[0].end()
    sum_branch[0].drain()
    feed_backward(0)
    sum_first[0].start()
    gather_feed[1].mid()
    gather_feed[1].end()
    sum_first[0].mid()
    sum_branch[1].drain()
    feed_backward(1)
    sum_first[1].start()
    first_back(0)
    gather_branch[0].start()
    feed_weights()
    reduce_feed.swap.start()
    sum_first[1].mid()
    gather_branch[0].mid()
    first_back(1)
    gather_branch[1].start()
    reduce_feed.join()
    gather_branch[0].end()
    context_back(0)
    attend_back(0)
    sum_feed[0].drain()
    input_back(0)
    sum_input[0].start()
    gather_branch[1].mid()
    gather_branch[1].end()
    context_back(1)
    sum_input[0].mid()
    attend_back(1)
    sum_feed[1].drain()
    input_back(1)
    sum_input[1].start()
    attend_weights()
    reduce_attn.swap.start()

    gf_ref[b] = reduce_feed.total()
    feed_out = [
        remote(gf_ref.at[b], gf_ref.at[b], gp_ss.at[0, k - 1], gp_rs.at[0, k - 1], (z, xor(b, k), c))
        for k in (1, 2, 3)
    ]
    for copy in feed_out:
        copy.start()
    reduce_attn.join()

    for g in (0, 1):
        for kind in (0, 1):
            row = 6 + (2 * g + kind) * 2
            values = eb_acc[2 * g + kind : 2 * g + kind + 1, :]
            for h in (0, 1):
                sm_acc[row + h : row + h + 1, chunk(odd, UB)] = jnp.where(half == h, values, 0.0)
    sm_copies = []
    steps = [sib, xdev, ydev, (xor(z, 1), b, c), (xor(z, 2), b, c)]
    sm_in[0] = sm_acc[...]
    for index, dev in enumerate(steps):
        copy = remote(sm_in.at[2 * index], sm_in.at[2 * index + 1], sm_ss.at[index], sm_rs.at[index], dev)
        copy.start()
        copy.wait_recv()
        sm_copies.append(copy)
        value = sm_in[2 * index] + sm_in[2 * index + 1]
        if index + 1 < len(steps):
            sm_in[2 * index + 2] = value
        else:
            sm_ref[...] = value

    ig_copies = []
    for m in (0, 1):
        if m == 1:
            sum_input[1].mid()
        ig_ref[2 * c + m] = gr1_s[m] + sum_input[m].end()
        copy = remote(ig_ref.at[2 * c + m], ig_ref.at[2 * c + m], io_ss.at[1, m], io_rs.at[1, m], sib)
        copy.start()
        ig_copies.append(copy)

    fin_a[...] = reduce_attn.total()
    slot = ga_ref.at[odd, c]
    attn_out = [
        remote(fin_a, slot, gp_ss.at[1, k], gp_rs.at[1 + odd, c], (z, xor(b, k), half))
        for k in (1, 2, 3)
    ]
    for copy in attn_out:
        copy.start()
    attn_cross = remote(fin_a, slot, gp_ss.at[1, 0], gp_rs.at[1 + odd, c], sib)

    @pl.when(c != half)
    def _():
        attn_cross.start()

    @pl.when(c == half)
    def _():
        ga_ref[odd, c] = fin_a[...]

    for parity in (0, 1):
        for core in (0, 1):
            mine = jnp.logical_and(c == half, jnp.logical_and(odd == parity, c == core))

            @pl.when(jnp.logical_not(mine))
            def _():
                remote(
                    fin_a, ga_ref.at[parity, core], gp_ss.at[1, 0], gp_rs.at[1 + parity, core], sib
                ).wait_recv()

    @pl.when(c != half)
    def _():
        attn_cross.wait_send()

    for copy in attn_out + sm_copies + [pack_copy, attn_share, share_gu, share_down]:
        copy.wait_send()
    for copy in feed_out + out_copies + ig_copies:
        copy.wait()

    @pl.when(c == half)
    def _():
        for kind in range(4):
            row, cross, local = attn_copies[kind]
            for copy in row:
                copy.wait_send()

            @pl.when(c != kind // 2)
            def _():
                cross.wait_send()

    for row, local in ffn_copies:
        for copy in row:
            copy.wait_send()
    for item in gather_x + gather_first + gather_feed + gather_branch + sum_first + sum_input:
        item.drain()
    reduce_feed.drain()
    reduce_attn.drain()


def planes(
    layer_input,
    sequence_lengths,
    alibi_slopes,
    project_weight,
    project_bias,
    output_weight,
    output_bias,
    first_gain,
    first_shift,
    expand_weight,
    expand_bias,
    down_weight,
    down_bias,
    second_gain,
    second_shift,
    layer_cotangent,
):
    batches, tokens, width = layer_input.shape
    units = expand_weight.shape[2]
    shard = project_weight.shape[0]
    half_width = project_weight.shape[2]
    heads = alibi_slopes.shape[0]
    rows = 4 * tokens
    part_units = units // 4
    wa = jnp.concatenate([jnp.transpose(project_weight, (1, 0, 2)), output_weight.T[None]], axis=0)
    wf = jnp.concatenate([jnp.transpose(expand_weight, (1, 0, 2)), down_weight.T[None]], axis=0)

    def padded(item):
        return jnp.pad(item, ((0, 0), (0, units - item.shape[1])))

    vectors = jnp.stack([output_bias, first_gain, first_shift, down_bias, second_gain, second_shift])
    pack = jnp.concatenate(
        [
            expand_bias,
            padded(project_bias),
            padded(vectors),
            jnp.broadcast_to(alibi_slopes[:, None], (heads, units)),
        ],
        axis=0,
    )
    lengths = sequence_lengths.reshape(batches * 3)
    vmem = pl.BlockSpec(memory_space=pltpu.VMEM)
    hbm = pl.BlockSpec(memory_space=pl.ANY)
    smem = pl.BlockSpec(memory_space=pltpu.SMEM)
    dma = pltpu.SemaphoreType.DMA
    full = pltpu.VMEM((8, tokens, width), BF)
    outs = pl.pallas_call(
        layer_kernel,
        out_shape=(
            jax.ShapeDtypeStruct((batches, tokens, width), BF),
            jax.ShapeDtypeStruct((batches, tokens, width), F32),
            jax.ShapeDtypeStruct((2, 2, shard, 512), BF),
            jax.ShapeDtypeStruct((4, shard, 3 * part_units), BF),
            jax.ShapeDtypeStruct((16, width), F32),
        ),
        in_specs=[vmem, vmem, hbm, hbm, vmem, smem],
        out_specs=(vmem, vmem, vmem, vmem, vmem),
        scratch_shapes=[
            full, full, full, full,
            pltpu.VMEM((width, 1024), BF),
            pltpu.VMEM((2, width, 2 * part_units), BF),
            pltpu.VMEM((width, 2 * part_units), BF),
            pltpu.VMEM((2,) + pack.shape, F32),
            pltpu.VMEM((2, 8, tokens, width), BF),
            pltpu.VMEM((4, 2, 2, tokens, width // 2), BF),
            pltpu.VMEM((4, 2, 2, tokens, width // 2), BF),
            pltpu.VMEM((4, 2, 2, tokens, width // 2), BF),
            pltpu.VMEM((6, rows, 64), BF),
            pltpu.VMEM((6, rows, 64), BF),
            pltpu.VMEM((6, rows, 64), BF),
            pltpu.VMEM((6, rows, 64), BF),
            pltpu.VMEM((6, rows, rows), BF),
            pltpu.VMEM((6, rows, 64), F32),
            pltpu.VMEM((2, rows, 256), BF),
            pltpu.VMEM((2, rows, 768), BF),
            pltpu.VMEM((rows, rows), BF),
            pltpu.VMEM((3, 3, rows, 64), BF),
            pltpu.VMEM((2, rows, rows), F32),
            pltpu.VMEM((2 * rows, 2 * part_units), BF),
            pltpu.VMEM((2 * rows, 2 * part_units), BF),
            pltpu.VMEM((2 * rows, 2 * part_units), BF),
            pltpu.VMEM((2, 2 * rows, 2 * part_units), BF),
            pltpu.VMEM((8, part_units), F32),
            pltpu.VMEM((2, tokens, width), F32),
            pltpu.VMEM((2, tokens, width), F32),
            pltpu.VMEM((2, tokens, 1), F32),
            pltpu.VMEM((2, tokens, width), F32),
            pltpu.VMEM((2, tokens, width), F32),
            pltpu.VMEM((2, width, 3 * part_units), BF),
            pltpu.VMEM((width, 3 * part_units), BF),
            pltpu.VMEM((3, shard, 3 * part_units), BF),
            pltpu.VMEM((2, width, 512), BF),
            pltpu.VMEM((width, 512), BF),
            pltpu.VMEM((3, shard, 512), BF),
            pltpu.VMEM((shard, 512), BF),
            pltpu.VMEM((16, width), F32),
            pltpu.VMEM((10, 16, width), F32),
            pltpu.VMEM((3, 8, 128), F32),
            dma((4, 2, 4)), dma((4, 2, 4)),
            dma((4, 2, 6)), dma((4, 2, 6)),
            dma((2,)),
            dma((4, 4)), dma((4, 4)),
            dma((4, 3)), dma((4, 3)),
            dma((8,)),
            dma((3,)), dma((3,)),
            dma((2,)), dma((2,)),
            dma((2, 3)), dma((2, 3)),
            dma((2, 4)), dma((3, 3)),
            dma((5,)), dma((5,)),
            dma((2, 2)), dma((2, 2)),
        ],
        compiler_params=pltpu.CompilerParams(
            collective_id=0, has_side_effects=True, vmem_limit_bytes=VMEM_BYTES
        ),
        name="encoder_layer",
    )(layer_input, layer_cotangent, wa, wf, pack, lengths)
    layer_output, input_gradient, attn, feed, sums = outs
    core = lax.axis_index("head")
    even, odd = attn[0], attn[1]
    low = jnp.concatenate([even[:, :, 0:192], odd[:, :, 64:256]], axis=2)
    high = jnp.concatenate([even[:, :, 256:448], odd[:, :, 320:512]], axis=2)
    project_grad = jnp.stack([low[0], high[0], low[1]], axis=1).astype(F32)
    output_grad = high[1].T.astype(F32)
    feed = feed.reshape(4, shard, 3, part_units)
    feed = jnp.transpose(feed, (1, 2, 0, 3)).reshape(shard, 3, units)
    expand_grad = feed[:, 0:2].astype(F32)
    down_grad = feed[:, 2].T.astype(F32)
    bias_rows = lax.dynamic_slice_in_dim(sums[6:14].reshape(2, 2, units), core, 1, 0)[0]
    project_bias_grad = lax.dynamic_slice_in_dim(sums[14:16], core * half_width, half_width, 1)
    return (
        layer_output,
        input_gradient,
        project_grad,
        project_bias_grad,
        output_grad,
        sums[0],
        sums[1],
        sums[2],
        expand_grad,
        bias_rows,
        down_grad,
        sums[3],
        sums[4],
        sums[5],
    )


def fits(mesh):
    shape = dict(mesh.shape)
    return shape["dp"] == 4 and shape["blk"] == 4 and shape["head"] == 2


def solution(mesh):
    in_specs = (
        P(None, ("dp", "blk"), None),
        P(None, "dp", None),
        P("head"),
        P("dp", None, "head"),
        P(None, "head"),
        P("head", "dp"),
        P(),
        P(),
        P(),
        P("dp", None, "head"),
        P(None, "head"),
        P("head", "dp"),
        P(),
        P(),
        P(),
        P(None, ("dp", "blk"), None),
    )
    out_specs = (
        P(None, ("dp", "blk"), None),
        P(None, ("dp", "blk"), None),
        P("dp", None, "head"),
        P(None, "head"),
        P("head", "dp"),
        P(),
        P(),
        P(),
        P("dp", None, "head"),
        P(None, "head"),
        P("head", "dp"),
        P(),
        P(),
        P(),
    )
    body = planes if fits(mesh) else general
    return jax.shard_map(body, mesh=mesh, in_specs=in_specs, out_specs=out_specs, check_vma=False)
```

```python
import functools
import math

import jax
import jax.numpy as jnp
from jax import lax
from jax.experimental import pallas as pl
from jax.experimental.pallas import tpu as pltpu
from jax.sharding import PartitionSpec as P

EPSILON = 1e-12
MASKED = -1e30


def shifted(value, axis, steps):
    count = lax.axis_size(axis)
    pairs = [(source, (source + steps) % count) for source in range(count)]
    return lax.ppermute(value, axis, pairs)


def normalize(rows, gain, shift):
    mean = jnp.mean(rows, axis=-1, keepdims=True)
    centered = rows - mean
    spread = jnp.mean(centered * centered, axis=-1, keepdims=True)
    return centered * lax.rsqrt(spread + EPSILON) * gain + shift


def gelu_product(gate_part, up_part):
    return jax.nn.gelu(gate_part, approximate=False) * up_part


def sequence_ids(lengths, positions):
    first = lengths[:, 0:1]
    second = first + lengths[:, 1:2]
    later = (positions[None, :] >= first).astype(jnp.int32)
    return later + (positions[None, :] >= second).astype(jnp.int32)


def block_scores(query, keys, slopes, query_pos, key_pos, query_seq, key_seq):
    scale = query.shape[-1] ** (-0.5)
    raw = jnp.einsum("mqhd,mkhd->mhqk", query, keys, preferred_element_type=jnp.float32)
    distance = jnp.abs(query_pos[:, None] - key_pos[None, :]).astype(jnp.float32)
    scores = raw * scale - slopes[None, :, None, None] * distance[None, None]
    same = (query_seq[:, :, None] == key_seq[:, None, :])[:, None]
    return (jnp.where(same, scores, MASKED), same)


def forward_update(state, query, keys, values, slopes, query_pos, key_pos, query_seq, key_seq):
    top, total, accum = state
    scores, same = block_scores(query, keys, slopes, query_pos, key_pos, query_seq, key_seq)
    new_top = jnp.maximum(top, jnp.max(scores, axis=-1))
    weights = jnp.where(same, jnp.exp(scores - new_top[..., None]), 0.0)
    factor = jnp.exp(top - new_top)
    total = total * factor + jnp.sum(weights, axis=-1)
    update = jnp.einsum(
        "mhqk,mkhd->mqhd", weights.astype(jnp.bfloat16), values, preferred_element_type=jnp.float32
    )
    accum = accum * jnp.transpose(factor, (0, 2, 1))[..., None] + update
    return (new_top, total, accum)


def over_blocks(function, state, arrays, start):
    count_rows = arrays[0].shape[1]
    block = math.gcd(count_rows, 512)
    if block == count_rows:
        return function(state, arrays, start)

    def step(index, carry):
        offset = index * block
        blocks = tuple((lax.dynamic_slice_in_dim(item, offset, block, 1) for item in arrays))
        return function(carry, blocks, start + offset)

    return lax.fori_loop(0, count_rows // block, step, state)


def general(
    layer_input,
    sequence_lengths,
    alibi_slopes,
    project_weight,
    project_bias,
    output_weight,
    output_bias,
    first_gain,
    first_shift,
    expand_weight,
    expand_bias,
    down_weight,
    down_bias,
    second_gain,
    second_shift,
    layer_cotangent,
):
    batches, tokens, width = layer_input.shape
    heads = alibi_slopes.shape[0]
    local_width = project_weight.shape[2]
    head_size = local_width // heads
    units = expand_weight.shape[2]
    rows_all = batches * tokens
    scale = head_size ** (-0.5)
    project_full, output_full, expand_full, down_full = (
        lax.all_gather(project_weight, "dp", axis=0, tiled=True),
        lax.all_gather(output_weight, "dp", axis=1, tiled=True),
        lax.all_gather(expand_weight, "dp", axis=0, tiled=True),
        lax.all_gather(down_weight, "dp", axis=1, tiled=True),
    )
    lengths = sequence_lengths.reshape(batches, 3)
    cycle_index = lax.axis_index("blk")
    cycle_size = lax.axis_size("blk")
    own_pos = cycle_index * tokens + jnp.arange(tokens, dtype=jnp.int32)
    own_seq = sequence_ids(lengths, own_pos)

    def split_heads(item):
        return item.reshape(item.shape[0], item.shape[1], heads, head_size)

    flat_input = layer_input.reshape(rows_all, width)
    mixed = jnp.dot(
        flat_input, project_full.reshape(width, 3 * local_width), preferred_element_type=jnp.float32
    )
    query = (
        (mixed[:, :local_width] + project_bias[0])
        .astype(jnp.bfloat16)
        .reshape(batches, tokens, local_width)
    )
    keys = (
        mixed[:, local_width : 2 * local_width]
        .astype(jnp.bfloat16)
        .reshape(batches, tokens, local_width)
    )
    values = (
        (mixed[:, 2 * local_width :] + project_bias[1])
        .astype(jnp.bfloat16)
        .reshape(batches, tokens, local_width)
    )
    query_heads = split_heads(query)
    initial = (
        jnp.full((batches, heads, tokens), MASKED, jnp.float32),
        jnp.zeros((batches, heads, tokens), jnp.float32),
        jnp.zeros((batches, tokens, heads, head_size), jnp.float32),
    )

    def inner(carry, blocks, block_start):
        key_pos = block_start + jnp.arange(blocks[0].shape[1], dtype=jnp.int32)
        key_seq = sequence_ids(lengths, key_pos)
        return forward_update(
            carry,
            query_heads,
            split_heads(blocks[0]),
            split_heads(blocks[1]),
            alibi_slopes,
            own_pos,
            key_pos,
            own_seq,
            key_seq,
        )

    top, total, accum = over_blocks(
        inner,
        initial,
        (
            lax.all_gather(keys, "blk", axis=1, tiled=True),
            lax.all_gather(values, "blk", axis=1, tiled=True),
        ),
        jnp.int32(0),
    )
    context = accum / jnp.transpose(total, (0, 2, 1))[..., None]
    log_total = top + jnp.log(total)
    context_low = context.astype(jnp.bfloat16).reshape(rows_all, local_width)
    branch_part = jnp.dot(context_low, output_full, preferred_element_type=jnp.float32)
    branch = lax.psum(branch_part.astype(jnp.bfloat16), "head").astype(jnp.float32) + output_bias
    first_in = flat_input.astype(jnp.float32) + branch
    first_out, first_pull = jax.vjp(normalize, first_in, first_gain, first_shift)
    first_low = first_out.astype(jnp.bfloat16)
    expanded = jnp.dot(
        first_low, expand_full.reshape(width, 2 * units), preferred_element_type=jnp.float32
    )
    expanded = expanded + expand_bias.reshape(2 * units)
    hidden_act, gelu_pull = jax.vjp(gelu_product, expanded[:, :units], expanded[:, units:])
    hidden_low = hidden_act.astype(jnp.bfloat16)
    feed_part = jnp.dot(hidden_low, down_full, preferred_element_type=jnp.float32)
    feed = lax.psum(feed_part.astype(jnp.bfloat16), "head").astype(jnp.float32) + down_bias
    second_in = first_out + feed
    result, second_pull = jax.vjp(normalize, second_in, second_gain, second_shift)
    layer_output = result.astype(jnp.bfloat16).reshape(batches, tokens, width)
    grad_result = layer_cotangent.reshape(rows_all, width).astype(jnp.float32)
    grad_second, second_gain_grad, second_shift_grad = second_pull(grad_result)
    grad_feed = grad_second.astype(jnp.bfloat16)
    down_bias_grad = jnp.sum(grad_feed.astype(jnp.float32), axis=0)
    down_part = jnp.einsum("rf,rd->fd", hidden_low, grad_feed, preferred_element_type=jnp.float32)
    grad_hidden = jnp.einsum("rd,fd->rf", grad_feed, down_full, preferred_element_type=jnp.float32)
    grad_gate, grad_up = gelu_pull(grad_hidden)
    grad_expanded = jnp.concatenate([grad_gate, grad_up], axis=1).astype(jnp.bfloat16)
    expand_bias_grad = jnp.sum(grad_expanded.astype(jnp.float32), axis=0).reshape(2, units)
    expand_part = jnp.einsum(
        "rd,rf->df", first_low, grad_expanded, preferred_element_type=jnp.float32
    ).reshape(width, 2, units)
    first_back = jnp.einsum(
        "rf,df->rd",
        grad_expanded,
        expand_full.reshape(width, 2 * units),
        preferred_element_type=jnp.float32,
    )
    grad_first = grad_second + lax.psum(first_back.astype(jnp.bfloat16), "head").astype(jnp.float32)
    grad_first_in, first_gain_grad, first_shift_grad = first_pull(grad_first)
    grad_branch = grad_first_in.astype(jnp.bfloat16)
    output_bias_grad = jnp.sum(grad_branch.astype(jnp.float32), axis=0)
    output_part = jnp.einsum(
        "rc,rd->cd", context_low, grad_branch, preferred_element_type=jnp.float32
    )
    grad_context = jnp.einsum(
        "rd,cd->rc", grad_branch, output_full, preferred_element_type=jnp.float32
    )
    grad_context = grad_context.astype(jnp.bfloat16).reshape(batches, tokens, local_width)
    grad_heads = split_heads(grad_context)
    delta_rows = jnp.sum(grad_heads.astype(jnp.float32) * context, axis=-1)
    delta_heads = jnp.transpose(delta_rows, (0, 2, 1))
    zeros_heads = jnp.zeros((batches, tokens, heads, head_size), jnp.float32)
    zeros_flat = jnp.zeros((batches, tokens, local_width), jnp.float32)

    def cycle_step(carry, anchor):
        keys_now, values_now, grad_keys_now, grad_values_now, grad_query = carry
        key_pos = anchor * tokens + jnp.arange(tokens, dtype=jnp.int32)
        key_seq = sequence_ids(lengths, key_pos)
        keys_block = split_heads(keys_now)
        values_block = split_heads(values_now)
        scores, same = block_scores(
            query_heads, keys_block, alibi_slopes, own_pos, key_pos, own_seq, key_seq
        )
        weights = jnp.where(same, jnp.exp(scores - log_total[..., None]), 0.0)
        grad_prob = jnp.einsum(
            "mqhd,mkhd->mhqk", grad_heads, values_block, preferred_element_type=jnp.float32
        )
        grad_score = (weights * (grad_prob - delta_heads[..., None])).astype(jnp.bfloat16)
        grad_query = (
            grad_query
            + jnp.einsum(
                "mhqk,mkhd->mqhd", grad_score, keys_block, preferred_element_type=jnp.float32
            )
            * scale
        )
        key_term = (
            jnp.einsum(
                "mhqk,mqhd->mkhd", grad_score, query_heads, preferred_element_type=jnp.float32
            )
            * scale
        )
        value_term = jnp.einsum(
            "mhqk,mqhd->mkhd",
            weights.astype(jnp.bfloat16),
            grad_heads,
            preferred_element_type=jnp.float32,
        )
        grad_keys_now = grad_keys_now + key_term.reshape(grad_keys_now.shape)
        grad_values_now = grad_values_now + value_term.reshape(grad_values_now.shape)
        return (keys_now, values_now, grad_keys_now, grad_values_now, grad_query)

    def cycle_turn(index, carry):
        anchor = (cycle_index - index) % cycle_size
        updated = cycle_step(carry, anchor)
        moved = (
            shifted(updated[0], "blk", 1),
            shifted(updated[1], "blk", 1),
            shifted(updated[2].astype(jnp.bfloat16), "blk", 1).astype(jnp.float32),
            shifted(updated[3].astype(jnp.bfloat16), "blk", 1).astype(jnp.float32),
        )
        return (
            moved[0],
            moved[1],
            moved[2].astype(jnp.float32),
            moved[3].astype(jnp.float32),
            updated[4],
        )

    carry = lax.fori_loop(
        0, cycle_size - 1, cycle_turn, (keys, values, zeros_flat, zeros_flat, zeros_heads)
    )
    final = cycle_step(carry, (cycle_index + 1) % cycle_size)
    returned = (
        shifted(final[2].astype(jnp.bfloat16), "blk", 1).astype(jnp.float32),
        shifted(final[3].astype(jnp.bfloat16), "blk", 1).astype(jnp.float32),
    )
    grad_keys = returned[0].astype(jnp.float32)
    grad_values = returned[1].astype(jnp.float32)
    grad_query = final[4].reshape(batches, tokens, local_width)
    grad_mixed = jnp.concatenate(
        [
            grad_query.reshape(rows_all, local_width),
            grad_keys.reshape(rows_all, local_width),
            grad_values.reshape(rows_all, local_width),
        ],
        axis=1,
    ).astype(jnp.bfloat16)
    project_bias_grad = jnp.stack(
        [
            jnp.sum(grad_mixed[:, :local_width].astype(jnp.float32), axis=0),
            jnp.sum(grad_mixed[:, 2 * local_width :].astype(jnp.float32), axis=0),
        ]
    )
    project_part = jnp.einsum(
        "rd,rc->dc", flat_input, grad_mixed, preferred_element_type=jnp.float32
    ).reshape(width, 3, local_width)
    input_back = jnp.einsum(
        "rc,dc->rd",
        grad_mixed,
        project_full.reshape(width, 3 * local_width),
        preferred_element_type=jnp.float32,
    )
    input_gradient = grad_first_in + lax.psum(input_back.astype(jnp.bfloat16), "head").astype(
        jnp.float32
    )
    shards = (
        lax.psum_scatter(
            project_part.astype(jnp.bfloat16), "dp", scatter_dimension=0, tiled=True
        ).astype(jnp.float32),
        lax.psum_scatter(
            output_part.astype(jnp.bfloat16), "dp", scatter_dimension=1, tiled=True
        ).astype(jnp.float32),
        lax.psum_scatter(
            expand_part.astype(jnp.bfloat16), "dp", scatter_dimension=0, tiled=True
        ).astype(jnp.float32),
        lax.psum_scatter(
            down_part.astype(jnp.bfloat16), "dp", scatter_dimension=1, tiled=True
        ).astype(jnp.float32),
    )
    totals = (
        lax.psum(shards[0].astype(jnp.bfloat16), "blk").astype(jnp.float32),
        lax.psum(shards[1].astype(jnp.bfloat16), "blk").astype(jnp.float32),
        lax.psum(shards[2].astype(jnp.bfloat16), "blk").astype(jnp.float32),
        lax.psum(shards[3].astype(jnp.bfloat16), "blk").astype(jnp.float32),
    )
    small = lax.psum(
        (
            project_bias_grad,
            output_bias_grad,
            first_gain_grad,
            first_shift_grad,
            expand_bias_grad,
            down_bias_grad,
            second_gain_grad,
            second_shift_grad,
        ),
        ("dp", "blk"),
    )
    return (
        layer_output,
        input_gradient.reshape(batches, tokens, width),
        totals[0],
        small[0],
        totals[1],
        small[1],
        small[2],
        small[3],
        totals[2],
        small[4],
        totals[3],
        small[5],
        small[6],
        small[7],
    )


MESH = pl.DeviceIdType.MESH
BF = jnp.bfloat16
F32 = jnp.float32
FAR = 1e33
VMEM_BYTES = 63 << 20
HEAD = 64


def dot(a, b):
    return lax.dot_general(a, b, (((1,), (0,)), ((), ())), preferred_element_type=F32)


def dot_nt(a, b):
    return lax.dot_general(a, b, (((1,), (1,)), ((), ())), preferred_element_type=F32)


def dot_tn(a, b):
    return lax.dot_general(a, b, (((0,), (0,)), ((), ())), preferred_element_type=F32)


def column_sum(rows):
    return jnp.sum(rows, axis=0, keepdims=True)


def row_mean(rows):
    return jnp.mean(rows, axis=-1, keepdims=True)


def standardize(rows):
    centered = rows - row_mean(rows)
    inverse = lax.rsqrt(row_mean(centered * centered) + EPSILON)
    return centered * inverse, inverse


def standardize_back(grad, normal, inverse):
    return inverse * (grad - row_mean(grad) - normal * row_mean(grad * normal))


def layer_kernel(
    x_ref, cot_ref, pw_ref, ow_ref, ew_ref, dw_ref, len_ref, slope_ref, pb_ref, eb_ref,
    ob_ref, g1_ref, s1_ref, db_ref, g2_ref, s2_ref,
    out_ref, ig_ref, ga_ref, gf_ref, early_ref, late_ref,
    x_full, first_full, feed_full, branch_full,
    w_attn, w_gu, w_down, packs, own_attn,
    part, r1x, r1y, r2,
    q_s, k_s, v_s, g_s, p_s, ctx_s, ctx_cat, dqkv, ds_s, dq_s, far_s,
    act_s, upd_s, hid_s, dgu_s, eb_acc,
    first_own, n1_s, a1_s, gr2_s, gr1_s,
    dwf, dwf_in, dwf_z, dwa, dwa_in, dwa_z, fin_a,
    early, late, slope_s,
    ag_ss, ag_rs, rs_ss, rs_rs, pk_sem, wa_ss, wa_rs, wf_ss, wf_rs, wl_sem, wc_ss, wc_rs,
    gc_ss, gc_rs, gz_ss, gz_rs, gp_ss, gp_rs, ge_ss, ge_rs, gl_ss, gl_rs, io_ss, io_rs,
):
    z, b, c = lax.axis_index("dp"), lax.axis_index("blk"), lax.axis_index("head")
    half, odd = b // 2, b % 2
    xor = jnp.bitwise_xor
    other = 1 - c
    bx, by, bd = xor(b, 1), xor(b, 2), xor(b, 3)
    sib, xdev, ydev = (z, b, other), (z, bx, c), (z, by, c)
    near, far, opposite = ((xor(z, k), b, c) for k in (1, 2, 3))
    inner = jnp.logical_or(z == 1, z == 2)
    outer = jnp.logical_not(inner)
    T = x_ref.shape[1]
    D = x_ref.shape[2]
    H2 = D // 2
    ROWS = 4 * T
    DZ = pw_ref.shape[1]
    UB = dw_ref.shape[1] // 4
    HW = 3 * HEAD
    lo, hi = pl.ds(0, H2), pl.ds(H2, H2)

    def chunk(index, size):
        return pl.ds(pl.multiple_of(index * size, size), size)

    mine_z, near_z, far_z, opposite_z = (chunk(xor(z, k), DZ) for k in range(4))
    started = []

    def raw(src, dst, ss, rs, dev):
        return pltpu.make_async_remote_copy(
            src_ref=src, dst_ref=dst, send_sem=ss, recv_sem=rs, device_id=dev, device_id_type=MESH
        )

    class Copy:
        def __init__(self, *args):
            self.copy = raw(*args)
            self.sent = self.received = False

        def start(self):
            self.copy.start()
            started.append(self)

        def wait_recv(self):
            self.copy.wait_recv()
            self.received = True

        def wait_send(self):
            self.copy.wait_send()
            self.sent = True

        def finish(self):
            if not self.received:
                self.wait_recv()
            if not self.sent:
                self.wait_send()

    partners = [(z, xor(b, k), cc) for k in (1, 2, 3) for cc in (c, other)] + [sib]
    partners += [(xor(z, k), b, cc) for k in (1, 2, 3) for cc in (c, other)]
    barrier = pltpu.get_barrier_semaphore()
    for dev in partners:
        pl.semaphore_signal(barrier, inc=1, device_id=dev, device_id_type=MESH)
    pl.semaphore_wait(barrier, len(partners))

    class Gather:
        def __init__(self, full, phase, m):
            ss, rs = ag_ss.at[phase, m], ag_rs.at[phase, m]
            own, sx, sy = m * 4 + b, m * 4 + bx, m * 4 + by
            self.cx = Copy(full.at[own], full.at[own], ss.at[0], rs.at[0], xdev)
            self.cy = Copy(full.at[own], full.at[own], ss.at[1], rs.at[1], ydev)
            self.fx = Copy(full.at[sx, :, lo], full.at[sx, :, lo], ss.at[2], rs.at[2], ydev)
            self.fy = Copy(full.at[sy, :, hi], full.at[sy, :, hi], ss.at[3], rs.at[3], xdev)

        def start(self):
            self.cx.start()
            self.cy.start()

        def mid(self):
            self.cx.wait_recv()
            self.fx.start()
            self.cy.wait_recv()
            self.fy.start()

        def end(self):
            self.fx.wait_recv()
            self.fy.wait_recv()

    class Scatter:
        def __init__(self, phase, m):
            ss, rs = rs_ss.at[phase, m], rs_rs.at[phase, m]
            buf = part.at[phase % 2]
            own, sx, sy, sd = m * 4 + b, m * 4 + bx, m * 4 + by, m * 4 + bd
            ix, iy, i2 = r1x.at[phase, m], r1y.at[phase, m], r2.at[phase, m]
            self.buf, self.own, self.sx, self.sy = buf, own, sx, sy
            self.ix, self.iy, self.i2 = ix, iy, i2
            self.xd = Copy(buf.at[sd, :, lo], ix.at[1], ss.at[0], rs.at[0], xdev)
            self.yd = Copy(buf.at[sd, :, hi], iy.at[1], ss.at[1], rs.at[1], ydev)
            self.xo = Copy(buf.at[sx, :, lo], ix.at[0], ss.at[2], rs.at[2], xdev)
            self.yo = Copy(buf.at[sy, :, hi], iy.at[0], ss.at[3], rs.at[3], ydev)
            self.y2 = Copy(buf.at[sy, :, lo], i2.at[0], ss.at[4], rs.at[4], ydev)
            self.x2 = Copy(buf.at[sx, :, hi], i2.at[1], ss.at[5], rs.at[5], xdev)

        def start(self):
            for copy in (self.xd, self.yd, self.xo, self.yo):
                copy.start()

        def mid(self):
            buf = self.buf
            self.xd.wait_recv()
            buf[self.sy, :, :H2] = (
                buf[self.sy, :, :H2].astype(F32) + self.ix[1].astype(F32)
            ).astype(BF)
            self.y2.start()
            self.yd.wait_recv()
            buf[self.sx, :, H2:] = (
                buf[self.sx, :, H2:].astype(F32) + self.iy[1].astype(F32)
            ).astype(BF)
            self.x2.start()

        def end(self):
            for copy in (self.xo, self.yo, self.y2, self.x2):
                copy.wait_recv()
            mine = self.buf[self.own].astype(F32)
            low = mine[:, :H2] + self.ix[0].astype(F32) + self.i2[0].astype(F32)
            high = mine[:, H2:] + self.iy[0].astype(F32) + self.i2[1].astype(F32)
            return jnp.concatenate([low, high], axis=1)

        def drain(self):
            for copy in (self.xd, self.yd, self.xo, self.yo, self.y2, self.x2):
                copy.wait_send()

    gather_x = [Gather(x_full, 0, m) for m in (0, 1)]
    gather_first = [Gather(first_full, 1, m) for m in (0, 1)]
    gather_feed = [Gather(feed_full, 2, m) for m in (0, 1)]
    gather_branch = [Gather(branch_full, 3, m) for m in (0, 1)]
    sum_branch = [Scatter(0, m) for m in (0, 1)]
    sum_feed = [Scatter(1, m) for m in (0, 1)]
    sum_first = [Scatter(2, m) for m in (0, 1)]
    sum_input = [Scatter(3, m) for m in (0, 1)]

    class Column:
        def __init__(self, pieces, ss, rs):
            self.pieces, self.ss, self.rs = pieces, ss, rs

        def copy(self, dz, index, src, dst, dev):
            return raw(src, dst, self.ss.at[dz, index], self.rs.at[dz, index], dev)

        def copies(self):
            for dz in (2, 1, 3):
                for index, (src, place_at, core) in enumerate(self.pieces):
                    yield dz, self.copy(dz, index, src, place_at(mine_z), (xor(z, dz), b, core))

        def send(self):
            for dz, copy in self.copies():
                if dz == 3:
                    pl.when(inner)(copy.start)
                else:
                    copy.start()

        def sent(self):
            for dz, copy in self.copies():
                if dz == 3:
                    pl.when(inner)(copy.wait_send)
                else:
                    copy.wait_send()

        def arrival(self, dz, index):
            src, place_at, _ = self.pieces[index]
            self.copy(dz, index, src, place_at(mine_z), near).wait_recv()

        def passing(self, index):
            rows = self.pieces[index][1](far_z)
            return raw(rows, rows, self.ss.at[0, index], self.rs.at[3, index], near)

        def relay(self, index):
            self.arrival(2, index)
            pl.when(inner)(self.passing(index).start)

        def relay_all(self):
            for index in range(len(self.pieces)):
                self.relay(index)

        def relayed(self, index):
            pl.when(inner)(self.passing(index).wait_send)

        def rest(self, index):
            self.arrival(1, index)
            self.arrival(3, index)

    def attn_place(k):
        return lambda rows: w_attn.at[rows, pl.ds(k * H2, H2)]

    attn_pieces = [(own_attn.at[:, pl.ds(k * H2, H2)], attn_place(k), k) for k in (0, 1)]
    attn_column = Column(attn_pieces, wa_ss, wa_rs)
    attn_own = []
    for index, (src, place_at, core) in enumerate(attn_pieces):
        dst = place_at(mine_z)
        cross = raw(src, dst, wa_ss.at[4, index], wa_rs.at[4, index], sib)
        local = pltpu.make_async_copy(src, dst, wl_sem.at[index])
        attn_own.append((cross, local))
    gu_column = Column(
        [
            (ew_ref.at[0, :, chunk(b, UB)], lambda rows: w_gu.at[c, rows, pl.ds(0, UB)], c),
            (ew_ref.at[1, :, chunk(b, UB)], lambda rows: w_gu.at[c, rows, pl.ds(UB, UB)], c),
        ],
        wf_ss.at[0],
        wf_rs.at[0],
    )
    down_column = Column(
        [(dw_ref.at[:, chunk(b, UB)], lambda rows: w_down.at[rows, chunk(c, UB)], c)],
        wf_ss.at[1],
        wf_rs.at[1],
    )
    feed_own = []
    for index, (src, place_at, _) in enumerate(gu_column.pieces + down_column.pieces):
        feed_own.append(pltpu.make_async_copy(src, place_at(mine_z), wl_sem.at[2 + index]))

    for m in (0, 1):
        x_full[m * 4 + b] = x_ref[2 * c + m]
    gather_x[0].start()

    @pl.when(c == half)
    def _():
        shards = [pw_ref[kind] for kind in range(3)] + [ow_ref[...]]
        own_attn[...] = jnp.concatenate(
            [jnp.where(odd == 0, item[:, 0:HW], item[:, HW : 2 * HW]) for item in shards], axis=1
        )
        attn_column.send()
        for index, (cross, local) in enumerate(attn_own):
            pl.when(c == index)(local.start)
            pl.when(c != index)(cross.start)

    for row in (0, 1):
        packs[c, row : row + 1, :] = eb_ref[row : row + 1, :]
        packs[c, row + 2 : row + 3, 0:H2] = pb_ref[row : row + 1, :]
    for i in range(6):
        packs[c, 10 + i : 11 + i, 0:128] = jnp.full((1, 128), slope_ref[i], F32)
    pack_copy = Copy(packs.at[c], packs.at[c], pk_sem.at[0], pk_sem.at[1], sib)
    pack_copy.start()
    gather_x[1].start()
    for copy in feed_own:
        copy.start()

    for m in (0, 1):
        start_one = len_ref[0, 0, 2 * c + m]
        start_two = start_one + len_ref[1, 0, 2 * c + m]
        for rb in range(4):
            rows = lax.broadcasted_iota(jnp.int32, (T, ROWS), 0) + rb * T
            cols = lax.broadcasted_iota(jnp.int32, (T, ROWS), 1)
            seq_r = (rows >= start_one).astype(jnp.int32) + (rows >= start_two).astype(jnp.int32)
            seq_c = (cols >= start_one).astype(jnp.int32) + (cols >= start_two).astype(jnp.int32)
            distance = jnp.abs(rows - cols).astype(F32)
            far_s[m, pl.ds(rb * T, T), :] = jnp.where(seq_r == seq_c, distance, FAR)
    early[...] = jnp.zeros_like(early)
    late[...] = jnp.zeros_like(late)
    eb_acc[...] = jnp.zeros_like(eb_acc)

    for index in (0, 1):
        pl.when(c == index)(functools.partial(attn_column.relay, index))
    gu_column.send()
    gather_x[0].mid()
    gather_x[1].mid()
    pack_copy.wait_recv()
    for index, (cross, local) in enumerate(attn_own):

        @pl.when(c == index)
        def _():
            pl.when(c == half)(local.wait)
            pl.when(c != half)(cross.wait_recv)
            attn_column.rest(index)

    lanes = w_attn.at[:, chunk(c, H2)]
    attn_share = Copy(lanes, lanes, wc_ss.at[0], wc_rs.at[0], sib)
    attn_share.start()

    for i in range(3):
        low, high = packs[half, 10 + i : 11 + i, 0:128], packs[half, 13 + i : 14 + i, 0:128]
        slope_s[i] = jnp.broadcast_to(jnp.where(odd == 0, low, high), (8, 128))

    def vector(ref):
        return ref[...].reshape(1, D)

    def project(m):
        biases = packs[half, 2:4, 0:H2]
        biases = jnp.where(odd == 0, biases[:, 0:HW], biases[:, HW : 2 * HW])

        def rows_of(t, _):
            rows = x_full[pl.ds(m * 4 + t * 2, 2)].reshape(2 * T, D)
            at = pl.ds(pl.multiple_of(t * 2 * T, 2 * T), 2 * T)
            mixed = dot(rows, w_attn[:, 0 : 3 * HW])
            query = (mixed[:, 0:HW] + biases[0:1]).astype(BF) * jnp.asarray(0.125, BF)
            keys = mixed[:, HW : 2 * HW].astype(BF)
            values = (mixed[:, 2 * HW : 3 * HW] + biases[1:2]).astype(BF)
            for i in range(3):
                cols = slice(i * HEAD, i * HEAD + HEAD)
                q_s[m * 3 + i, at, :] = query[:, cols]
                k_s[m * 3 + i, at, :] = keys[:, cols]
                v_s[m * 3 + i, at, :] = values[:, cols]
            return 0

        lax.fori_loop(0, 2, rows_of, 0)

    def attend(m, first, last):
        def one(index, _):
            i, rb = index // 4, index % 4
            at = chunk(rb, T)
            h = m * 3 + i
            scores = dot_nt(q_s[h, at, :], k_s[h])
            scores = scores - slope_s[i][0:1, 0:1] * far_s[m, at, :]
            top = jnp.max(scores, axis=-1, keepdims=True)
            weights = jnp.exp(scores - top)
            total = jnp.sum(weights, axis=-1, keepdims=True)
            probs = (weights * (1.0 / total)).astype(BF)
            p_s[h, at, :] = probs
            ctx_s[h, at, :] = dot(probs, v_s[h])
            return 0

        lax.fori_loop(first, last, one, 0)

    def put_part(buf, m, t, rows):
        buf[pl.ds(m * 4 + 2 * t, 2)] = rows.astype(BF).reshape(2, T, D)

    def branch(m):
        def rows_of(t, _):
            at = pl.ds(pl.multiple_of(t * 2 * T, 2 * T), 2 * T)
            cat = jnp.concatenate([ctx_s[m * 3 + i, at, :].astype(BF) for i in range(3)], axis=1)
            ctx_cat[m, at, :] = cat
            put_part(sum_branch[m].buf, m, t, dot_nt(cat, w_attn[:, 3 * HW : 4 * HW]))
            return 0

        lax.fori_loop(0, 2, rows_of, 0)

    def first_norm(m):
        rows = x_ref[2 * c + m].astype(F32) + sum_branch[m].end() + vector(ob_ref)
        normal, inverse = standardize(rows)
        first = normal * vector(g1_ref) + vector(s1_ref)
        n1_s[m], a1_s[m] = normal, inverse
        first_own[m] = first
        first_full[m * 4 + b] = first.astype(BF)

    def feed_forward(m):
        def rows_of(t, _):
            at = pl.ds(pl.multiple_of(m * ROWS + t * 2 * T, 2 * T), 2 * T)
            rows = first_full[pl.ds(m * 4 + t * 2, 2)].reshape(2 * T, D)
            for g in (0, 1):
                cols = pl.ds(g * UB, UB)
                bias = packs[g, 0:2, chunk(b, UB)]
                both = dot(rows, w_gu[g])
                gate = both[:, :UB] + bias[0:1]
                up = both[:, UB:] + bias[1:2]
                cdf = 0.5 + 0.5 * lax.erf(gate * 0.7071067811865476)
                act = gate * cdf
                slope = cdf + gate * (jnp.exp(-0.5 * gate * gate) * 0.3989422804014327)
                hid_s[at, cols] = (act * up).astype(BF)
                act_s[at, cols] = act.astype(BF)
                upd_s[at, cols] = (up * slope).astype(BF)
            return 0

        lax.fori_loop(0, 2, rows_of, 0)

    def feed_out(m):
        def rows_of(t, _):
            at = pl.ds(pl.multiple_of(m * ROWS + t * 2 * T, 2 * T), 2 * T)
            put_part(sum_feed[m].buf, m, t, dot_nt(hid_s[at, :], w_down[...]))
            return 0

        lax.fori_loop(0, 2, rows_of, 0)

    def add_early(row, rows):
        early[0, row : row + 1, :] += column_sum(rows)

    def second_norm(m):
        rows = first_own[m] + sum_feed[m].end() + vector(db_ref)
        normal, inverse = standardize(rows)
        out_ref[2 * c + m] = (normal * vector(g2_ref) + vector(s2_ref)).astype(BF)
        grad = cot_ref[2 * c + m].astype(F32)
        add_early(4, grad * normal)
        add_early(5, grad)
        back = standardize_back(grad * vector(g2_ref), normal, inverse)
        gr2_s[m] = back
        low = back.astype(BF)
        feed_full[m * 4 + b] = low
        add_early(3, low.astype(F32))

    def feed_backward(m):
        def rows_of(t, _):
            at = pl.ds(pl.multiple_of(m * ROWS + t * 2 * T, 2 * T), 2 * T)
            rows = feed_full[pl.ds(m * 4 + t * 2, 2)].reshape(2 * T, D)
            hidden = dot(rows, w_down[...])
            dgate = (hidden * upd_s[at, :].astype(F32)).astype(BF)
            dup = (hidden * act_s[at, :].astype(F32)).astype(BF)
            for g in (0, 1):
                cols = slice(g * UB, g * UB + UB)
                dgu_s[g, at, 0:UB] = dgate[:, cols]
                dgu_s[g, at, UB : 2 * UB] = dup[:, cols]
                eb_acc[2 * g : 2 * g + 1, :] += column_sum(dgate[:, cols].astype(F32))
                eb_acc[2 * g + 1 : 2 * g + 2, :] += column_sum(dup[:, cols].astype(F32))
            back = dot_nt(dgu_s[0, at, :], w_gu[0]) + dot_nt(dgu_s[1, at, :], w_gu[1])
            put_part(sum_first[m].buf, m, t, back)
            return 0

        lax.fori_loop(0, 2, rows_of, 0)

    def down_weights():
        def cols_of(t, _):
            at = chunk(t, 256)
            rows = feed_full[:, :, at].reshape(2 * ROWS, 256)
            down = dot_tn(rows, hid_s[...]).astype(BF)
            for g in (0, 1):
                dwf[g, at, 2 * UB : 3 * UB] = down[:, g * UB : g * UB + UB]
            return 0

        lax.fori_loop(0, D // 256, cols_of, 0)

    def expand_weights():
        def cols_of(t, _):
            at = chunk(t, 256)
            rows = first_full[:, :, at].reshape(2 * ROWS, 256)
            for g in (0, 1):
                dwf[g, at, 0 : 2 * UB] = dot_tn(rows, dgu_s[g]).astype(BF)
            return 0

        lax.fori_loop(0, D // 256, cols_of, 0)

    def first_back(m):
        grad = gr2_s[m] + sum_first[m].end()
        normal = n1_s[m]
        add_early(1, grad * normal)
        add_early(2, grad)
        back = standardize_back(grad * vector(g1_ref), normal, a1_s[m])
        gr1_s[m] = back
        low = back.astype(BF)
        branch_full[m * 4 + b] = low
        add_early(0, low.astype(F32))

    def context_back(m):
        def rows_of(t, _):
            at = pl.ds(pl.multiple_of(t * 2 * T, 2 * T), 2 * T)
            rows = branch_full[pl.ds(m * 4 + t * 2, 2)].reshape(2 * T, D)
            grads = dot(rows, w_attn[:, 3 * HW : 4 * HW]).astype(BF)
            for i in range(3):
                g_s[m * 3 + i, at, :] = grads[:, i * HEAD : i * HEAD + HEAD]
            return 0

        lax.fori_loop(0, 2, rows_of, 0)

    def attend_back(m, first, last):
        def one(i, _):
            h = m * 3 + i

            def block(rb, _):
                at = chunk(rb, T)
                rows = g_s[h, at, :]
                delta = jnp.sum(rows.astype(F32) * ctx_s[h, at, :], axis=-1, keepdims=True)
                probs = p_s[h, at, :].astype(F32)
                score = (probs * (dot_nt(rows, v_s[h]) - delta)).astype(BF)
                ds_s[at, :] = score
                dq_s[0, i, at, :] = (dot(score, k_s[h]) * 0.125).astype(BF)
                return 0

            lax.fori_loop(0, 4, block, 0)
            dq_s[1, i] = dot_tn(q_s[h], ds_s[...]).T.astype(BF)
            dq_s[2, i] = dot_tn(g_s[h], p_s[h]).T.astype(BF)
            return 0

        lax.fori_loop(first, last, one, 0)

    def collect(m):
        for kind in range(3):
            cat = jnp.concatenate([dq_s[kind, i] for i in range(3)], axis=1)
            dqkv[m, :, kind * HW : kind * HW + HW] = cat
            if kind != 1:
                sums = column_sum(cat.astype(F32))
                for h in (0, 1):
                    lanes = pl.ds(pl.multiple_of(odd * H2, H2), HW)
                    late[0, kind + h : kind + h + 1, lanes] += jnp.where(half == h, sums, 0.0)

    def input_back(m):
        def rows_of(t, _):
            at = pl.ds(pl.multiple_of(t * 2 * T, 2 * T), 2 * T)
            put_part(sum_input[m].buf, m, t, dot_nt(dqkv[m, at, :], w_attn[:, 0 : 3 * HW]))
            return 0

        lax.fori_loop(0, 2, rows_of, 0)

    def attend_weights():
        def cols_of(t, _):
            at = chunk(t, 256)
            rows = x_full[:, :, at].reshape(2 * ROWS, 256)
            grads = dot_tn(rows, dqkv[...].reshape(2 * ROWS, 3 * HW)).astype(BF)
            dwa[0, at, :] = grads[:, 0:H2]
            dwa[1, at, 0:HW] = grads[:, H2 : 3 * HW]
            rows = branch_full[:, :, at].reshape(2 * ROWS, 256)
            outs = dot_tn(rows, ctx_cat[...].reshape(2 * ROWS, HW)).astype(BF)
            dwa[1, at, HW : 2 * HW] = outs
            return 0

        lax.fori_loop(0, D // 256, cols_of, 0)

    class Reduce:
        def __init__(self, index, buf, incoming, zin):
            self.buf, self.incoming, self.zin = buf, incoming, zin
            self.swap = Copy(buf.at[other], incoming, gc_ss.at[index], gc_rs.at[index], sib)

            def push(rows, slot, dev):
                ss, rs = gz_ss.at[index, slot], gz_rs.at[index, slot]
                return raw(buf.at[c, rows, :], zin.at[slot], ss, rs, dev)

            self.to_near = push(near_z, 0, near)
            self.to_far = push(far_z, 1, far)
            self.to_opposite = push(opposite_z, 2, opposite)
            self.by_near = push(opposite_z, 3, near)

        def join(self):
            self.swap.wait_recv()

            def add(rows):
                mine = self.buf[c, rows, :].astype(F32)
                self.buf[c, rows, :] = (mine + self.incoming[rows, :].astype(F32)).astype(BF)

            add(opposite_z)
            pl.when(outer)(self.by_near.start)
            pl.when(inner)(self.to_opposite.start)
            add(far_z)
            pl.when(outer)(self.to_far.start)
            add(near_z)
            self.to_near.start()
            add(mine_z)

        def relay(self):
            @pl.when(inner)
            def _():
                self.by_near.wait_recv()
                mine = self.buf[c, far_z, :].astype(F32)
                self.buf[c, far_z, :] = (mine + self.zin[3].astype(F32)).astype(BF)
                self.to_far.start()

        def total(self, put):
            self.to_near.wait_recv()
            self.to_far.wait_recv()

            def value():
                low = self.buf[c, mine_z, :].astype(F32)
                return low + self.zin[0].astype(F32) + self.zin[1].astype(F32)

            @pl.when(inner)
            def _():
                self.to_opposite.wait_recv()
                put((value() + self.zin[2].astype(F32)).astype(BF))

            @pl.when(outer)
            def _():
                put(value().astype(BF))

        def sent(self):
            self.to_near.wait_send()
            self.to_far.wait_send()
            pl.when(inner)(self.to_opposite.wait_send)
            pl.when(outer)(self.by_near.wait_send)

    reduce_feed = Reduce(0, dwf, dwf_in, dwf_z)
    reduce_attn = Reduce(1, dwa, dwa_in, dwa_z)

    class Everywhere:
        def __init__(self, buf, ss, rs, result):
            devices = [sib, xdev, ydev, near, far]
            self.buf, self.result = buf, result
            self.copies = [
                Copy(buf.at[2 * i], buf.at[2 * i + 1], ss.at[i], rs.at[i], dev)
                for i, dev in enumerate(devices)
            ]

        def start(self):
            self.copies[0].start()

        def step(self, i):
            self.copies[i].wait_recv()
            value = self.buf[2 * i] + self.buf[2 * i + 1]
            if i + 1 < len(self.copies):
                self.buf[2 * i + 2] = value
                self.copies[i + 1].start()
            else:
                self.result[...] = value

    early_sum = Everywhere(early, ge_ss, ge_rs, early_ref)
    late_sum = Everywhere(late, gl_ss, gl_rs, late_ref)

    def early_start():
        for g in (0, 1):
            for kind in (0, 1):
                row = 6 + (2 * g + kind) * 2
                values = eb_acc[2 * g + kind : 2 * g + kind + 1, :]
                for h in (0, 1):
                    at = slice(row + h, row + h + 1)
                    early[0, at, chunk(odd, UB)] = jnp.where(half == h, values, 0.0)
        early_sum.start()

    share_gu = Copy(w_gu.at[c], w_gu.at[c], wc_ss.at[1], wc_rs.at[1], sib)
    down_lanes = w_down.at[:, chunk(c, UB)]
    share_down = Copy(down_lanes, down_lanes, wc_ss.at[2], wc_rs.at[2], sib)

    def take(column, own, share):
        for index in range(len(column.pieces)):
            column.rest(index)
        for copy in own:
            copy.wait()
        share.start()

    def send_rows(refs, index, m):
        rows = refs.at[2 * c + m]
        Copy(rows, rows, io_ss.at[index, m], io_rs.at[index, m], sib).start()

    def finish_input(m):
        ig_ref[2 * c + m] = gr1_s[m] + sum_input[m].end()
        send_rows(ig_ref, 1, m)

    class Spread:
        def __init__(self):
            top, bottom = pl.ds(0, DZ // 2), pl.ds(DZ // 2, DZ // 2)
            ss, rs = gp_ss.at[0], gp_rs.at[0]
            self.cx = Copy(gf_ref.at[b], gf_ref.at[b], ss.at[0], rs.at[0], xdev)
            self.cy = Copy(gf_ref.at[b], gf_ref.at[b], ss.at[1], rs.at[1], ydev)
            self.fx = Copy(gf_ref.at[bx, top], gf_ref.at[bx, top], ss.at[2], rs.at[2], ydev)
            self.fy = Copy(gf_ref.at[by, bottom], gf_ref.at[by, bottom], ss.at[3], rs.at[3], xdev)

        def start(self):
            def put(value):
                gf_ref[b] = value

            reduce_feed.total(put)
            self.cx.start()
            self.cy.start()

        def mid(self):
            self.cx.wait_recv()
            self.fx.start()
            self.cy.wait_recv()
            self.fy.start()

    spread = Spread()

    def finish_attn():
        def put(value):
            fin_a[...] = value

        reduce_attn.total(put)
        slot, rs = ga_ref.at[odd, c], gp_rs.at[1 + odd, c]
        copies = [raw(fin_a, slot, gp_ss.at[1, k], rs, (z, xor(b, k), half)) for k in (3, 1, 2)]
        cross = raw(fin_a, slot, gp_ss.at[1, 0], rs, sib)
        for copy in copies:
            copy.start()
        pl.when(c != half)(cross.start)

        @pl.when(c == half)
        def _():
            ga_ref[odd, c] = fin_a[...]

        for parity in (0, 1):
            for core in (0, 1):
                own = jnp.logical_and(c == half, jnp.logical_and(odd == parity, c == core))
                rs = gp_rs.at[1 + parity, core]
                arrival = raw(fin_a, ga_ref.at[parity, core], gp_ss.at[1, 0], rs, sib)
                pl.when(jnp.logical_not(own))(arrival.wait_recv)
        pl.when(c != half)(cross.wait_send)
        for copy in copies:
            copy.wait_send()

    steps = [
        attn_share.wait_recv,
        gather_x[0].end,
        lambda: project(0),
        lambda: attend(0, 0, 12),
        lambda: branch(0),
        sum_branch[0].start,
        gather_x[1].end,
        gu_column.relay_all,
        down_column.send,
        lambda: project(1),
        lambda: attend(1, 0, 6),
        sum_branch[0].mid,
        lambda: attend(1, 6, 12),
        lambda: branch(1),
        sum_branch[1].start,
        lambda: first_norm(0),
        gather_first[0].start,
        down_column.relay_all,
        lambda: take(gu_column, feed_own[:2], share_gu),
        sum_branch[1].mid,
        gather_first[0].mid,
        lambda: first_norm(1),
        gather_first[1].start,
        share_gu.wait_recv,
        gather_first[0].end,
        lambda: feed_forward(0),
        lambda: take(down_column, feed_own[2:], share_down),
        gather_first[1].mid,
        share_down.wait_recv,
        lambda: feed_out(0),
        sum_feed[0].start,
        gather_first[1].end,
        lambda: feed_forward(1),
        sum_feed[0].mid,
        lambda: feed_out(1),
        sum_feed[1].start,
        lambda: second_norm(0),
        gather_feed[0].start,
        sum_feed[1].mid,
        gather_feed[0].mid,
        lambda: second_norm(1),
        gather_feed[1].start,
        lambda: send_rows(out_ref, 0, 0),
        lambda: send_rows(out_ref, 0, 1),
        gather_feed[0].end,
        sum_branch[0].drain,
        lambda: feed_backward(0),
        sum_first[0].start,
        gather_feed[1].mid,
        gather_feed[1].end,
        sum_branch[1].drain,
        lambda: feed_backward(1),
        sum_first[0].mid,
        sum_first[1].start,
        down_weights,
        lambda: first_back(0),
        gather_branch[0].start,
        sum_first[1].mid,
        expand_weights,
        lambda: reduce_feed.swap.start(),
        gather_branch[0].mid,
        lambda: first_back(1),
        gather_branch[1].start,
        early_start,
        reduce_feed.join,
        gather_branch[0].end,
        lambda: context_back(0),
        lambda: attend_back(0, 0, 1),
        lambda: gather_branch[1].mid(),
        reduce_feed.relay,
        lambda: early_sum.step(0),
        lambda: attend_back(0, 1, 2),
        lambda: early_sum.step(1),
        lambda: attend_back(0, 2, 3),
        lambda: collect(0),
        sum_feed[0].drain,
        lambda: input_back(0),
        sum_input[0].start,
        lambda: early_sum.step(2),
        gather_branch[1].end,
        lambda: context_back(1),
        lambda: attend_back(1, 0, 1),
        lambda: early_sum.step(3),
        sum_input[0].mid,
        lambda: attend_back(1, 1, 3),
        lambda: early_sum.step(4),
        lambda: collect(1),
        sum_feed[1].drain,
        lambda: input_back(1),
        sum_input[1].start,
        late_sum.start,
        attend_weights,
        lambda: reduce_attn.swap.start(),
        lambda: late_sum.step(0),
        sum_input[1].mid,
        reduce_attn.join,
        lambda: late_sum.step(1),
        lambda: finish_input(0),
        lambda: late_sum.step(2),
        reduce_attn.relay,
        spread.start,
        lambda: late_sum.step(3),
        lambda: finish_input(1),
        lambda: late_sum.step(4),
        spread.mid,
        finish_attn,
    ]
    for step in steps:
        step()

    @pl.when(c == half)
    def _():
        attn_column.sent()
        for index, (cross, _) in enumerate(attn_own):
            pl.when(c != index)(cross.wait_send)

    for index in (0, 1):
        pl.when(c == index)(functools.partial(attn_column.relayed, index))
    for column in (gu_column, down_column):
        column.sent()
        for index in range(len(column.pieces)):
            column.relayed(index)
    reduce_feed.sent()
    reduce_attn.sent()
    for copy in started:
        copy.finish()


def result_kernel(
    ga_ref, gf_ref, early_ref, late_ref, out_in, ig_in,
    out_ref, ig_ref, pw_ref, pb_ref, ow_ref, ob_ref, g1_ref, s1_ref,
    ew_ref, eb_ref, dw_ref, db_ref, g2_ref, s2_ref,
    gf_in, out_buf, ig_buf, ew_out, dw_out, in_sems, out_sems,
):
    loads = [pltpu.make_async_copy(gf_ref.at[n], gf_in.at[n], in_sems.at[n]) for n in range(4)]
    loads.append(pltpu.make_async_copy(out_in, out_buf, in_sems.at[4]))
    loads.append(pltpu.make_async_copy(ig_in, ig_buf, in_sems.at[5]))
    stores = [
        pltpu.make_async_copy(src, dst, out_sems.at[n])
        for n, (src, dst) in enumerate(
            ((out_buf, out_ref), (ig_buf, ig_ref), (ew_out, ew_ref), (dw_out, dw_ref))
        )
    ]
    for copy in loads:
        copy.start()
    core = lax.axis_index("head")
    UB = gf_ref.shape[2] // 3
    HW = 3 * HEAD
    for n in range(4):
        loads[n].wait()
        for kind in (0, 1):
            ew_out[:, kind, n * UB : n * UB + UB] = gf_in[n, :, kind * UB : kind * UB + UB].astype(F32)
        dw_out[:, n * UB : n * UB + UB] = gf_in[n, :, 2 * UB : 3 * UB].astype(F32)
    stores[2].start()
    stores[3].start()
    for n in (0, 1):
        loads[4 + n].wait()
        stores[n].start()
    sides = [
        jnp.concatenate([ga_ref[parity, 0], ga_ref[parity, 1]], axis=1).astype(F32)
        for parity in (0, 1)
    ]
    for kind in range(4):
        cols = slice(kind * HW, kind * HW + HW)
        both = jnp.concatenate([sides[0][:, cols], sides[1][:, cols]], axis=1)
        if kind < 3:
            pw_ref[kind] = both
        else:
            ow_ref[...] = both
    D = early_ref.shape[1]
    for kind in (0, 1):
        first, second = late_ref[2 * kind : 2 * kind + 1], late_ref[2 * kind + 1 : 2 * kind + 2]
        pair = jnp.where(core == 0, first, second)
        pb_ref[kind : kind + 1, 0:HW] = pair[:, 0:HW]
        pb_ref[kind : kind + 1, HW : 2 * HW] = pair[:, D // 2 : D // 2 + HW]
        for h in (0, 1):
            low, high = 6 + 2 * kind + h, 10 + 2 * kind + h
            row = jnp.where(core == 0, early_ref[low : low + 1, :], early_ref[high : high + 1, :])
            eb_ref[kind : kind + 1, h * D : h * D + D] = row
    for row, ref in enumerate((ob_ref, g1_ref, s1_ref, db_ref, g2_ref, s2_ref)):
        ref[...] = early_ref[row : row + 1, :].reshape(D)
    for copy in stores:
        copy.wait()


def planes(
    layer_input,
    sequence_lengths,
    alibi_slopes,
    project_weight,
    project_bias,
    output_weight,
    output_bias,
    first_gain,
    first_shift,
    expand_weight,
    expand_bias,
    down_weight,
    down_bias,
    second_gain,
    second_shift,
    layer_cotangent,
):
    batches, tokens, width = layer_input.shape
    units = expand_weight.shape[2]
    shard = project_weight.shape[0]
    half_width = project_weight.shape[2]
    rows = 4 * tokens
    unit = units // 4
    vmem = pl.BlockSpec(memory_space=pltpu.VMEM)
    hbm = pl.BlockSpec(memory_space=pl.ANY)
    smem = pl.BlockSpec(memory_space=pltpu.SMEM)
    dma = pltpu.SemaphoreType.DMA
    full = pltpu.VMEM((8, tokens, width), BF)
    head = pltpu.VMEM((6, rows, HEAD), BF)
    own = pltpu.VMEM((2, tokens, width), F32)
    hidden = pltpu.VMEM((2 * rows, 2 * unit), BF)
    halves = pltpu.VMEM((4, 2, 2, tokens, width // 2), BF)
    shape = jax.ShapeDtypeStruct
    outs = pl.pallas_call(
        layer_kernel,
        out_shape=(
            shape((batches, tokens, width), BF),
            shape((batches, tokens, width), F32),
            shape((2, 2, shard, half_width), BF),
            shape((4, shard, 3 * unit), BF),
            shape((16, width), F32),
            shape((8, width), F32),
        ),
        in_specs=[vmem] * 4 + [hbm] * 2 + [smem] * 2 + [vmem] * 8,
        out_specs=(vmem,) * 6,
        scratch_shapes=[
            full, full, full, full,
            pltpu.VMEM((width, width), BF),
            pltpu.VMEM((2, width, 2 * unit), BF),
            pltpu.VMEM((width, 2 * unit), BF),
            pltpu.VMEM((2, 16, units), F32),
            pltpu.VMEM((shard, width), BF),
            pltpu.VMEM((2, 8, tokens, width), BF),
            halves, halves, halves,
            head, head, head, head,
            pltpu.VMEM((6, rows, rows), BF),
            pltpu.VMEM((6, rows, HEAD), F32),
            pltpu.VMEM((2, rows, 3 * HEAD), BF),
            pltpu.VMEM((2, rows, 9 * HEAD), BF),
            pltpu.VMEM((rows, rows), BF),
            pltpu.VMEM((3, 3, rows, HEAD), BF),
            pltpu.VMEM((2, rows, rows), F32),
            hidden, hidden, hidden,
            pltpu.VMEM((2, 2 * rows, 2 * unit), BF),
            pltpu.VMEM((8, unit), F32),
            own, own,
            pltpu.VMEM((2, tokens, 1), F32),
            own, own,
            pltpu.VMEM((2, width, 3 * unit), BF),
            pltpu.VMEM((width, 3 * unit), BF),
            pltpu.VMEM((4, shard, 3 * unit), BF),
            pltpu.VMEM((2, width, half_width), BF),
            pltpu.VMEM((width, half_width), BF),
            pltpu.VMEM((4, shard, half_width), BF),
            pltpu.VMEM((shard, half_width), BF),
            pltpu.VMEM((10, 16, width), F32),
            pltpu.VMEM((10, 8, width), F32),
            pltpu.VMEM((3, 8, 128), F32),
            dma((4, 2, 4)), dma((4, 2, 4)),
            dma((4, 2, 6)), dma((4, 2, 6)),
            dma((2,)),
            dma((5, 2)), dma((5, 2)),
            dma((2, 4, 2)), dma((2, 4, 2)),
            dma((5,)),
            dma((3,)), dma((3,)),
            dma((2,)), dma((2,)),
            dma((2, 4)), dma((2, 4)),
            dma((2, 4)), dma((3, 4)),
            dma((5,)), dma((5,)),
            dma((5,)), dma((5,)),
            dma((2, 2)), dma((2, 2)),
        ],
        compiler_params=pltpu.CompilerParams(
            collective_id=0, has_side_effects=True, vmem_limit_bytes=VMEM_BYTES
        ),
        name="encoder_layer",
    )(
        layer_input, layer_cotangent, jnp.transpose(project_weight, (1, 0, 2)), output_weight.T,
        jnp.transpose(expand_weight, (1, 0, 2)), down_weight.T, jnp.transpose(sequence_lengths, (2, 1, 0)), alibi_slopes,
        project_bias, expand_bias, output_bias, first_gain, first_shift, down_bias, second_gain, second_shift,
    )
    layer_output, input_gradient, attn, feed, early, late = outs
    vector = shape((width,), F32)
    results = pl.pallas_call(
        result_kernel,
        out_shape=(
            shape((batches, tokens, width), BF),
            shape((batches, tokens, width), F32),
            shape((3, shard, half_width), F32),
            shape(project_bias.shape, F32),
            shape((shard, half_width), F32),
            vector, vector, vector,
            shape(expand_weight.shape, F32),
            shape(expand_bias.shape, F32),
            shape((shard, units), F32),
            vector, vector, vector,
        ),
        in_specs=[vmem, hbm, vmem, vmem, hbm, hbm],
        out_specs=(hbm,) * 2 + (vmem,) * 6 + (hbm, vmem, hbm) + (vmem,) * 3,
        scratch_shapes=[
            pltpu.VMEM(feed.shape, BF),
            pltpu.VMEM(layer_output.shape, BF),
            pltpu.VMEM(input_gradient.shape, F32),
            pltpu.VMEM(expand_weight.shape, F32),
            pltpu.VMEM((shard, units), F32),
            dma((6,)), dma((4,)),
        ],
        compiler_params=pltpu.CompilerParams(vmem_limit_bytes=VMEM_BYTES),
        name="gradient_results",
    )(attn, feed, early, late, layer_output, input_gradient)
    results = list(results)
    results[2] = jnp.transpose(results[2], (1, 0, 2))
    results[4] = results[4].T
    results[10] = results[10].T
    return tuple(results)


def fits(mesh):
    shape = dict(mesh.shape)
    return shape["dp"] == 4 and shape["blk"] == 4 and shape["head"] == 2


def solution(mesh):
    in_specs = (
        P(None, ("dp", "blk"), None),
        P(None, "dp", None),
        P("head"),
        P("dp", None, "head"),
        P(None, "head"),
        P("head", "dp"),
        P(),
        P(),
        P(),
        P("dp", None, "head"),
        P(None, "head"),
        P("head", "dp"),
        P(),
        P(),
        P(),
        P(None, ("dp", "blk"), None),
    )
    out_specs = (
        P(None, ("dp", "blk"), None),
        P(None, ("dp", "blk"), None),
        P("dp", None, "head"),
        P(None, "head"),
        P("head", "dp"),
        P(),
        P(),
        P(),
        P("dp", None, "head"),
        P(None, "head"),
        P("head", "dp"),
        P(),
        P(),
        P(),
    )
    body = planes if fits(mesh) else general
    return jax.shard_map(body, mesh=mesh, in_specs=in_specs, out_specs=out_specs, check_vma=False)
```

```python
import functools
import math

import jax
import jax.numpy as jnp
from jax import lax
from jax.experimental import pallas as pl
from jax.experimental.pallas import tpu as pltpu
from jax.sharding import PartitionSpec as P

EPSILON = 1e-12
MASKED = -1e30


def shifted(value, axis, steps):
    count = lax.axis_size(axis)
    pairs = [(source, (source + steps) % count) for source in range(count)]
    return lax.ppermute(value, axis, pairs)


def normalize(rows, gain, shift):
    mean = jnp.mean(rows, axis=-1, keepdims=True)
    centered = rows - mean
    spread = jnp.mean(centered * centered, axis=-1, keepdims=True)
    return centered * lax.rsqrt(spread + EPSILON) * gain + shift


def gelu_product(gate_part, up_part):
    return jax.nn.gelu(gate_part, approximate=False) * up_part


def sequence_ids(lengths, positions):
    first = lengths[:, 0:1]
    second = first + lengths[:, 1:2]
    later = (positions[None, :] >= first).astype(jnp.int32)
    return later + (positions[None, :] >= second).astype(jnp.int32)


def block_scores(query, keys, slopes, query_pos, key_pos, query_seq, key_seq):
    scale = query.shape[-1] ** (-0.5)
    raw = jnp.einsum("mqhd,mkhd->mhqk", query, keys, preferred_element_type=jnp.float32)
    distance = jnp.abs(query_pos[:, None] - key_pos[None, :]).astype(jnp.float32)
    scores = raw * scale - slopes[None, :, None, None] * distance[None, None]
    same = (query_seq[:, :, None] == key_seq[:, None, :])[:, None]
    return (jnp.where(same, scores, MASKED), same)


def forward_update(state, query, keys, values, slopes, query_pos, key_pos, query_seq, key_seq):
    top, total, accum = state
    scores, same = block_scores(query, keys, slopes, query_pos, key_pos, query_seq, key_seq)
    new_top = jnp.maximum(top, jnp.max(scores, axis=-1))
    weights = jnp.where(same, jnp.exp(scores - new_top[..., None]), 0.0)
    factor = jnp.exp(top - new_top)
    total = total * factor + jnp.sum(weights, axis=-1)
    update = jnp.einsum(
        "mhqk,mkhd->mqhd", weights.astype(jnp.bfloat16), values, preferred_element_type=jnp.float32
    )
    accum = accum * jnp.transpose(factor, (0, 2, 1))[..., None] + update
    return (new_top, total, accum)


def over_blocks(function, state, arrays, start):
    count_rows = arrays[0].shape[1]
    block = math.gcd(count_rows, 512)
    if block == count_rows:
        return function(state, arrays, start)

    def step(index, carry):
        offset = index * block
        blocks = tuple((lax.dynamic_slice_in_dim(item, offset, block, 1) for item in arrays))
        return function(carry, blocks, start + offset)

    return lax.fori_loop(0, count_rows // block, step, state)


def general(
    layer_input,
    sequence_lengths,
    alibi_slopes,
    project_weight,
    project_bias,
    output_weight,
    output_bias,
    first_gain,
    first_shift,
    expand_weight,
    expand_bias,
    down_weight,
    down_bias,
    second_gain,
    second_shift,
    layer_cotangent,
):
    batches, tokens, width = layer_input.shape
    heads = alibi_slopes.shape[0]
    local_width = project_weight.shape[2]
    head_size = local_width // heads
    units = expand_weight.shape[2]
    rows_all = batches * tokens
    scale = head_size ** (-0.5)
    project_full, output_full, expand_full, down_full = (
        lax.all_gather(project_weight, "dp", axis=0, tiled=True),
        lax.all_gather(output_weight, "dp", axis=1, tiled=True),
        lax.all_gather(expand_weight, "dp", axis=0, tiled=True),
        lax.all_gather(down_weight, "dp", axis=1, tiled=True),
    )
    lengths = sequence_lengths.reshape(batches, 3)
    cycle_index = lax.axis_index("blk")
    cycle_size = lax.axis_size("blk")
    own_pos = cycle_index * tokens + jnp.arange(tokens, dtype=jnp.int32)
    own_seq = sequence_ids(lengths, own_pos)

    def split_heads(item):
        return item.reshape(item.shape[0], item.shape[1], heads, head_size)

    flat_input = layer_input.reshape(rows_all, width)
    mixed = jnp.dot(
        flat_input, project_full.reshape(width, 3 * local_width), preferred_element_type=jnp.float32
    )
    query = (
        (mixed[:, :local_width] + project_bias[0])
        .astype(jnp.bfloat16)
        .reshape(batches, tokens, local_width)
    )
    keys = (
        mixed[:, local_width : 2 * local_width]
        .astype(jnp.bfloat16)
        .reshape(batches, tokens, local_width)
    )
    values = (
        (mixed[:, 2 * local_width :] + project_bias[1])
        .astype(jnp.bfloat16)
        .reshape(batches, tokens, local_width)
    )
    query_heads = split_heads(query)
    initial = (
        jnp.full((batches, heads, tokens), MASKED, jnp.float32),
        jnp.zeros((batches, heads, tokens), jnp.float32),
        jnp.zeros((batches, tokens, heads, head_size), jnp.float32),
    )

    def inner(carry, blocks, block_start):
        key_pos = block_start + jnp.arange(blocks[0].shape[1], dtype=jnp.int32)
        key_seq = sequence_ids(lengths, key_pos)
        return forward_update(
            carry,
            query_heads,
            split_heads(blocks[0]),
            split_heads(blocks[1]),
            alibi_slopes,
            own_pos,
            key_pos,
            own_seq,
            key_seq,
        )

    top, total, accum = over_blocks(
        inner,
        initial,
        (
            lax.all_gather(keys, "blk", axis=1, tiled=True),
            lax.all_gather(values, "blk", axis=1, tiled=True),
        ),
        jnp.int32(0),
    )
    context = accum / jnp.transpose(total, (0, 2, 1))[..., None]
    log_total = top + jnp.log(total)
    context_low = context.astype(jnp.bfloat16).reshape(rows_all, local_width)
    branch_part = jnp.dot(context_low, output_full, preferred_element_type=jnp.float32)
    branch = lax.psum(branch_part.astype(jnp.bfloat16), "head").astype(jnp.float32) + output_bias
    first_in = flat_input.astype(jnp.float32) + branch
    first_out, first_pull = jax.vjp(normalize, first_in, first_gain, first_shift)
    first_low = first_out.astype(jnp.bfloat16)
    expanded = jnp.dot(
        first_low, expand_full.reshape(width, 2 * units), preferred_element_type=jnp.float32
    )
    expanded = expanded + expand_bias.reshape(2 * units)
    hidden_act, gelu_pull = jax.vjp(gelu_product, expanded[:, :units], expanded[:, units:])
    hidden_low = hidden_act.astype(jnp.bfloat16)
    feed_part = jnp.dot(hidden_low, down_full, preferred_element_type=jnp.float32)
    feed = lax.psum(feed_part.astype(jnp.bfloat16), "head").astype(jnp.float32) + down_bias
    second_in = first_out + feed
    result, second_pull = jax.vjp(normalize, second_in, second_gain, second_shift)
    layer_output = result.astype(jnp.bfloat16).reshape(batches, tokens, width)
    grad_result = layer_cotangent.reshape(rows_all, width).astype(jnp.float32)
    grad_second, second_gain_grad, second_shift_grad = second_pull(grad_result)
    grad_feed = grad_second.astype(jnp.bfloat16)
    down_bias_grad = jnp.sum(grad_feed.astype(jnp.float32), axis=0)
    down_part = jnp.einsum("rf,rd->fd", hidden_low, grad_feed, preferred_element_type=jnp.float32)
    grad_hidden = jnp.einsum("rd,fd->rf", grad_feed, down_full, preferred_element_type=jnp.float32)
    grad_gate, grad_up = gelu_pull(grad_hidden)
    grad_expanded = jnp.concatenate([grad_gate, grad_up], axis=1).astype(jnp.bfloat16)
    expand_bias_grad = jnp.sum(grad_expanded.astype(jnp.float32), axis=0).reshape(2, units)
    expand_part = jnp.einsum(
        "rd,rf->df", first_low, grad_expanded, preferred_element_type=jnp.float32
    ).reshape(width, 2, units)
    first_back = jnp.einsum(
        "rf,df->rd",
        grad_expanded,
        expand_full.reshape(width, 2 * units),
        preferred_element_type=jnp.float32,
    )
    grad_first = grad_second + lax.psum(first_back.astype(jnp.bfloat16), "head").astype(jnp.float32)
    grad_first_in, first_gain_grad, first_shift_grad = first_pull(grad_first)
    grad_branch = grad_first_in.astype(jnp.bfloat16)
    output_bias_grad = jnp.sum(grad_branch.astype(jnp.float32), axis=0)
    output_part = jnp.einsum(
        "rc,rd->cd", context_low, grad_branch, preferred_element_type=jnp.float32
    )
    grad_context = jnp.einsum(
        "rd,cd->rc", grad_branch, output_full, preferred_element_type=jnp.float32
    )
    grad_context = grad_context.astype(jnp.bfloat16).reshape(batches, tokens, local_width)
    grad_heads = split_heads(grad_context)
    delta_rows = jnp.sum(grad_heads.astype(jnp.float32) * context, axis=-1)
    delta_heads = jnp.transpose(delta_rows, (0, 2, 1))
    zeros_heads = jnp.zeros((batches, tokens, heads, head_size), jnp.float32)
    zeros_flat = jnp.zeros((batches, tokens, local_width), jnp.float32)

    def cycle_step(carry, anchor):
        keys_now, values_now, grad_keys_now, grad_values_now, grad_query = carry
        key_pos = anchor * tokens + jnp.arange(tokens, dtype=jnp.int32)
        key_seq = sequence_ids(lengths, key_pos)
        keys_block = split_heads(keys_now)
        values_block = split_heads(values_now)
        scores, same = block_scores(
            query_heads, keys_block, alibi_slopes, own_pos, key_pos, own_seq, key_seq
        )
        weights = jnp.where(same, jnp.exp(scores - log_total[..., None]), 0.0)
        grad_prob = jnp.einsum(
            "mqhd,mkhd->mhqk", grad_heads, values_block, preferred_element_type=jnp.float32
        )
        grad_score = (weights * (grad_prob - delta_heads[..., None])).astype(jnp.bfloat16)
        grad_query = (
            grad_query
            + jnp.einsum(
                "mhqk,mkhd->mqhd", grad_score, keys_block, preferred_element_type=jnp.float32
            )
            * scale
        )
        key_term = (
            jnp.einsum(
                "mhqk,mqhd->mkhd", grad_score, query_heads, preferred_element_type=jnp.float32
            )
            * scale
        )
        value_term = jnp.einsum(
            "mhqk,mqhd->mkhd",
            weights.astype(jnp.bfloat16),
            grad_heads,
            preferred_element_type=jnp.float32,
        )
        grad_keys_now = grad_keys_now + key_term.reshape(grad_keys_now.shape)
        grad_values_now = grad_values_now + value_term.reshape(grad_values_now.shape)
        return (keys_now, values_now, grad_keys_now, grad_values_now, grad_query)

    def cycle_turn(index, carry):
        anchor = (cycle_index - index) % cycle_size
        updated = cycle_step(carry, anchor)
        moved = (
            shifted(updated[0], "blk", 1),
            shifted(updated[1], "blk", 1),
            shifted(updated[2].astype(jnp.bfloat16), "blk", 1).astype(jnp.float32),
            shifted(updated[3].astype(jnp.bfloat16), "blk", 1).astype(jnp.float32),
        )
        return (
            moved[0],
            moved[1],
            moved[2].astype(jnp.float32),
            moved[3].astype(jnp.float32),
            updated[4],
        )

    carry = lax.fori_loop(
        0, cycle_size - 1, cycle_turn, (keys, values, zeros_flat, zeros_flat, zeros_heads)
    )
    final = cycle_step(carry, (cycle_index + 1) % cycle_size)
    returned = (
        shifted(final[2].astype(jnp.bfloat16), "blk", 1).astype(jnp.float32),
        shifted(final[3].astype(jnp.bfloat16), "blk", 1).astype(jnp.float32),
    )
    grad_keys = returned[0].astype(jnp.float32)
    grad_values = returned[1].astype(jnp.float32)
    grad_query = final[4].reshape(batches, tokens, local_width)
    grad_mixed = jnp.concatenate(
        [
            grad_query.reshape(rows_all, local_width),
            grad_keys.reshape(rows_all, local_width),
            grad_values.reshape(rows_all, local_width),
        ],
        axis=1,
    ).astype(jnp.bfloat16)
    project_bias_grad = jnp.stack(
        [
            jnp.sum(grad_mixed[:, :local_width].astype(jnp.float32), axis=0),
            jnp.sum(grad_mixed[:, 2 * local_width :].astype(jnp.float32), axis=0),
        ]
    )
    project_part = jnp.einsum(
        "rd,rc->dc", flat_input, grad_mixed, preferred_element_type=jnp.float32
    ).reshape(width, 3, local_width)
    input_back = jnp.einsum(
        "rc,dc->rd",
        grad_mixed,
        project_full.reshape(width, 3 * local_width),
        preferred_element_type=jnp.float32,
    )
    input_gradient = grad_first_in + lax.psum(input_back.astype(jnp.bfloat16), "head").astype(
        jnp.float32
    )
    shards = (
        lax.psum_scatter(
            project_part.astype(jnp.bfloat16), "dp", scatter_dimension=0, tiled=True
        ).astype(jnp.float32),
        lax.psum_scatter(
            output_part.astype(jnp.bfloat16), "dp", scatter_dimension=1, tiled=True
        ).astype(jnp.float32),
        lax.psum_scatter(
            expand_part.astype(jnp.bfloat16), "dp", scatter_dimension=0, tiled=True
        ).astype(jnp.float32),
        lax.psum_scatter(
            down_part.astype(jnp.bfloat16), "dp", scatter_dimension=1, tiled=True
        ).astype(jnp.float32),
    )
    totals = (
        lax.psum(shards[0].astype(jnp.bfloat16), "blk").astype(jnp.float32),
        lax.psum(shards[1].astype(jnp.bfloat16), "blk").astype(jnp.float32),
        lax.psum(shards[2].astype(jnp.bfloat16), "blk").astype(jnp.float32),
        lax.psum(shards[3].astype(jnp.bfloat16), "blk").astype(jnp.float32),
    )
    small = lax.psum(
        (
            project_bias_grad,
            output_bias_grad,
            first_gain_grad,
            first_shift_grad,
            expand_bias_grad,
            down_bias_grad,
            second_gain_grad,
            second_shift_grad,
        ),
        ("dp", "blk"),
    )
    return (
        layer_output,
        input_gradient.reshape(batches, tokens, width),
        totals[0],
        small[0],
        totals[1],
        small[1],
        small[2],
        small[3],
        totals[2],
        small[4],
        totals[3],
        small[5],
        small[6],
        small[7],
    )


MESH = pl.DeviceIdType.MESH
BF = jnp.bfloat16
F32 = jnp.float32
FAR = 1e33
VMEM_BYTES = 63 << 20
HEAD = 64


def dot(a, b):
    return lax.dot_general(a, b, (((1,), (0,)), ((), ())), preferred_element_type=F32)


def dot_nt(a, b):
    return lax.dot_general(a, b, (((1,), (1,)), ((), ())), preferred_element_type=F32)


def dot_tn(a, b):
    return lax.dot_general(a, b, (((0,), (0,)), ((), ())), preferred_element_type=F32)


def column_sum(rows):
    return jnp.sum(rows, axis=0, keepdims=True)


def row_mean(rows):
    return jnp.mean(rows, axis=-1, keepdims=True)


def standardize(rows):
    centered = rows - row_mean(rows)
    inverse = lax.rsqrt(row_mean(centered * centered) + EPSILON)
    return centered * inverse, inverse


def standardize_back(grad, normal, inverse):
    return inverse * (grad - row_mean(grad) - normal * row_mean(grad * normal))


def layer_kernel(
    x_ref, cot_ref, pw_ref, ow_ref, ew_ref, dw_ref, len_ref, slope_ref, pb_ref, eb_ref,
    ob_ref, g1_ref, s1_ref, db_ref, g2_ref, s2_ref,
    out_ref, ig_ref, ga_ref, gf_ref, early_ref, late_ref,
    x_full, first_full, feed_full, branch_full,
    w_attn, w_gu, w_down, packs, own_attn,
    part, r1x, r1y, r2,
    q_s, k_s, v_s, g_s, p_s, ctx_s, ctx_cat, dqkv, ds_s, dq_s, far_s,
    act_s, upd_s, hid_s, dgu_s, eb_acc,
    first_own, n1_s, a1_s, gr2_s, gr1_s,
    dwd, dwd_in, dwd_z, dwe, dwe_in, dwe_z, dwa, dwa_in, dwa_z, fin_a,
    early, late, slope_s,
    ag_ss, ag_rs, rs_ss, rs_rs, pk_sem, wa_ss, wa_rs, wf_ss, wf_rs, wl_sem, wc_ss, wc_rs,
    gc_ss, gc_rs, gz_ss, gz_rs, gp_ss, gp_rs, ge_ss, ge_rs, gl_ss, gl_rs, io_ss, io_rs,
):
    z, b, c = lax.axis_index("dp"), lax.axis_index("blk"), lax.axis_index("head")
    half, odd = b // 2, b % 2
    xor = jnp.bitwise_xor
    other = 1 - c
    bx, by, bd = xor(b, 1), xor(b, 2), xor(b, 3)
    sib, xdev, ydev = (z, b, other), (z, bx, c), (z, by, c)
    near, far, opposite = ((xor(z, k), b, c) for k in (1, 2, 3))
    inner = jnp.logical_or(z == 1, z == 2)
    outer = jnp.logical_not(inner)
    T = x_ref.shape[1]
    D = x_ref.shape[2]
    H2 = D // 2
    ROWS = 4 * T
    DZ = pw_ref.shape[1]
    UB = dw_ref.shape[1] // 4
    HW = 3 * HEAD
    S = T // 2
    lo, hi, both = pl.ds(0, H2), pl.ds(H2, H2), pl.ds(0, D)

    def chunk(index, size):
        return pl.ds(pl.multiple_of(index * size, size), size)

    mine_z, near_z, far_z, opposite_z = (chunk(xor(z, k), DZ) for k in range(4))
    started = []

    def raw(src, dst, ss, rs, dev):
        return pltpu.make_async_remote_copy(
            src_ref=src, dst_ref=dst, send_sem=ss, recv_sem=rs, device_id=dev, device_id_type=MESH
        )

    class Copy:
        def __init__(self, *args):
            self.copy = raw(*args)
            self.sent = self.received = False

        def start(self):
            self.copy.start()
            started.append(self)

        def wait_recv(self):
            self.copy.wait_recv()
            self.received = True

        def wait_send(self):
            self.copy.wait_send()
            self.sent = True

        def finish(self):
            if not self.received:
                self.wait_recv()
            if not self.sent:
                self.wait_send()

    partners = [(z, xor(b, k), cc) for k in (1, 2, 3) for cc in (c, other)] + [sib]
    partners += [(xor(z, k), b, cc) for k in (1, 2, 3) for cc in (c, other)]
    barrier = pltpu.get_barrier_semaphore()
    for dev in partners:
        pl.semaphore_signal(barrier, inc=1, device_id=dev, device_id_type=MESH)

    class Gather:
        def __init__(self, full, phase, m, r):
            ss, rs = ag_ss.at[phase, m, r], ag_rs.at[phase, m, r]
            part_rows = pl.ds(r * S, S)

            def send(slot, lanes, index, dev):
                rows = full.at[m * 4 + slot, part_rows, lanes]
                return Copy(rows, rows, ss.at[index], rs.at[index], dev)

            self.cx, self.cy = send(b, both, 0, xdev), send(b, both, 1, ydev)
            self.fx, self.fy = send(bx, lo, 2, ydev), send(by, hi, 3, xdev)

        def start(self):
            self.cx.start()
            self.cy.start()

        def mid_x(self):
            self.cx.wait_recv()
            self.fx.start()

        def mid_y(self):
            self.cy.wait_recv()
            self.fy.start()

        def end(self):
            for copy in (self.fx, self.fy):
                if not copy.received:
                    copy.wait_recv()

    class Scatter:
        def __init__(self, phase, m, r):
            ss, rs = rs_ss.at[phase, m, r], rs_rs.at[phase, m, r]
            buf = part.at[phase % 2]
            rows = pl.ds(r * S, S)
            ix, iy, i2 = r1x.at[phase, m], r1y.at[phase, m], r2.at[phase, m]
            self.own, self.sx, self.sy = m * 4 + b, m * 4 + bx, m * 4 + by
            self.buf, self.rows, self.ix, self.iy, self.i2 = buf, rows, ix, iy, i2

            def send(slot, lanes, into, at, index, dev):
                src = buf.at[m * 4 + slot, rows, lanes]
                return Copy(src, into.at[at, rows], ss.at[index], rs.at[index], dev)

            self.xd = send(bd, lo, ix, 1, 0, xdev)
            self.yd = send(bd, hi, iy, 1, 1, ydev)
            self.xo = send(bx, lo, ix, 0, 2, xdev)
            self.yo = send(by, hi, iy, 0, 3, ydev)
            self.y2 = send(by, lo, i2, 0, 4, ydev)
            self.x2 = send(bx, hi, i2, 1, 5, xdev)

        def start(self):
            for copy in (self.xd, self.yd, self.xo, self.yo):
                copy.start()

        def add(self, slot, lanes, term):
            value = self.buf[slot, self.rows, lanes].astype(F32) + term[1, self.rows].astype(F32)
            self.buf[slot, self.rows, lanes] = value.astype(BF)

        def mid_x(self):
            self.xd.wait_recv()
            self.add(self.sy, lo, self.ix)
            self.y2.start()

        def mid_y(self):
            self.yd.wait_recv()
            self.add(self.sx, hi, self.iy)
            self.x2.start()

        def end(self):
            for copy in (self.xo, self.yo, self.y2, self.x2):
                copy.wait_recv()
            mine = self.buf[self.own, self.rows].astype(F32)
            rows = self.rows
            low = mine[:, :H2] + self.ix[0, rows].astype(F32) + self.i2[0, rows].astype(F32)
            high = mine[:, H2:] + self.iy[0, rows].astype(F32) + self.i2[1, rows].astype(F32)
            return jnp.concatenate([low, high], axis=1)

        def drain(self):
            for copy in (self.xd, self.yd, self.xo, self.yo, self.y2, self.x2):
                copy.wait_send()

    def chunks(kind, *args):
        return [[kind(*args, m, r) for r in (0, 1)] for m in (0, 1)]

    gather_x, gather_first = chunks(Gather, x_full, 0), chunks(Gather, first_full, 1)
    gather_feed, gather_branch = chunks(Gather, feed_full, 2), chunks(Gather, branch_full, 3)
    sum_branch, sum_feed = chunks(Scatter, 0), chunks(Scatter, 1)
    sum_first, sum_input = chunks(Scatter, 2), chunks(Scatter, 3)

    class Column:
        def __init__(self, pieces, ss, rs):
            self.pieces, self.ss, self.rs = pieces, ss, rs

        def copy(self, dz, index, src, dst, dev):
            return raw(src, dst, self.ss.at[dz, index], self.rs.at[dz, index], dev)

        def copies(self):
            for dz in (2, 1, 3):
                for index, (src, place_at, core) in enumerate(self.pieces):
                    yield dz, self.copy(dz, index, src, place_at(mine_z), (xor(z, dz), b, core))

        def send(self):
            for dz, copy in self.copies():
                if dz != 3:
                    copy.start()

        def send_opposite(self):
            for dz, copy in self.copies():
                if dz == 3:
                    pl.when(inner)(copy.start)

        def sent(self):
            for dz, copy in self.copies():
                if dz == 3:
                    pl.when(inner)(copy.wait_send)
                else:
                    copy.wait_send()

        def arrival(self, dz, index):
            src, place_at, _ = self.pieces[index]
            self.copy(dz, index, src, place_at(mine_z), near).wait_recv()

        def passing(self, index):
            rows = self.pieces[index][1](far_z)
            return raw(rows, rows, self.ss.at[0, index], self.rs.at[3, index], near)

        def relay(self, index):
            self.arrival(2, index)
            pl.when(inner)(self.passing(index).start)

        def relay_all(self):
            for index in range(len(self.pieces)):
                self.relay(index)
            self.send_opposite()

        def relayed(self, index):
            pl.when(inner)(self.passing(index).wait_send)

        def rest(self, index):
            self.arrival(1, index)
            self.arrival(3, index)

    def attn_place(k):
        return lambda rows: w_attn.at[rows, pl.ds(k * H2, H2)]

    attn_pieces = [(own_attn.at[:, pl.ds(k * H2, H2)], attn_place(k), k) for k in (0, 1)]
    attn_column = Column(attn_pieces, wa_ss, wa_rs)
    attn_own = []
    for index, (src, place_at, core) in enumerate(attn_pieces):
        dst = place_at(mine_z)
        cross = raw(src, dst, wa_ss.at[4, index], wa_rs.at[4, index], sib)
        local = pltpu.make_async_copy(src, dst, wl_sem.at[index])
        attn_own.append((cross, local))
    gu_column = Column(
        [
            (ew_ref.at[0, :, chunk(b, UB)], lambda rows: w_gu.at[c, rows, pl.ds(0, UB)], c),
            (ew_ref.at[1, :, chunk(b, UB)], lambda rows: w_gu.at[c, rows, pl.ds(UB, UB)], c),
        ],
        wf_ss.at[0],
        wf_rs.at[0],
    )
    down_column = Column(
        [(dw_ref.at[:, chunk(b, UB)], lambda rows: w_down.at[rows, chunk(c, UB)], c)],
        wf_ss.at[1],
        wf_rs.at[1],
    )
    feed_own = []
    for index, (src, place_at, _) in enumerate(gu_column.pieces + down_column.pieces):
        feed_own.append(pltpu.make_async_copy(src, place_at(mine_z), wl_sem.at[2 + index]))

    def prepare():
        for copy in feed_own:
            copy.start()
        shards = [pw_ref[kind] for kind in range(3)] + [ow_ref[...]]
        own_attn[...] = jnp.concatenate(
            [jnp.where(odd == 0, item[:, 0:HW], item[:, HW : 2 * HW]) for item in shards], axis=1
        )
        for m in (0, 1):
            x_full[m * 4 + b] = x_ref[2 * c + m]
        for row in (0, 1):
            packs[c, row : row + 1, :] = eb_ref[row : row + 1, :]
            packs[c, row + 2 : row + 3, 0:H2] = pb_ref[row : row + 1, :]
        for i in range(6):
            packs[c, 10 + i : 11 + i, 0:128] = jnp.full((1, 128), slope_ref[i], F32)
        pl.semaphore_wait(barrier, len(partners))

    def start_attn():
        @pl.when(c == half)
        def _():
            attn_column.send()
            for index, (cross, local) in enumerate(attn_own):
                pl.when(c == index)(local.start)
                pl.when(c != index)(cross.start)

        pack_copy.start()

    pack_copy = Copy(packs.at[c], packs.at[c], pk_sem.at[0], pk_sem.at[1], sib)

    def constants():
        for m in (0, 1):
            start_one = len_ref[0, 0, 2 * c + m]
            start_two = start_one + len_ref[1, 0, 2 * c + m]
            for rb in range(4):
                rows = lax.broadcasted_iota(jnp.int32, (T, ROWS), 0) + rb * T
                cols = lax.broadcasted_iota(jnp.int32, (T, ROWS), 1)
                seq_r = (rows >= start_one).astype(jnp.int32) + (rows >= start_two).astype(jnp.int32)
                seq_c = (cols >= start_one).astype(jnp.int32) + (cols >= start_two).astype(jnp.int32)
                distance = jnp.abs(rows - cols).astype(F32)
                far_s[m, pl.ds(rb * T, T), :] = jnp.where(seq_r == seq_c, distance, FAR)
        early[...] = jnp.zeros_like(early)
        late[...] = jnp.zeros_like(late)
        eb_acc[...] = jnp.zeros_like(eb_acc)
        pack_copy.wait_recv()
        for i in range(3):
            low, high = packs[half, 10 + i : 11 + i, 0:128], packs[half, 13 + i : 14 + i, 0:128]
            slope_s[i] = jnp.broadcast_to(jnp.where(odd == 0, low, high), (8, 128))

    def relay_attn():
        for index in (0, 1):
            pl.when(c == index)(functools.partial(attn_column.relay, index))
        pl.when(c == half)(attn_column.send_opposite)

    lanes = w_attn.at[:, chunk(c, H2)]
    attn_share = Copy(lanes, lanes, wc_ss.at[0], wc_rs.at[0], sib)

    def share_attn():
        for index, (cross, local) in enumerate(attn_own):

            @pl.when(c == index)
            def _():
                pl.when(c == half)(local.wait)
                pl.when(c != half)(cross.wait_recv)
                attn_column.rest(index)

        attn_share.start()

    def vector(ref):
        return ref[...].reshape(1, D)

    def project(m):
        if m == 0:
            attn_share.wait_recv()
        for r in (0, 1):
            gather_x[m][r].end()
        biases = packs[half, 2:4, 0:H2]
        biases = jnp.where(odd == 0, biases[:, 0:HW], biases[:, HW : 2 * HW])

        def rows_of(t, _):
            rows = x_full[pl.ds(m * 4 + t * 2, 2)].reshape(2 * T, D)
            at = pl.ds(pl.multiple_of(t * 2 * T, 2 * T), 2 * T)
            mixed = dot(rows, w_attn[:, 0 : 3 * HW])
            query = (mixed[:, 0:HW] + biases[0:1]).astype(BF) * jnp.asarray(0.125, BF)
            keys = mixed[:, HW : 2 * HW].astype(BF)
            values = (mixed[:, 2 * HW : 3 * HW] + biases[1:2]).astype(BF)
            for i in range(3):
                cols = slice(i * HEAD, i * HEAD + HEAD)
                q_s[m * 3 + i, at, :] = query[:, cols]
                k_s[m * 3 + i, at, :] = keys[:, cols]
                v_s[m * 3 + i, at, :] = values[:, cols]
            return 0

        lax.fori_loop(0, 2, rows_of, 0)

    def attend(m, r):
        heads = [m * 3 + i for i in range(3)]

        def one(slot, _):
            at = pl.ds(pl.multiple_of(slot * T + r * S, S), S)
            reach = far_s[m, at, :]
            scores = [dot_nt(q_s[h, at, :], k_s[h]) for h in heads]
            scores = [item - slope_s[i][0:1, 0:1] * reach for i, item in enumerate(scores)]
            tops = [jnp.max(item, axis=-1, keepdims=True) for item in scores]
            weights = [jnp.exp(item - top) for item, top in zip(scores, tops)]
            totals = [jnp.sum(item, axis=-1, keepdims=True) for item in weights]
            probs = [(item * (1.0 / total)).astype(BF) for item, total in zip(weights, totals)]
            for h, item in zip(heads, probs):
                p_s[h, at, :] = item
                ctx_s[h, at, :] = dot(item, v_s[h])
            return 0

        lax.fori_loop(0, 4, one, 0)
        for slot in range(4):
            at = pl.ds(slot * T + r * S, S)
            cat = jnp.concatenate([ctx_s[m * 3 + i, at, :].astype(BF) for i in range(3)], axis=1)
            ctx_cat[m * 4 + slot, pl.ds(r * S, S), :] = cat
        total = sum_branch[m][r]
        put(total, m, r, dot_nt(take(ctx_cat, m, r), w_attn[:, 3 * HW : 4 * HW]))
        total.start()

    def put(total, m, r, rows):
        total.buf[m * 4 : m * 4 + 4, pl.ds(r * S, S), :] = rows.astype(BF).reshape(4, S, D)

    def take(refs, m, r):
        rows = refs[m * 4 : m * 4 + 4, pl.ds(r * S, S), :]
        return rows.reshape(4 * S, rows.shape[2])

    def keep(refs, m, r, lanes, rows):
        refs[m * 4 : m * 4 + 4, pl.ds(r * S, S), lanes] = rows.reshape(4, S, rows.shape[1])

    def first_norm(m, r):
        at = pl.ds(r * S, S)
        rows = x_ref[2 * c + m, at, :].astype(F32) + sum_branch[m][r].end() + vector(ob_ref)
        normal, inverse = standardize(rows)
        first = normal * vector(g1_ref) + vector(s1_ref)
        n1_s[m, at, :], a1_s[m, at, :] = normal, inverse
        first_own[m, at, :] = first
        first_full[m * 4 + b, at, :] = first.astype(BF)
        gather_first[m][r].start()

    def feed_forward(m, r):
        if m + r == 0:
            share_gu.wait_recv()
        gather_first[m][r].end()
        rows = take(first_full, m, r)
        for g in (0, 1):
            cols = pl.ds(g * UB, UB)
            bias = packs[g, 0:2, chunk(b, UB)]
            pair = dot(rows, w_gu[g])
            gate = pair[:, :UB] + bias[0:1]
            up = pair[:, UB:] + bias[1:2]
            cdf = 0.5 + 0.5 * lax.erf(gate * 0.7071067811865476)
            act = gate * cdf
            slope = cdf + gate * (jnp.exp(-0.5 * gate * gate) * 0.3989422804014327)
            keep(hid_s, m, r, cols, (act * up).astype(BF))
            keep(act_s, m, r, cols, act.astype(BF))
            keep(upd_s, m, r, cols, (up * slope).astype(BF))

    def feed_out(m, r):
        if m + r == 0:
            share_down.wait_recv()
        total = sum_feed[m][r]
        put(total, m, r, dot_nt(take(hid_s, m, r), w_down[...]))
        total.start()

    def add_early(row, rows):
        early[0, row : row + 1, :] += column_sum(rows)

    def second_norm(m, r):
        at = pl.ds(r * S, S)
        rows = first_own[m, at, :] + sum_feed[m][r].end() + vector(db_ref)
        normal, inverse = standardize(rows)
        out_ref[2 * c + m, at, :] = (normal * vector(g2_ref) + vector(s2_ref)).astype(BF)
        grad = cot_ref[2 * c + m, at, :].astype(F32)
        back = standardize_back(grad * vector(g2_ref), normal, inverse)
        gr2_s[m, at, :] = back
        low = back.astype(BF)
        feed_full[m * 4 + b, at, :] = low
        gather_feed[m][r].start()
        add_early(4, grad * normal)
        add_early(5, grad)
        add_early(3, low.astype(F32))
        if r == 1:
            send_rows(out_ref, 0, m)

    def feed_backward(m, r):
        gather_feed[m][r].end()
        sum_branch[m][r].drain()
        hidden = dot(take(feed_full, m, r), w_down[...])
        dgate = (hidden * take(upd_s, m, r).astype(F32)).astype(BF)
        dup = (hidden * take(act_s, m, r).astype(F32)).astype(BF)
        for g in (0, 1):
            cols = slice(g * UB, g * UB + UB)
            keep(dgu_s.at[g], m, r, pl.ds(0, UB), dgate[:, cols])
            keep(dgu_s.at[g], m, r, pl.ds(UB, UB), dup[:, cols])
        back = dot_nt(take(dgu_s.at[0], m, r), w_gu[0]) + dot_nt(take(dgu_s.at[1], m, r), w_gu[1])
        total = sum_first[m][r]
        put(total, m, r, back)
        total.start()
        for g in (0, 1):
            cols = slice(g * UB, g * UB + UB)
            eb_acc[2 * g : 2 * g + 1, :] += column_sum(dgate[:, cols].astype(F32))
            eb_acc[2 * g + 1 : 2 * g + 2, :] += column_sum(dup[:, cols].astype(F32))

    def down_weights():
        for m, r in ((0, 0), (0, 1), (1, 0), (1, 1)):
            gather_feed[m][r].end()

        def cols_of(t, _):
            at = chunk(t, 256)
            rows = feed_full[:, :, at].reshape(2 * ROWS, 256)
            down = dot_tn(rows, hid_s[...].reshape(2 * ROWS, 2 * UB)).astype(BF)
            for g in (0, 1):
                dwd[g, at, :] = down[:, g * UB : g * UB + UB]
            return 0

        lax.fori_loop(0, D // 256, cols_of, 0)

    def expand_weights(t):
        at = pl.ds(t * 256, 256)
        rows = first_full[:, :, at].reshape(2 * ROWS, 256)

        def units_of(g, _):
            dwe[g, at, :] = dot_tn(rows, dgu_s[g].reshape(2 * ROWS, 2 * UB)).astype(BF)
            return 0

        lax.fori_loop(0, 2, units_of, 0)

    def first_back(m, r):
        at = pl.ds(r * S, S)
        grad = gr2_s[m, at, :] + sum_first[m][r].end()
        normal = n1_s[m, at, :]
        back = standardize_back(grad * vector(g1_ref), normal, a1_s[m, at, :])
        gr1_s[m, at, :] = back
        low = back.astype(BF)
        branch_full[m * 4 + b, at, :] = low
        gather_branch[m][r].start()
        add_early(1, grad * normal)
        add_early(2, grad)
        add_early(0, low.astype(F32))

    def context_back(m):
        for r in (0, 1):
            gather_branch[m][r].end()
        def rows_of(t, _):
            at = pl.ds(pl.multiple_of(t * 2 * T, 2 * T), 2 * T)
            rows = branch_full[pl.ds(m * 4 + t * 2, 2)].reshape(2 * T, D)
            grads = dot(rows, w_attn[:, 3 * HW : 4 * HW]).astype(BF)
            for i in range(3):
                g_s[m * 3 + i, at, :] = grads[:, i * HEAD : i * HEAD + HEAD]
            return 0

        lax.fori_loop(0, 2, rows_of, 0)

    def attend_back(m, part):
        heads = [m * 3 + i for i in range(3)]

        def block(rb, _):
            at = chunk(rb, T)
            rows = [g_s[h, at, :] for h in heads]
            terms = [dot_nt(item, v_s[h]) for item, h in zip(rows, heads)]
            deltas = [
                jnp.sum(item.astype(F32) * ctx_s[h, at, :], axis=-1, keepdims=True)
                for item, h in zip(rows, heads)
            ]
            for i, h in enumerate(heads):
                score = (p_s[h, at, :].astype(F32) * (terms[i] - deltas[i])).astype(BF)
                ds_s[i, at, :] = score
                dq_s[0, i, at, :] = (dot(score, k_s[h]) * 0.125).astype(BF)
            return 0

        if part < 2:
            lax.fori_loop(2 * part, 2 * part + 2, block, 0)
        else:
            for i, h in enumerate(heads):
                dq_s[1, i] = dot_tn(q_s[h], ds_s[i]).T.astype(BF)
                dq_s[2, i] = dot_tn(g_s[h], p_s[h]).T.astype(BF)

    def input_back(m, r):
        if r == 0:
            for kind in range(3):
                cat = jnp.concatenate([dq_s[kind, i] for i in range(3)], axis=1)
                dqkv[m * 4 : m * 4 + 4, :, kind * HW : kind * HW + HW] = cat.reshape(4, T, HW)
                if kind != 1:
                    sums = column_sum(cat.astype(F32))
                    for h in (0, 1):
                        lanes = pl.ds(pl.multiple_of(odd * H2, H2), HW)
                        late[0, kind + h : kind + h + 1, lanes] += jnp.where(half == h, sums, 0.0)
        total = sum_input[m][r]
        sum_feed[m][r].drain()
        put(total, m, r, dot_nt(take(dqkv, m, r), w_attn[:, 0 : 3 * HW]))
        total.start()

    def attend_weights():
        def cols_of(t, _):
            at = chunk(t, 256)
            rows = x_full[:, :, at].reshape(2 * ROWS, 256)
            grads = dot_tn(rows, dqkv[...].reshape(2 * ROWS, 3 * HW)).astype(BF)
            dwa[0, at, :] = grads[:, 0:H2]
            dwa[1, at, 0:HW] = grads[:, H2 : 3 * HW]
            rows = branch_full[:, :, at].reshape(2 * ROWS, 256)
            outs = dot_tn(rows, ctx_cat[...].reshape(2 * ROWS, HW)).astype(BF)
            dwa[1, at, HW : 2 * HW] = outs
            return 0

        lax.fori_loop(0, D // 256, cols_of, 0)
        reduce_attn.swap.start()

    class Reduce:
        def __init__(self, index, buf, incoming, zin):
            self.buf, self.incoming, self.zin = buf, incoming, zin
            self.swap = Copy(buf.at[other], incoming, gc_ss.at[index], gc_rs.at[index], sib)

            def push(rows, slot, dev):
                ss, rs = gz_ss.at[index, slot], gz_rs.at[index, slot]
                return raw(buf.at[c, rows, :], zin.at[slot], ss, rs, dev)

            self.to_near = push(near_z, 0, near)
            self.to_far = push(far_z, 1, far)
            self.to_opposite = push(opposite_z, 2, opposite)
            self.by_near = push(opposite_z, 3, near)

        def join(self):
            self.swap.wait_recv()

            def add(rows):
                mine = self.buf[c, rows, :].astype(F32)
                self.buf[c, rows, :] = (mine + self.incoming[rows, :].astype(F32)).astype(BF)

            add(opposite_z)
            pl.when(outer)(self.by_near.start)
            pl.when(inner)(self.to_opposite.start)
            add(far_z)
            pl.when(outer)(self.to_far.start)
            add(near_z)
            self.to_near.start()
            add(mine_z)

        def relay(self):
            @pl.when(inner)
            def _():
                self.by_near.wait_recv()
                mine = self.buf[c, far_z, :].astype(F32)
                self.buf[c, far_z, :] = (mine + self.zin[3].astype(F32)).astype(BF)
                self.to_far.start()

        def total(self, put):
            self.to_near.wait_recv()
            self.to_far.wait_recv()

            def value():
                low = self.buf[c, mine_z, :].astype(F32)
                return low + self.zin[0].astype(F32) + self.zin[1].astype(F32)

            @pl.when(inner)
            def _():
                self.to_opposite.wait_recv()
                put((value() + self.zin[2].astype(F32)).astype(BF))

            @pl.when(outer)
            def _():
                put(value().astype(BF))

        def sent(self):
            self.to_near.wait_send()
            self.to_far.wait_send()
            pl.when(inner)(self.to_opposite.wait_send)
            pl.when(outer)(self.by_near.wait_send)

    reduce_down = Reduce(0, dwd, dwd_in, dwd_z)
    reduce_expand = Reduce(1, dwe, dwe_in, dwe_z)
    reduce_attn = Reduce(2, dwa, dwa_in, dwa_z)

    class Everywhere:
        def __init__(self, buf, ss, rs, result):
            devices = [near, far, sib, xdev, ydev]
            self.buf, self.result = buf, result
            self.copies = [
                Copy(buf.at[2 * i], buf.at[2 * i + 1], ss.at[i], rs.at[i], dev)
                for i, dev in enumerate(devices)
            ]

        def start(self):
            self.copies[0].start()

        def step(self, i):
            self.copies[i].wait_recv()
            value = self.buf[2 * i] + self.buf[2 * i + 1]
            if i + 1 < len(self.copies):
                self.buf[2 * i + 2] = value
                self.copies[i + 1].start()
            else:
                self.result[...] = value

    early_sum = Everywhere(early, ge_ss, ge_rs, early_ref)
    late_sum = Everywhere(late, gl_ss, gl_rs, late_ref)

    def early_start():
        for g in (0, 1):
            for kind in (0, 1):
                row = 6 + (2 * g + kind) * 2
                values = eb_acc[2 * g + kind : 2 * g + kind + 1, :]
                for h in (0, 1):
                    at = slice(row + h, row + h + 1)
                    early[0, at, chunk(odd, UB)] = jnp.where(half == h, values, 0.0)
        early_sum.start()

    share_gu = Copy(w_gu.at[c], w_gu.at[c], wc_ss.at[1], wc_rs.at[1], sib)
    down_lanes = w_down.at[:, chunk(c, UB)]
    share_down = Copy(down_lanes, down_lanes, wc_ss.at[2], wc_rs.at[2], sib)

    def take_weights(column, own, share):
        for index in range(len(column.pieces)):
            column.rest(index)
        for copy in own:
            copy.wait()
        share.start()

    def send_rows(refs, index, m):
        rows = refs.at[2 * c + m]
        Copy(rows, rows, io_ss.at[index, m], io_rs.at[index, m], sib).start()

    def finish_input(m, r):
        at = pl.ds(r * S, S)
        ig_ref[2 * c + m, at, :] = gr1_s[m, at, :] + sum_input[m][r].end()
        if r == 1:
            send_rows(ig_ref, 1, m)

    class Spread:
        def __init__(self, index, reduce, lanes):
            self.reduce, self.lanes = reduce, lanes
            ss, rs = gp_ss.at[index], gp_rs.at[index]

            def send(slot, rows, at, dev):
                piece = gf_ref.at[slot, rows, lanes]
                return Copy(piece, piece, ss.at[at], rs.at[at], dev)

            every, top, bottom = pl.ds(0, DZ), pl.ds(0, DZ // 2), pl.ds(DZ // 2, DZ // 2)
            self.cx, self.cy = send(b, every, 0, xdev), send(b, every, 1, ydev)
            self.fx, self.fy = send(bx, top, 2, ydev), send(by, bottom, 3, xdev)

        def start(self):
            def put_sum(value):
                gf_ref[b, :, self.lanes] = value

            self.reduce.total(put_sum)
            self.cx.start()
            self.cy.start()

        def mid(self):
            self.cx.wait_recv()
            self.fx.start()
            self.cy.wait_recv()
            self.fy.start()

    spread_down = Spread(0, reduce_down, pl.ds(2 * UB, UB))
    spread_expand = Spread(1, reduce_expand, pl.ds(0, 2 * UB))

    def finish_attn():
        def put_fin(value):
            fin_a[...] = value

        reduce_attn.total(put_fin)
        slot, rs = ga_ref.at[odd, c], gp_rs.at[2 + odd, c]
        copies = [raw(fin_a, slot, gp_ss.at[2, k], rs, (z, xor(b, k), half)) for k in (3, 1, 2)]
        cross = raw(fin_a, slot, gp_ss.at[2, 0], rs, sib)
        for copy in copies:
            copy.start()
        pl.when(c != half)(cross.start)

        @pl.when(c == half)
        def _():
            ga_ref[odd, c] = fin_a[...]

        for parity in (0, 1):
            for core in (0, 1):
                own = jnp.logical_and(c == half, jnp.logical_and(odd == parity, c == core))
                rs = gp_rs.at[2 + parity, core]
                arrival = raw(fin_a, ga_ref.at[parity, core], gp_ss.at[2, 0], rs, sib)
                pl.when(jnp.logical_not(own))(arrival.wait_recv)
        pl.when(c != half)(cross.wait_send)
        for copy in copies:
            copy.wait_send()

    def finish():
        @pl.when(c == half)
        def _():
            attn_column.sent()
            for index, (cross, _) in enumerate(attn_own):
                pl.when(c != index)(cross.wait_send)

        for index in (0, 1):
            pl.when(c == index)(functools.partial(attn_column.relayed, index))
        for column in (gu_column, down_column):
            column.sent()
            for index in range(len(column.pieces)):
                column.relayed(index)
        for item in (reduce_down, reduce_expand, reduce_attn):
            item.sent()
        for copy in started:
            copy.finish()

    steps = [
        prepare,
        start_attn,
        gather_x[0][0].start,
        gather_x[0][1].start,
        gather_x[1][0].start,
        gather_x[1][1].start,
        constants,
        gather_x[0][0].mid_x,
        gather_x[0][0].mid_y,
        gather_x[0][1].mid_x,
        gather_x[0][1].mid_y,
        relay_attn,
        gu_column.send,
        gather_x[1][0].mid_x,
        gather_x[1][0].mid_y,
        gather_x[1][1].mid_x,
        gather_x[1][1].mid_y,
        share_attn,
        lambda: project(0),
        lambda: attend(0, 0),
        lambda: attend(0, 1),
        lambda: project(1),
        sum_branch[0][0].mid_x,
        sum_branch[0][0].mid_y,
        lambda: attend(1, 0),
        sum_branch[0][1].mid_x,
        sum_branch[0][1].mid_y,
        gu_column.relay_all,
        lambda: first_norm(0, 0),
        down_column.send,
        lambda: attend(1, 1),
        sum_branch[1][0].mid_x,
        sum_branch[1][0].mid_y,
        lambda: first_norm(0, 1),
        gather_first[0][0].mid_x,
        gather_first[0][0].mid_y,
        sum_branch[1][1].mid_x,
        sum_branch[1][1].mid_y,
        lambda: take_weights(gu_column, feed_own[:2], share_gu),
        lambda: first_norm(1, 0),
        gather_first[0][1].mid_x,
        gather_first[0][1].mid_y,
        lambda: feed_forward(0, 0),
        lambda: first_norm(1, 1),
        down_column.relay_all,
        gather_first[1][0].mid_x,
        gather_first[1][0].mid_y,
        lambda: feed_forward(0, 1),
        gather_first[1][1].mid_x,
        gather_first[1][1].mid_y,
        lambda: take_weights(down_column, feed_own[2:], share_down),
        lambda: feed_forward(1, 0),
        lambda: feed_forward(1, 1),
        lambda: feed_out(0, 0),
        lambda: feed_out(0, 1),
        lambda: feed_out(1, 0),
        lambda: feed_out(1, 1),
        sum_feed[0][0].mid_x,
        sum_feed[0][0].mid_y,
        sum_feed[0][1].mid_x,
        sum_feed[0][1].mid_y,
        sum_feed[1][0].mid_x,
        sum_feed[1][0].mid_y,
        sum_feed[1][1].mid_x,
        sum_feed[1][1].mid_y,
        lambda: second_norm(0, 0),
        lambda: second_norm(0, 1),
        lambda: second_norm(1, 0),
        lambda: second_norm(1, 1),
        gather_feed[0][0].mid_x,
        gather_feed[0][0].mid_y,
        gather_feed[0][1].mid_x,
        gather_feed[0][1].mid_y,
        gather_feed[1][0].mid_x,
        gather_feed[1][0].mid_y,
        gather_feed[1][1].mid_x,
        gather_feed[1][1].mid_y,
        lambda: feed_backward(0, 0),
        lambda: feed_backward(0, 1),
        down_weights,
        sum_first[0][0].mid_x,
        sum_first[0][0].mid_y,
        reduce_down.swap.start,
        lambda: feed_backward(1, 0),
        sum_first[0][1].mid_x,
        sum_first[0][1].mid_y,
        lambda: feed_backward(1, 1),
        lambda: first_back(0, 0),
        reduce_down.join,
        sum_first[1][0].mid_x,
        sum_first[1][0].mid_y,
        lambda: expand_weights(0),
        lambda: expand_weights(1),
        sum_first[1][1].mid_x,
        sum_first[1][1].mid_y,
        lambda: first_back(0, 1),
        lambda: expand_weights(2),
        reduce_expand.swap.start,
        gather_branch[0][0].mid_x,
        gather_branch[0][0].mid_y,
        lambda: first_back(1, 0),
        reduce_down.relay,
        lambda: first_back(1, 1),
        early_start,
        reduce_expand.join,
        gather_branch[0][1].mid_x,
        gather_branch[0][1].mid_y,
        gather_branch[1][0].mid_x,
        gather_branch[1][0].mid_y,
        spread_down.start,
        lambda: early_sum.step(0),
        gather_branch[1][1].mid_x,
        gather_branch[1][1].mid_y,
        lambda: context_back(0),
        lambda: attend_back(0, 0),
        lambda: attend_back(0, 1),
        lambda: attend_back(0, 2),
        lambda: input_back(0, 0),
        spread_down.mid,
        lambda: input_back(0, 1),
        lambda: context_back(1),
        lambda: attend_back(1, 0),
        lambda: attend_back(1, 1),
        sum_input[0][0].mid_x,
        sum_input[0][0].mid_y,
        lambda: attend_back(1, 2),
        lambda: input_back(1, 0),
        late_sum.start,
        reduce_expand.relay,
        sum_input[0][1].mid_x,
        sum_input[0][1].mid_y,
        lambda: input_back(1, 1),
        attend_weights,
        sum_input[1][0].mid_x,
        sum_input[1][0].mid_y,
        lambda: late_sum.step(0),
        lambda: finish_input(0, 0),
        lambda: early_sum.step(1),
        lambda: finish_input(0, 1),
        sum_input[1][1].mid_x,
        sum_input[1][1].mid_y,
        reduce_attn.join,
        lambda: early_sum.step(2),
        lambda: finish_input(1, 0),
        spread_expand.start,
        lambda: late_sum.step(1),
        lambda: finish_input(1, 1),
        lambda: early_sum.step(3),
        lambda: late_sum.step(2),
        reduce_attn.relay,
        spread_expand.mid,
        lambda: late_sum.step(3),
        lambda: early_sum.step(4),
        finish_attn,
        lambda: late_sum.step(4),
        finish,
    ]
    for step in steps:
        step()


def result_kernel(
    ga_ref, gf_ref, early_ref, late_ref, out_in, ig_in,
    out_ref, ig_ref, pw_ref, pb_ref, ow_ref, ob_ref, g1_ref, s1_ref,
    ew_ref, eb_ref, dw_ref, db_ref, g2_ref, s2_ref,
    gf_in, out_buf, ig_buf, ew_out, dw_out, in_sems, out_sems,
):
    loads = [pltpu.make_async_copy(gf_ref.at[n], gf_in.at[n], in_sems.at[n]) for n in range(4)]
    loads.append(pltpu.make_async_copy(out_in, out_buf, in_sems.at[4]))
    loads.append(pltpu.make_async_copy(ig_in, ig_buf, in_sems.at[5]))
    stores = [
        pltpu.make_async_copy(src, dst, out_sems.at[n])
        for n, (src, dst) in enumerate(
            ((out_buf, out_ref), (ig_buf, ig_ref), (ew_out, ew_ref), (dw_out, dw_ref))
        )
    ]
    for copy in loads:
        copy.start()
    core = lax.axis_index("head")
    UB = gf_ref.shape[2] // 3
    HW = 3 * HEAD
    for n in range(4):
        loads[n].wait()
        for kind in (0, 1):
            ew_out[:, kind, n * UB : n * UB + UB] = gf_in[n, :, kind * UB : kind * UB + UB].astype(F32)
        dw_out[:, n * UB : n * UB + UB] = gf_in[n, :, 2 * UB : 3 * UB].astype(F32)
    stores[2].start()
    stores[3].start()
    for n in (0, 1):
        loads[4 + n].wait()
        stores[n].start()
    sides = [
        jnp.concatenate([ga_ref[parity, 0], ga_ref[parity, 1]], axis=1).astype(F32)
        for parity in (0, 1)
    ]
    for kind in range(4):
        cols = slice(kind * HW, kind * HW + HW)
        both = jnp.concatenate([sides[0][:, cols], sides[1][:, cols]], axis=1)
        if kind < 3:
            pw_ref[kind] = both
        else:
            ow_ref[...] = both
    D = early_ref.shape[1]
    for kind in (0, 1):
        first, second = late_ref[2 * kind : 2 * kind + 1], late_ref[2 * kind + 1 : 2 * kind + 2]
        pair = jnp.where(core == 0, first, second)
        pb_ref[kind : kind + 1, 0:HW] = pair[:, 0:HW]
        pb_ref[kind : kind + 1, HW : 2 * HW] = pair[:, D // 2 : D // 2 + HW]
        for h in (0, 1):
            low, high = 6 + 2 * kind + h, 10 + 2 * kind + h
            row = jnp.where(core == 0, early_ref[low : low + 1, :], early_ref[high : high + 1, :])
            eb_ref[kind : kind + 1, h * D : h * D + D] = row
    for row, ref in enumerate((ob_ref, g1_ref, s1_ref, db_ref, g2_ref, s2_ref)):
        ref[...] = early_ref[row : row + 1, :].reshape(D)
    for copy in stores:
        copy.wait()


def planes(
    layer_input,
    sequence_lengths,
    alibi_slopes,
    project_weight,
    project_bias,
    output_weight,
    output_bias,
    first_gain,
    first_shift,
    expand_weight,
    expand_bias,
    down_weight,
    down_bias,
    second_gain,
    second_shift,
    layer_cotangent,
):
    batches, tokens, width = layer_input.shape
    units = expand_weight.shape[2]
    shard = project_weight.shape[0]
    half_width = project_weight.shape[2]
    rows = 4 * tokens
    unit = units // 4
    vmem = pl.BlockSpec(memory_space=pltpu.VMEM)
    hbm = pl.BlockSpec(memory_space=pl.ANY)
    smem = pl.BlockSpec(memory_space=pltpu.SMEM)
    dma = pltpu.SemaphoreType.DMA
    full = pltpu.VMEM((8, tokens, width), BF)
    head = pltpu.VMEM((6, rows, HEAD), BF)
    own = pltpu.VMEM((2, tokens, width), F32)
    hidden = pltpu.VMEM((8, tokens, 2 * unit), BF)
    halves = pltpu.VMEM((4, 2, 2, tokens, width // 2), BF)
    shape = jax.ShapeDtypeStruct
    outs = pl.pallas_call(
        layer_kernel,
        out_shape=(
            shape((batches, tokens, width), BF),
            shape((batches, tokens, width), F32),
            shape((2, 2, shard, half_width), BF),
            shape((4, shard, 3 * unit), BF),
            shape((16, width), F32),
            shape((8, width), F32),
        ),
        in_specs=[vmem] * 4 + [hbm] * 2 + [smem] * 2 + [vmem] * 8,
        out_specs=(vmem,) * 6,
        scratch_shapes=[
            full, full, full, full,
            pltpu.VMEM((width, width), BF),
            pltpu.VMEM((2, width, 2 * unit), BF),
            pltpu.VMEM((width, 2 * unit), BF),
            pltpu.VMEM((2, 16, units), F32),
            pltpu.VMEM((shard, width), BF),
            pltpu.VMEM((2, 8, tokens, width), BF),
            halves, halves, halves,
            head, head, head, head,
            pltpu.VMEM((6, rows, rows), BF),
            pltpu.VMEM((6, rows, HEAD), F32),
            pltpu.VMEM((8, tokens, 3 * HEAD), BF),
            pltpu.VMEM((8, tokens, 9 * HEAD), BF),
            pltpu.VMEM((3, rows, rows), BF),
            pltpu.VMEM((3, 3, rows, HEAD), BF),
            pltpu.VMEM((2, rows, rows), F32),
            hidden, hidden, hidden,
            pltpu.VMEM((2, 8, tokens, 2 * unit), BF),
            pltpu.VMEM((8, unit), F32),
            own, own,
            pltpu.VMEM((2, tokens, 1), F32),
            own, own,
            pltpu.VMEM((2, width, unit), BF),
            pltpu.VMEM((width, unit), BF),
            pltpu.VMEM((4, shard, unit), BF),
            pltpu.VMEM((2, width, 2 * unit), BF),
            pltpu.VMEM((width, 2 * unit), BF),
            pltpu.VMEM((4, shard, 2 * unit), BF),
            pltpu.VMEM((2, width, half_width), BF),
            pltpu.VMEM((width, half_width), BF),
            pltpu.VMEM((4, shard, half_width), BF),
            pltpu.VMEM((shard, half_width), BF),
            pltpu.VMEM((10, 16, width), F32),
            pltpu.VMEM((10, 8, width), F32),
            pltpu.VMEM((3, 8, 128), F32),
            dma((4, 2, 2, 4)), dma((4, 2, 2, 4)),
            dma((4, 2, 2, 6)), dma((4, 2, 2, 6)),
            dma((2,)),
            dma((5, 2)), dma((5, 2)),
            dma((2, 4, 2)), dma((2, 4, 2)),
            dma((5,)),
            dma((3,)), dma((3,)),
            dma((3,)), dma((3,)),
            dma((3, 4)), dma((3, 4)),
            dma((3, 4)), dma((4, 4)),
            dma((5,)), dma((5,)),
            dma((5,)), dma((5,)),
            dma((2, 2)), dma((2, 2)),
        ],
        compiler_params=pltpu.CompilerParams(
            collective_id=0, has_side_effects=True, vmem_limit_bytes=VMEM_BYTES
        ),
        name="encoder_layer",
    )(
        layer_input, layer_cotangent, jnp.transpose(project_weight, (1, 0, 2)), output_weight.T,
        jnp.transpose(expand_weight, (1, 0, 2)), down_weight.T, jnp.transpose(sequence_lengths, (2, 1, 0)), alibi_slopes,
        project_bias, expand_bias, output_bias, first_gain, first_shift, down_bias, second_gain, second_shift,
    )
    layer_output, input_gradient, attn, feed, early, late = outs
    vector = shape((width,), F32)
    results = pl.pallas_call(
        result_kernel,
        out_shape=(
            shape((batches, tokens, width), BF),
            shape((batches, tokens, width), F32),
            shape((3, shard, half_width), F32),
            shape(project_bias.shape, F32),
            shape((shard, half_width), F32),
            vector, vector, vector,
            shape(expand_weight.shape, F32),
            shape(expand_bias.shape, F32),
            shape((shard, units), F32),
            vector, vector, vector,
        ),
        in_specs=[vmem, hbm, vmem, vmem, hbm, hbm],
        out_specs=(hbm,) * 2 + (vmem,) * 6 + (hbm, vmem, hbm) + (vmem,) * 3,
        scratch_shapes=[
            pltpu.VMEM(feed.shape, BF),
            pltpu.VMEM(layer_output.shape, BF),
            pltpu.VMEM(input_gradient.shape, F32),
            pltpu.VMEM(expand_weight.shape, F32),
            pltpu.VMEM((shard, units), F32),
            dma((6,)), dma((4,)),
        ],
        compiler_params=pltpu.CompilerParams(vmem_limit_bytes=VMEM_BYTES),
        name="gradient_results",
    )(attn, feed, early, late, layer_output, input_gradient)
    results = list(results)
    results[2] = jnp.transpose(results[2], (1, 0, 2))
    results[4] = results[4].T
    results[10] = results[10].T
    return tuple(results)


def fits(mesh):
    shape = dict(mesh.shape)
    return shape["dp"] == 4 and shape["blk"] == 4 and shape["head"] == 2


def solution(mesh):
    in_specs = (
        P(None, ("dp", "blk"), None),
        P(None, "dp", None),
        P("head"),
        P("dp", None, "head"),
        P(None, "head"),
        P("head", "dp"),
        P(),
        P(),
        P(),
        P("dp", None, "head"),
        P(None, "head"),
        P("head", "dp"),
        P(),
        P(),
        P(),
        P(None, ("dp", "blk"), None),
    )
    out_specs = (
        P(None, ("dp", "blk"), None),
        P(None, ("dp", "blk"), None),
        P("dp", None, "head"),
        P(None, "head"),
        P("head", "dp"),
        P(),
        P(),
        P(),
        P("dp", None, "head"),
        P(None, "head"),
        P("head", "dp"),
        P(),
        P(),
        P(),
    )
    body = planes if fits(mesh) else general
    return jax.shard_map(body, mesh=mesh, in_specs=in_specs, out_specs=out_specs, check_vma=False)
```

```python
import functools
import math

import jax
import jax.numpy as jnp
from jax import lax
from jax.experimental import pallas as pl
from jax.experimental.pallas import tpu as pltpu
from jax.sharding import PartitionSpec as P

EPSILON = 1e-12
MASKED = -1e30


def shifted(value, axis, steps):
    count = lax.axis_size(axis)
    pairs = [(source, (source + steps) % count) for source in range(count)]
    return lax.ppermute(value, axis, pairs)


def normalize(rows, gain, shift):
    mean = jnp.mean(rows, axis=-1, keepdims=True)
    centered = rows - mean
    spread = jnp.mean(centered * centered, axis=-1, keepdims=True)
    return centered * lax.rsqrt(spread + EPSILON) * gain + shift


def gelu_product(gate_part, up_part):
    return jax.nn.gelu(gate_part, approximate=False) * up_part


def sequence_ids(lengths, positions):
    first = lengths[:, 0:1]
    second = first + lengths[:, 1:2]
    later = (positions[None, :] >= first).astype(jnp.int32)
    return later + (positions[None, :] >= second).astype(jnp.int32)


def block_scores(query, keys, slopes, query_pos, key_pos, query_seq, key_seq):
    scale = query.shape[-1] ** (-0.5)
    raw = jnp.einsum("mqhd,mkhd->mhqk", query, keys, preferred_element_type=jnp.float32)
    distance = jnp.abs(query_pos[:, None] - key_pos[None, :]).astype(jnp.float32)
    scores = raw * scale - slopes[None, :, None, None] * distance[None, None]
    same = (query_seq[:, :, None] == key_seq[:, None, :])[:, None]
    return (jnp.where(same, scores, MASKED), same)


def forward_update(state, query, keys, values, slopes, query_pos, key_pos, query_seq, key_seq):
    top, total, accum = state
    scores, same = block_scores(query, keys, slopes, query_pos, key_pos, query_seq, key_seq)
    new_top = jnp.maximum(top, jnp.max(scores, axis=-1))
    weights = jnp.where(same, jnp.exp(scores - new_top[..., None]), 0.0)
    factor = jnp.exp(top - new_top)
    total = total * factor + jnp.sum(weights, axis=-1)
    update = jnp.einsum(
        "mhqk,mkhd->mqhd", weights.astype(jnp.bfloat16), values, preferred_element_type=jnp.float32
    )
    accum = accum * jnp.transpose(factor, (0, 2, 1))[..., None] + update
    return (new_top, total, accum)


def over_blocks(function, state, arrays, start):
    count_rows = arrays[0].shape[1]
    block = math.gcd(count_rows, 512)
    if block == count_rows:
        return function(state, arrays, start)

    def step(index, carry):
        offset = index * block
        blocks = tuple((lax.dynamic_slice_in_dim(item, offset, block, 1) for item in arrays))
        return function(carry, blocks, start + offset)

    return lax.fori_loop(0, count_rows // block, step, state)


def general(
    layer_input,
    sequence_lengths,
    alibi_slopes,
    project_weight,
    project_bias,
    output_weight,
    output_bias,
    first_gain,
    first_shift,
    expand_weight,
    expand_bias,
    down_weight,
    down_bias,
    second_gain,
    second_shift,
    layer_cotangent,
):
    batches, tokens, width = layer_input.shape
    heads = alibi_slopes.shape[0]
    local_width = project_weight.shape[2]
    head_size = local_width // heads
    units = expand_weight.shape[2]
    rows_all = batches * tokens
    scale = head_size ** (-0.5)
    project_full, output_full, expand_full, down_full = (
        lax.all_gather(project_weight, "dp", axis=0, tiled=True),
        lax.all_gather(output_weight, "dp", axis=1, tiled=True),
        lax.all_gather(expand_weight, "dp", axis=0, tiled=True),
        lax.all_gather(down_weight, "dp", axis=1, tiled=True),
    )
    lengths = sequence_lengths.reshape(batches, 3)
    cycle_index = lax.axis_index("blk")
    cycle_size = lax.axis_size("blk")
    own_pos = cycle_index * tokens + jnp.arange(tokens, dtype=jnp.int32)
    own_seq = sequence_ids(lengths, own_pos)

    def split_heads(item):
        return item.reshape(item.shape[0], item.shape[1], heads, head_size)

    flat_input = layer_input.reshape(rows_all, width)
    mixed = jnp.dot(
        flat_input, project_full.reshape(width, 3 * local_width), preferred_element_type=jnp.float32
    )
    query = (
        (mixed[:, :local_width] + project_bias[0])
        .astype(jnp.bfloat16)
        .reshape(batches, tokens, local_width)
    )
    keys = (
        mixed[:, local_width : 2 * local_width]
        .astype(jnp.bfloat16)
        .reshape(batches, tokens, local_width)
    )
    values = (
        (mixed[:, 2 * local_width :] + project_bias[1])
        .astype(jnp.bfloat16)
        .reshape(batches, tokens, local_width)
    )
    query_heads = split_heads(query)
    initial = (
        jnp.full((batches, heads, tokens), MASKED, jnp.float32),
        jnp.zeros((batches, heads, tokens), jnp.float32),
        jnp.zeros((batches, tokens, heads, head_size), jnp.float32),
    )

    def inner(carry, blocks, block_start):
        key_pos = block_start + jnp.arange(blocks[0].shape[1], dtype=jnp.int32)
        key_seq = sequence_ids(lengths, key_pos)
        return forward_update(
            carry,
            query_heads,
            split_heads(blocks[0]),
            split_heads(blocks[1]),
            alibi_slopes,
            own_pos,
            key_pos,
            own_seq,
            key_seq,
        )

    top, total, accum = over_blocks(
        inner,
        initial,
        (
            lax.all_gather(keys, "blk", axis=1, tiled=True),
            lax.all_gather(values, "blk", axis=1, tiled=True),
        ),
        jnp.int32(0),
    )
    context = accum / jnp.transpose(total, (0, 2, 1))[..., None]
    log_total = top + jnp.log(total)
    context_low = context.astype(jnp.bfloat16).reshape(rows_all, local_width)
    branch_part = jnp.dot(context_low, output_full, preferred_element_type=jnp.float32)
    branch = lax.psum(branch_part.astype(jnp.bfloat16), "head").astype(jnp.float32) + output_bias
    first_in = flat_input.astype(jnp.float32) + branch
    first_out, first_pull = jax.vjp(normalize, first_in, first_gain, first_shift)
    first_low = first_out.astype(jnp.bfloat16)
    expanded = jnp.dot(
        first_low, expand_full.reshape(width, 2 * units), preferred_element_type=jnp.float32
    )
    expanded = expanded + expand_bias.reshape(2 * units)
    hidden_act, gelu_pull = jax.vjp(gelu_product, expanded[:, :units], expanded[:, units:])
    hidden_low = hidden_act.astype(jnp.bfloat16)
    feed_part = jnp.dot(hidden_low, down_full, preferred_element_type=jnp.float32)
    feed = lax.psum(feed_part.astype(jnp.bfloat16), "head").astype(jnp.float32) + down_bias
    second_in = first_out + feed
    result, second_pull = jax.vjp(normalize, second_in, second_gain, second_shift)
    layer_output = result.astype(jnp.bfloat16).reshape(batches, tokens, width)
    grad_result = layer_cotangent.reshape(rows_all, width).astype(jnp.float32)
    grad_second, second_gain_grad, second_shift_grad = second_pull(grad_result)
    grad_feed = grad_second.astype(jnp.bfloat16)
    down_bias_grad = jnp.sum(grad_feed.astype(jnp.float32), axis=0)
    down_part = jnp.einsum("rf,rd->fd", hidden_low, grad_feed, preferred_element_type=jnp.float32)
    grad_hidden = jnp.einsum("rd,fd->rf", grad_feed, down_full, preferred_element_type=jnp.float32)
    grad_gate, grad_up = gelu_pull(grad_hidden)
    grad_expanded = jnp.concatenate([grad_gate, grad_up], axis=1).astype(jnp.bfloat16)
    expand_bias_grad = jnp.sum(grad_expanded.astype(jnp.float32), axis=0).reshape(2, units)
    expand_part = jnp.einsum(
        "rd,rf->df", first_low, grad_expanded, preferred_element_type=jnp.float32
    ).reshape(width, 2, units)
    first_back = jnp.einsum(
        "rf,df->rd",
        grad_expanded,
        expand_full.reshape(width, 2 * units),
        preferred_element_type=jnp.float32,
    )
    grad_first = grad_second + lax.psum(first_back.astype(jnp.bfloat16), "head").astype(jnp.float32)
    grad_first_in, first_gain_grad, first_shift_grad = first_pull(grad_first)
    grad_branch = grad_first_in.astype(jnp.bfloat16)
    output_bias_grad = jnp.sum(grad_branch.astype(jnp.float32), axis=0)
    output_part = jnp.einsum(
        "rc,rd->cd", context_low, grad_branch, preferred_element_type=jnp.float32
    )
    grad_context = jnp.einsum(
        "rd,cd->rc", grad_branch, output_full, preferred_element_type=jnp.float32
    )
    grad_context = grad_context.astype(jnp.bfloat16).reshape(batches, tokens, local_width)
    grad_heads = split_heads(grad_context)
    delta_rows = jnp.sum(grad_heads.astype(jnp.float32) * context, axis=-1)
    delta_heads = jnp.transpose(delta_rows, (0, 2, 1))
    zeros_heads = jnp.zeros((batches, tokens, heads, head_size), jnp.float32)
    zeros_flat = jnp.zeros((batches, tokens, local_width), jnp.float32)

    def cycle_step(carry, anchor):
        keys_now, values_now, grad_keys_now, grad_values_now, grad_query = carry
        key_pos = anchor * tokens + jnp.arange(tokens, dtype=jnp.int32)
        key_seq = sequence_ids(lengths, key_pos)
        keys_block = split_heads(keys_now)
        values_block = split_heads(values_now)
        scores, same = block_scores(
            query_heads, keys_block, alibi_slopes, own_pos, key_pos, own_seq, key_seq
        )
        weights = jnp.where(same, jnp.exp(scores - log_total[..., None]), 0.0)
        grad_prob = jnp.einsum(
            "mqhd,mkhd->mhqk", grad_heads, values_block, preferred_element_type=jnp.float32
        )
        grad_score = (weights * (grad_prob - delta_heads[..., None])).astype(jnp.bfloat16)
        grad_query = (
            grad_query
            + jnp.einsum(
                "mhqk,mkhd->mqhd", grad_score, keys_block, preferred_element_type=jnp.float32
            )
            * scale
        )
        key_term = (
            jnp.einsum(
                "mhqk,mqhd->mkhd", grad_score, query_heads, preferred_element_type=jnp.float32
            )
            * scale
        )
        value_term = jnp.einsum(
            "mhqk,mqhd->mkhd",
            weights.astype(jnp.bfloat16),
            grad_heads,
            preferred_element_type=jnp.float32,
        )
        grad_keys_now = grad_keys_now + key_term.reshape(grad_keys_now.shape)
        grad_values_now = grad_values_now + value_term.reshape(grad_values_now.shape)
        return (keys_now, values_now, grad_keys_now, grad_values_now, grad_query)

    def cycle_turn(index, carry):
        anchor = (cycle_index - index) % cycle_size
        updated = cycle_step(carry, anchor)
        moved = (
            shifted(updated[0], "blk", 1),
            shifted(updated[1], "blk", 1),
            shifted(updated[2].astype(jnp.bfloat16), "blk", 1).astype(jnp.float32),
            shifted(updated[3].astype(jnp.bfloat16), "blk", 1).astype(jnp.float32),
        )
        return (
            moved[0],
            moved[1],
            moved[2].astype(jnp.float32),
            moved[3].astype(jnp.float32),
            updated[4],
        )

    carry = lax.fori_loop(
        0, cycle_size - 1, cycle_turn, (keys, values, zeros_flat, zeros_flat, zeros_heads)
    )
    final = cycle_step(carry, (cycle_index + 1) % cycle_size)
    returned = (
        shifted(final[2].astype(jnp.bfloat16), "blk", 1).astype(jnp.float32),
        shifted(final[3].astype(jnp.bfloat16), "blk", 1).astype(jnp.float32),
    )
    grad_keys = returned[0].astype(jnp.float32)
    grad_values = returned[1].astype(jnp.float32)
    grad_query = final[4].reshape(batches, tokens, local_width)
    grad_mixed = jnp.concatenate(
        [
            grad_query.reshape(rows_all, local_width),
            grad_keys.reshape(rows_all, local_width),
            grad_values.reshape(rows_all, local_width),
        ],
        axis=1,
    ).astype(jnp.bfloat16)
    project_bias_grad = jnp.stack(
        [
            jnp.sum(grad_mixed[:, :local_width].astype(jnp.float32), axis=0),
            jnp.sum(grad_mixed[:, 2 * local_width :].astype(jnp.float32), axis=0),
        ]
    )
    project_part = jnp.einsum(
        "rd,rc->dc", flat_input, grad_mixed, preferred_element_type=jnp.float32
    ).reshape(width, 3, local_width)
    input_back = jnp.einsum(
        "rc,dc->rd",
        grad_mixed,
        project_full.reshape(width, 3 * local_width),
        preferred_element_type=jnp.float32,
    )
    input_gradient = grad_first_in + lax.psum(input_back.astype(jnp.bfloat16), "head").astype(
        jnp.float32
    )
    shards = (
        lax.psum_scatter(
            project_part.astype(jnp.bfloat16), "dp", scatter_dimension=0, tiled=True
        ).astype(jnp.float32),
        lax.psum_scatter(
            output_part.astype(jnp.bfloat16), "dp", scatter_dimension=1, tiled=True
        ).astype(jnp.float32),
        lax.psum_scatter(
            expand_part.astype(jnp.bfloat16), "dp", scatter_dimension=0, tiled=True
        ).astype(jnp.float32),
        lax.psum_scatter(
            down_part.astype(jnp.bfloat16), "dp", scatter_dimension=1, tiled=True
        ).astype(jnp.float32),
    )
    totals = (
        lax.psum(shards[0].astype(jnp.bfloat16), "blk").astype(jnp.float32),
        lax.psum(shards[1].astype(jnp.bfloat16), "blk").astype(jnp.float32),
        lax.psum(shards[2].astype(jnp.bfloat16), "blk").astype(jnp.float32),
        lax.psum(shards[3].astype(jnp.bfloat16), "blk").astype(jnp.float32),
    )
    small = lax.psum(
        (
            project_bias_grad,
            output_bias_grad,
            first_gain_grad,
            first_shift_grad,
            expand_bias_grad,
            down_bias_grad,
            second_gain_grad,
            second_shift_grad,
        ),
        ("dp", "blk"),
    )
    return (
        layer_output,
        input_gradient.reshape(batches, tokens, width),
        totals[0],
        small[0],
        totals[1],
        small[1],
        small[2],
        small[3],
        totals[2],
        small[4],
        totals[3],
        small[5],
        small[6],
        small[7],
    )


MESH = pl.DeviceIdType.MESH
BF = jnp.bfloat16
F32 = jnp.float32
FAR = 1e33
VMEM_BYTES = 63 << 20
HEAD = 64


def dot(a, b):
    return lax.dot_general(a, b, (((1,), (0,)), ((), ())), preferred_element_type=F32)


def dot_nt(a, b):
    return lax.dot_general(a, b, (((1,), (1,)), ((), ())), preferred_element_type=F32)


def dot_tn(a, b):
    return lax.dot_general(a, b, (((0,), (0,)), ((), ())), preferred_element_type=F32)


def column_sum(rows):
    return jnp.sum(rows, axis=0, keepdims=True)


def row_mean(rows):
    return jnp.mean(rows, axis=-1, keepdims=True)


def standardize(rows):
    centered = rows - row_mean(rows)
    inverse = lax.rsqrt(row_mean(centered * centered) + EPSILON)
    return centered * inverse, inverse


def standardize_back(grad, normal, inverse):
    return inverse * (grad - row_mean(grad) - normal * row_mean(grad * normal))


def layer_kernel(
    x_ref, cot_ref, pw_ref, ow_ref, ew_ref, dw_ref, len_ref, slope_ref, pb_ref, eb_ref,
    ob_ref, g1_ref, s1_ref, db_ref, g2_ref, s2_ref,
    out_ref, ig_ref, ga_ref, gf_ref, early_ref, late_ref,
    x_full, first_full, feed_full, branch_full,
    w_attn, w_gu, w_down, packs, own_attn,
    part, r1x, r1y, r2,
    q_s, k_s, v_s, g_s, p_s, ctx_s, ctx_cat, dqkv, ds_s, dq_s, far_s,
    act_s, upd_s, hid_s, dgu_s, eb_acc,
    first_own, n1_s, a1_s, gr2_s, gr1_s,
    dwd, dwd_in, dwd_z, dwe, dwe_in, dwe_z, dwa, dwa_in, dwa_z, fin_a,
    early, late, slope_s, out_s, ig_s, gf_s, ew_s, own_gu,
    ag_ss, ag_rs, rs_ss, rs_rs, pk_sem, wa_ss, wa_rs, wf_ss, wf_rs, wl_sem, wc_ss, wc_rs,
    gc_ss, gc_rs, gz_ss, gz_rs, gp_ss, gp_rs, ge_ss, ge_rs, gl_ss, gl_rs, io_ss, io_rs, st_sem,
):
    z, b, c = lax.axis_index("dp"), lax.axis_index("blk"), lax.axis_index("head")
    half, odd = b // 2, b % 2
    xor = jnp.bitwise_xor
    other = 1 - c
    bx, by, bd = xor(b, 1), xor(b, 2), xor(b, 3)
    sib, xdev, ydev = (z, b, other), (z, bx, c), (z, by, c)
    near, far, opposite = ((xor(z, k), b, c) for k in (1, 2, 3))
    inner = jnp.logical_or(z == 1, z == 2)
    outer = jnp.logical_not(inner)
    T = x_ref.shape[1]
    D = x_ref.shape[2]
    H2 = D // 2
    ROWS = 4 * T
    DZ = pw_ref.shape[1]
    UB = dw_ref.shape[1] // 4
    HW = 3 * HEAD
    S = T // 2
    lo, hi, both = pl.ds(0, H2), pl.ds(H2, H2), pl.ds(0, D)

    def chunk(index, size):
        return pl.ds(pl.multiple_of(index * size, size), size)

    mine_z, near_z, far_z, opposite_z = (chunk(xor(z, k), DZ) for k in range(4))
    started = []
    earlier = {}
    stored = []

    def store(src, dst, index):
        copy = pltpu.make_async_copy(src, dst, st_sem.at[index])
        copy.start()
        stored.append(copy)

    def raw(src, dst, ss, rs, dev):
        return pltpu.make_async_remote_copy(
            src_ref=src, dst_ref=dst, send_sem=ss, recv_sem=rs, device_id=dev, device_id_type=MESH
        )

    class Copy:
        def __init__(self, *args):
            self.copy = raw(*args)
            self.sent = self.received = False

        def start(self):
            self.copy.start()
            started.append(self)

        def wait_recv(self):
            self.copy.wait_recv()
            self.received = True

        def wait_send(self):
            self.copy.wait_send()
            self.sent = True

        def finish(self):
            if not self.received:
                self.wait_recv()
            if not self.sent:
                self.wait_send()

    partners = [(z, xor(b, k), cc) for k in (1, 2, 3) for cc in (c, other)] + [sib]
    partners += [(xor(z, k), b, cc) for k in (1, 2, 3) for cc in (c, other)]
    barrier = pltpu.get_barrier_semaphore()
    for dev in partners:
        pl.semaphore_signal(barrier, inc=1, device_id=dev, device_id_type=MESH)

    class Gather:
        def __init__(self, full, phase, m, r):
            ss, rs = ag_ss.at[m, r], ag_rs.at[m, r]
            part_rows = pl.ds(r * S, S)
            self.before = earlier.get((Gather, m, r))
            earlier[Gather, m, r] = self

            def send(slot, lanes, index, dev):
                rows = full.at[m * 4 + slot, part_rows, lanes]
                return Copy(rows, rows, ss.at[index], rs.at[index], dev)

            self.cx, self.cy = send(b, both, 0, xdev), send(b, both, 1, ydev)
            self.fx, self.fy = send(bx, lo, 2, ydev), send(by, hi, 3, xdev)

        def start(self):
            if self.before is not None:
                for copy in (self.before.cx, self.before.cy, self.before.fx, self.before.fy):
                    copy.wait_send()
            self.cx.start()
            self.cy.start()

        def mid_x(self):
            self.cx.wait_recv()
            self.fx.start()

        def mid_y(self):
            self.cy.wait_recv()
            self.fy.start()

        def end(self):
            for copy in (self.fx, self.fy):
                if not copy.received:
                    copy.wait_recv()

    class Scatter:
        def __init__(self, phase, m, r):
            ss, rs = rs_ss.at[m, r], rs_rs.at[m, r]
            self.before = earlier.get((Scatter, m, r))
            earlier[Scatter, m, r] = self
            buf = part.at[phase % 2]
            rows = pl.ds(r * S, S)
            ix, iy, i2 = r1x.at[phase, m], r1y.at[phase, m], r2.at[phase, m]
            self.own, self.sx, self.sy = m * 4 + b, m * 4 + bx, m * 4 + by
            self.buf, self.rows, self.ix, self.iy, self.i2 = buf, rows, ix, iy, i2

            def send(slot, lanes, into, at, index, dev):
                src = buf.at[m * 4 + slot, rows, lanes]
                return Copy(src, into.at[at, rows], ss.at[index], rs.at[index], dev)

            self.xd = send(bd, lo, ix, 1, 0, xdev)
            self.yd = send(bd, hi, iy, 1, 1, ydev)
            self.xo = send(bx, lo, ix, 0, 2, xdev)
            self.yo = send(by, hi, iy, 0, 3, ydev)
            self.y2 = send(by, lo, i2, 0, 4, ydev)
            self.x2 = send(bx, hi, i2, 1, 5, xdev)

        def start(self):
            if self.before is not None:
                self.before.drain()
            for copy in (self.xd, self.yd, self.xo, self.yo):
                copy.start()

        def add(self, slot, lanes, term):
            value = self.buf[slot, self.rows, lanes].astype(F32) + term[1, self.rows].astype(F32)
            self.buf[slot, self.rows, lanes] = value.astype(BF)

        def mid_x(self):
            self.xd.wait_recv()
            self.add(self.sy, lo, self.ix)
            self.y2.start()

        def mid_y(self):
            self.yd.wait_recv()
            self.add(self.sx, hi, self.iy)
            self.x2.start()

        def end(self):
            for copy in (self.xo, self.yo, self.y2, self.x2):
                copy.wait_recv()
            mine = self.buf[self.own, self.rows].astype(F32)
            rows = self.rows
            low = mine[:, :H2] + self.ix[0, rows].astype(F32) + self.i2[0, rows].astype(F32)
            high = mine[:, H2:] + self.iy[0, rows].astype(F32) + self.i2[1, rows].astype(F32)
            return jnp.concatenate([low, high], axis=1)

        def drain(self):
            for copy in (self.xd, self.yd, self.xo, self.yo, self.y2, self.x2):
                if not copy.sent:
                    copy.wait_send()

    def chunks(kind, *args):
        return [[kind(*args, m, r) for r in (0, 1)] for m in (0, 1)]

    gather_x, gather_first = chunks(Gather, x_full, 0), chunks(Gather, first_full, 1)
    gather_feed, gather_branch = chunks(Gather, feed_full, 2), chunks(Gather, branch_full, 3)
    sum_branch, sum_feed = chunks(Scatter, 0), chunks(Scatter, 1)
    sum_first, sum_input = chunks(Scatter, 2), chunks(Scatter, 3)

    class Column:
        def __init__(self, pieces, ss, rs):
            self.pieces, self.ss, self.rs = pieces, ss, rs

        def copy(self, dz, index, src, dst, dev):
            return raw(src, dst, self.ss.at[dz, index], self.rs.at[dz, index], dev)

        def copies(self, index):
            src, place_at, core = self.pieces[index]
            for dz in (2, 1, 3):
                yield self.copy(dz, index, src, place_at(mine_z), (xor(z, dz), b, core))

        def send(self):
            for index in range(len(self.pieces)):
                to_far, to_near, _ = self.copies(index)
                to_far.start()
                to_near.start()

        def send_opposite(self, index):
            pl.when(inner)(list(self.copies(index))[2].start)

        def sent(self):
            for index in range(len(self.pieces)):
                to_far, to_near, to_opposite = self.copies(index)
                to_far.wait_send()
                to_near.wait_send()
                pl.when(inner)(to_opposite.wait_send)

        def arrival(self, dz, index):
            src, place_at, _ = self.pieces[index]
            self.copy(dz, index, src, place_at(mine_z), near).wait_recv()

        def passing(self, index):
            rows = self.pieces[index][1](far_z)
            return raw(rows, rows, self.ss.at[0, index], self.rs.at[3, index], near)

        def relay(self, index):
            self.arrival(2, index)
            pl.when(inner)(self.passing(index).start)

        def pass_on(self, index):
            self.relay(index)
            self.send_opposite(index)

        def relayed(self, index):
            pl.when(inner)(self.passing(index).wait_send)

        def rest(self, index):
            self.arrival(1, index)
            self.arrival(3, index)

    def attn_place(k):
        return lambda rows: w_attn.at[rows, pl.ds(k * H2, H2)]

    attn_pieces = [(own_attn.at[:, pl.ds(k * H2, H2)], attn_place(k), k) for k in (0, 1)]
    attn_column = Column(attn_pieces, wa_ss, wa_rs)
    attn_own = []
    for index, (src, place_at, core) in enumerate(attn_pieces):
        dst = place_at(mine_z)
        cross = raw(src, dst, wa_ss.at[4, index], wa_rs.at[4, index], sib)
        local = pltpu.make_async_copy(src, dst, wl_sem.at[index])
        attn_own.append((cross, local))
    gu_column = Column(
        [
            (own_gu.at[0], lambda rows: w_gu.at[c, rows, pl.ds(0, UB)], c),
            (own_gu.at[1], lambda rows: w_gu.at[c, rows, pl.ds(UB, UB)], c),
        ],
        wf_ss.at[0],
        wf_rs.at[0],
    )
    down_column = Column(
        [(dw_ref.at[:, chunk(b, UB)], lambda rows: w_down.at[rows, chunk(c, UB)], c)],
        wf_ss.at[1],
        wf_rs.at[1],
    )
    feed_own = []
    for index, (src, place_at, _) in enumerate(gu_column.pieces + down_column.pieces):
        feed_own.append(pltpu.make_async_copy(src, place_at(mine_z), wl_sem.at[2 + index]))

    expand_copy = pltpu.make_async_copy(ew_ref.at[:, :, chunk(b, UB)], ew_s, wl_sem.at[5])

    def relay_out():
        expand_copy.wait()
        for kind in (0, 1):
            own_gu[kind] = ew_s[:, kind, :].astype(F32).astype(BF)
            feed_own[kind].start()

    def prepare():
        expand_copy.start()
        feed_own[2].start()
        shards = [pw_ref[kind] for kind in range(3)] + [ow_ref[...]]
        own_attn[...] = jnp.concatenate(
            [jnp.where(odd == 0, item[:, 0:HW], item[:, HW : 2 * HW]) for item in shards], axis=1
        )
        for m in (0, 1):
            x_full[m * 4 + b] = x_ref[2 * c + m]
        for row in (0, 1):
            packs[c, row : row + 1, :] = eb_ref[row : row + 1, :]
            packs[c, row + 2 : row + 3, 0:H2] = pb_ref[row : row + 1, :]
        for i in range(6):
            packs[c, 10 + i : 11 + i, 0:128] = jnp.full((1, 128), slope_ref[i], F32)
        pl.semaphore_wait(barrier, len(partners))

    def start_attn():
        @pl.when(c == half)
        def _():
            attn_column.send()
            for index, (cross, local) in enumerate(attn_own):
                pl.when(c == index)(local.start)
                pl.when(c != index)(cross.start)

        pack_copy.start()

    pack_copy = Copy(packs.at[c], packs.at[c], pk_sem.at[0], pk_sem.at[1], sib)

    def constants():
        for m in (0, 1):
            start_one = len_ref[0, 0, 2 * c + m]
            start_two = start_one + len_ref[1, 0, 2 * c + m]
            for rb in range(4):
                rows = lax.broadcasted_iota(jnp.int32, (T, ROWS), 0) + rb * T
                cols = lax.broadcasted_iota(jnp.int32, (T, ROWS), 1)
                seq_r = (rows >= start_one).astype(jnp.int32) + (rows >= start_two).astype(jnp.int32)
                seq_c = (cols >= start_one).astype(jnp.int32) + (cols >= start_two).astype(jnp.int32)
                distance = jnp.abs(rows - cols).astype(F32)
                far_s[m, pl.ds(rb * T, T), :] = jnp.where(seq_r == seq_c, distance, FAR)
        early[...] = jnp.zeros_like(early)
        late[...] = jnp.zeros_like(late)
        eb_acc[...] = jnp.zeros_like(eb_acc)
        pack_copy.wait_recv()
        for i in range(3):
            low, high = packs[half, 10 + i : 11 + i, 0:128], packs[half, 13 + i : 14 + i, 0:128]
            slope_s[i] = jnp.broadcast_to(jnp.where(odd == 0, low, high), (8, 128))

    def relay_attn():
        for index in (0, 1):
            pl.when(c == index)(functools.partial(attn_column.relay, index))
        for index in (0, 1):
            pl.when(c == half)(functools.partial(attn_column.send_opposite, index))

    lanes = w_attn.at[:, chunk(c, H2)]
    attn_share = Copy(lanes, lanes, wc_ss.at[0], wc_rs.at[0], sib)

    def share_attn():
        for index, (cross, local) in enumerate(attn_own):

            @pl.when(c == index)
            def _():
                pl.when(c == half)(local.wait)
                pl.when(c != half)(cross.wait_recv)
                attn_column.rest(index)

        attn_share.start()

    def vector(ref):
        return ref[...].reshape(1, D)

    def project(m):
        if m == 0:
            attn_share.wait_recv()
        for r in (0, 1):
            gather_x[m][r].end()
        biases = packs[half, 2:4, 0:H2]
        biases = jnp.where(odd == 0, biases[:, 0:HW], biases[:, HW : 2 * HW])

        def rows_of(t, _):
            rows = x_full[pl.ds(m * 4 + t * 2, 2)].reshape(2 * T, D)
            at = pl.ds(pl.multiple_of(t * 2 * T, 2 * T), 2 * T)
            mixed = dot(rows, w_attn[:, 0 : 3 * HW])
            query = (mixed[:, 0:HW] + biases[0:1]).astype(BF) * jnp.asarray(0.125, BF)
            keys = mixed[:, HW : 2 * HW].astype(BF)
            values = (mixed[:, 2 * HW : 3 * HW] + biases[1:2]).astype(BF)
            for i in range(3):
                cols = slice(i * HEAD, i * HEAD + HEAD)
                q_s[m * 3 + i, at, :] = query[:, cols]
                k_s[m * 3 + i, at, :] = keys[:, cols]
                v_s[m * 3 + i, at, :] = values[:, cols]
            return 0

        lax.fori_loop(0, 2, rows_of, 0)

    def attend(m, r):
        heads = [m * 3 + i for i in range(3)]

        def one(slot, _):
            at = pl.ds(pl.multiple_of(slot * T + r * S, S), S)
            reach = far_s[m, at, :]
            scores = [dot_nt(q_s[h, at, :], k_s[h]) for h in heads]
            scores = [item - slope_s[i][0:1, 0:1] * reach for i, item in enumerate(scores)]
            tops = [jnp.max(item, axis=-1, keepdims=True) for item in scores]
            weights = [jnp.exp(item - top) for item, top in zip(scores, tops)]
            totals = [jnp.sum(item, axis=-1, keepdims=True) for item in weights]
            probs = [(item * (1.0 / total)).astype(BF) for item, total in zip(weights, totals)]
            for h, item in zip(heads, probs):
                p_s[h, at, :] = item
                ctx_s[h, at, :] = dot(item, v_s[h])
            return 0

        lax.fori_loop(0, 4, one, 0)
        for slot in range(4):
            at = pl.ds(slot * T + r * S, S)
            cat = jnp.concatenate([ctx_s[m * 3 + i, at, :].astype(BF) for i in range(3)], axis=1)
            ctx_cat[m * 4 + slot, pl.ds(r * S, S), :] = cat
        total = sum_branch[m][r]
        put(total, m, r, dot_nt(take(ctx_cat, m, r), w_attn[:, 3 * HW : 4 * HW]))
        total.start()

    def put(total, m, r, rows):
        total.buf[m * 4 : m * 4 + 4, pl.ds(r * S, S), :] = rows.astype(BF).reshape(4, S, D)

    def take(refs, m, r):
        rows = refs[m * 4 : m * 4 + 4, pl.ds(r * S, S), :]
        return rows.reshape(4 * S, rows.shape[2])

    def keep(refs, m, r, lanes, rows):
        refs[m * 4 : m * 4 + 4, pl.ds(r * S, S), lanes] = rows.reshape(4, S, rows.shape[1])

    def first_norm(m, r):
        at = pl.ds(r * S, S)
        rows = x_ref[2 * c + m, at, :].astype(F32) + sum_branch[m][r].end() + vector(ob_ref)
        normal, inverse = standardize(rows)
        first = normal * vector(g1_ref) + vector(s1_ref)
        n1_s[m, at, :], a1_s[m, at, :] = normal, inverse
        first_own[m, at, :] = first
        first_full[m * 4 + b, at, :] = first.astype(BF)
        gather_first[m][r].start()

    def feed_forward(m, r):
        if m + r == 0:
            share_gu.wait_recv()
        gather_first[m][r].end()
        rows = take(first_full, m, r)
        for g in (0, 1):
            cols = pl.ds(g * UB, UB)
            bias = packs[g, 0:2, chunk(b, UB)]
            pair = dot(rows, w_gu[g])
            gate = pair[:, :UB] + bias[0:1]
            up = pair[:, UB:] + bias[1:2]
            cdf = 0.5 + 0.5 * lax.erf(gate * 0.7071067811865476)
            act = gate * cdf
            slope = cdf + gate * (jnp.exp(-0.5 * gate * gate) * 0.3989422804014327)
            keep(hid_s, m, r, cols, (act * up).astype(BF))
            keep(act_s, m, r, cols, act.astype(BF))
            keep(upd_s, m, r, cols, (up * slope).astype(BF))

    def feed_out(m, r):
        if m + r == 0:
            share_down.wait_recv()
        total = sum_feed[m][r]
        put(total, m, r, dot_nt(take(hid_s, m, r), w_down[...]))
        total.start()

    def add_early(row, rows):
        early[0, row : row + 1, :] += column_sum(rows)

    def second_norm(m, r):
        at = pl.ds(r * S, S)
        rows = first_own[m, at, :] + sum_feed[m][r].end() + vector(db_ref)
        normal, inverse = standardize(rows)
        out_s[m, at, :] = (normal * vector(g2_ref) + vector(s2_ref)).astype(BF)
        grad = cot_ref[2 * c + m, at, :].astype(F32)
        back = standardize_back(grad * vector(g2_ref), normal, inverse)
        gr2_s[m, at, :] = back
        low = back.astype(BF)
        feed_full[m * 4 + b, at, :] = low
        gather_feed[m][r].start()
        add_early(4, grad * normal)
        add_early(5, grad)
        add_early(3, low.astype(F32))
        if r == 1:
            send_rows(out_s, out_ref, 0, m)

    def feed_backward(m, r):
        gather_feed[m][r].end()
        sum_branch[m][r].drain()
        hidden = dot(take(feed_full, m, r), w_down[...])
        dgate = (hidden * take(upd_s, m, r).astype(F32)).astype(BF)
        dup = (hidden * take(act_s, m, r).astype(F32)).astype(BF)
        for g in (0, 1):
            cols = slice(g * UB, g * UB + UB)
            keep(dgu_s.at[g], m, r, pl.ds(0, UB), dgate[:, cols])
            keep(dgu_s.at[g], m, r, pl.ds(UB, UB), dup[:, cols])
        back = dot_nt(take(dgu_s.at[0], m, r), w_gu[0]) + dot_nt(take(dgu_s.at[1], m, r), w_gu[1])
        total = sum_first[m][r]
        put(total, m, r, back)
        total.start()
        for g in (0, 1):
            cols = slice(g * UB, g * UB + UB)
            eb_acc[2 * g : 2 * g + 1, :] += column_sum(dgate[:, cols].astype(F32))
            eb_acc[2 * g + 1 : 2 * g + 2, :] += column_sum(dup[:, cols].astype(F32))

    def down_weights():
        for m, r in ((0, 0), (0, 1), (1, 0), (1, 1)):
            gather_feed[m][r].end()

        def cols_of(t, _):
            at = chunk(t, 256)
            rows = feed_full[:, :, at].reshape(2 * ROWS, 256)
            down = dot_tn(rows, hid_s[...].reshape(2 * ROWS, 2 * UB)).astype(BF)
            for g in (0, 1):
                dwd[g, at, :] = down[:, g * UB : g * UB + UB]
            return 0

        lax.fori_loop(0, D // 256, cols_of, 0)

    def expand_weights(t):
        at = pl.ds(t * 256, 256)
        rows = first_full[:, :, at].reshape(2 * ROWS, 256)

        def units_of(g, _):
            dwe[g, at, :] = dot_tn(rows, dgu_s[g].reshape(2 * ROWS, 2 * UB)).astype(BF)
            return 0

        lax.fori_loop(0, 2, units_of, 0)

    def first_back(m, r):
        at = pl.ds(r * S, S)
        grad = gr2_s[m, at, :] + sum_first[m][r].end()
        normal = n1_s[m, at, :]
        back = standardize_back(grad * vector(g1_ref), normal, a1_s[m, at, :])
        gr1_s[m, at, :] = back
        low = back.astype(BF)
        branch_full[m * 4 + b, at, :] = low
        gather_branch[m][r].start()
        add_early(1, grad * normal)
        add_early(2, grad)
        add_early(0, low.astype(F32))

    def context_back(m):
        for r in (0, 1):
            gather_branch[m][r].end()
        def rows_of(t, _):
            at = pl.ds(pl.multiple_of(t * 2 * T, 2 * T), 2 * T)
            rows = branch_full[pl.ds(m * 4 + t * 2, 2)].reshape(2 * T, D)
            grads = dot(rows, w_attn[:, 3 * HW : 4 * HW]).astype(BF)
            for i in range(3):
                g_s[m * 3 + i, at, :] = grads[:, i * HEAD : i * HEAD + HEAD]
            return 0

        lax.fori_loop(0, 2, rows_of, 0)

    def attend_back(m, part):
        heads = [m * 3 + i for i in range(3)]

        def block(rb, _):
            at = chunk(rb, T)
            rows = [g_s[h, at, :] for h in heads]
            terms = [dot_nt(item, v_s[h]) for item, h in zip(rows, heads)]
            deltas = [
                jnp.sum(item.astype(F32) * ctx_s[h, at, :], axis=-1, keepdims=True)
                for item, h in zip(rows, heads)
            ]
            for i, h in enumerate(heads):
                score = (p_s[h, at, :].astype(F32) * (terms[i] - deltas[i])).astype(BF)
                ds_s[i, at, :] = score
                dq_s[0, i, at, :] = (dot(score, k_s[h]) * 0.125).astype(BF)
            return 0

        if part < 2:
            lax.fori_loop(2 * part, 2 * part + 2, block, 0)
        else:
            for i, h in enumerate(heads):
                dq_s[1, i] = dot_tn(q_s[h], ds_s[i]).T.astype(BF)
                dq_s[2, i] = dot_tn(g_s[h], p_s[h]).T.astype(BF)

    def input_back(m, r):
        if r == 0:
            for kind in range(3):
                cat = jnp.concatenate([dq_s[kind, i] for i in range(3)], axis=1)
                dqkv[m * 4 : m * 4 + 4, :, kind * HW : kind * HW + HW] = cat.reshape(4, T, HW)
                if kind != 1:
                    sums = column_sum(cat.astype(F32))
                    for h in (0, 1):
                        lanes = pl.ds(pl.multiple_of(odd * H2, H2), HW)
                        late[0, kind + h : kind + h + 1, lanes] += jnp.where(half == h, sums, 0.0)
        total = sum_input[m][r]
        sum_feed[m][r].drain()
        put(total, m, r, dot_nt(take(dqkv, m, r), w_attn[:, 0 : 3 * HW]))
        total.start()

    def attend_weights():
        def cols_of(t, _):
            at = chunk(t, 256)
            rows = x_full[:, :, at].reshape(2 * ROWS, 256)
            grads = dot_tn(rows, dqkv[...].reshape(2 * ROWS, 3 * HW)).astype(BF)
            dwa[0, at, :] = grads[:, 0:H2]
            dwa[1, at, 0:HW] = grads[:, H2 : 3 * HW]
            rows = branch_full[:, :, at].reshape(2 * ROWS, 256)
            outs = dot_tn(rows, ctx_cat[...].reshape(2 * ROWS, HW)).astype(BF)
            dwa[1, at, HW : 2 * HW] = outs
            return 0

        lax.fori_loop(0, D // 256, cols_of, 0)
        reduce_attn.swap.start()

    class Reduce:
        def __init__(self, index, buf, incoming, zin):
            self.buf, self.incoming, self.zin = buf, incoming, zin
            self.swap = Copy(buf.at[other], incoming, gc_ss.at[index], gc_rs.at[index], sib)

            def push(rows, slot, dev):
                ss, rs = gz_ss.at[index, slot], gz_rs.at[index, slot]
                return raw(buf.at[c, rows, :], zin.at[slot], ss, rs, dev)

            self.to_near = push(near_z, 0, near)
            self.to_far = push(far_z, 1, far)
            self.to_opposite = push(opposite_z, 2, opposite)
            self.by_near = push(opposite_z, 3, near)

        def join(self):
            self.swap.wait_recv()

            def add(rows):
                mine = self.buf[c, rows, :].astype(F32)
                self.buf[c, rows, :] = (mine + self.incoming[rows, :].astype(F32)).astype(BF)

            add(opposite_z)
            pl.when(outer)(self.by_near.start)
            pl.when(inner)(self.to_opposite.start)
            add(far_z)
            pl.when(outer)(self.to_far.start)
            add(near_z)
            self.to_near.start()
            add(mine_z)

        def relay(self):
            @pl.when(inner)
            def _():
                self.by_near.wait_recv()
                mine = self.buf[c, far_z, :].astype(F32)
                self.buf[c, far_z, :] = (mine + self.zin[3].astype(F32)).astype(BF)
                self.to_far.start()

        def total(self, put):
            self.to_near.wait_recv()
            self.to_far.wait_recv()

            def value():
                low = self.buf[c, mine_z, :].astype(F32)
                return low + self.zin[0].astype(F32) + self.zin[1].astype(F32)

            @pl.when(inner)
            def _():
                self.to_opposite.wait_recv()
                put((value() + self.zin[2].astype(F32)).astype(BF))

            @pl.when(outer)
            def _():
                put(value().astype(BF))

        def sent(self):
            self.to_near.wait_send()
            self.to_far.wait_send()
            pl.when(inner)(self.to_opposite.wait_send)
            pl.when(outer)(self.by_near.wait_send)

    reduce_down = Reduce(0, dwd, dwd_in, dwd_z)
    reduce_expand = Reduce(1, dwe, dwe_in, dwe_z)
    reduce_attn = Reduce(2, dwa, dwa_in, dwa_z)

    class Everywhere:
        def __init__(self, buf, ss, rs, result):
            devices = [near, far, sib, xdev, ydev]
            self.buf, self.result = buf, result
            self.copies = [
                Copy(buf.at[2 * i], buf.at[2 * i + 1], ss.at[i], rs.at[i], dev)
                for i, dev in enumerate(devices)
            ]

        def start(self):
            self.copies[0].start()

        def step(self, i):
            self.copies[i].wait_recv()
            value = self.buf[2 * i] + self.buf[2 * i + 1]
            if i + 1 < len(self.copies):
                self.buf[2 * i + 2] = value
                self.copies[i + 1].start()
            else:
                self.result[...] = value

    early_sum = Everywhere(early, ge_ss, ge_rs, early_ref)
    late_sum = Everywhere(late, gl_ss, gl_rs, late_ref)

    def early_start():
        for g in (0, 1):
            for kind in (0, 1):
                row = 6 + (2 * g + kind) * 2
                values = eb_acc[2 * g + kind : 2 * g + kind + 1, :]
                for h in (0, 1):
                    at = slice(row + h, row + h + 1)
                    early[0, at, chunk(odd, UB)] = jnp.where(half == h, values, 0.0)
        early_sum.start()

    share_gu = Copy(w_gu.at[c], w_gu.at[c], wc_ss.at[1], wc_rs.at[1], sib)
    down_lanes = w_down.at[:, chunk(c, UB)]
    share_down = Copy(down_lanes, down_lanes, wc_ss.at[2], wc_rs.at[2], sib)

    def take_weights(column, own, share):
        for index in range(len(column.pieces)):
            column.rest(index)
        for copy in own:
            copy.wait()
        share.start()

    def send_rows(buf, refs, index, m):
        rows = refs.at[2 * c + m]
        Copy(buf.at[m], rows, io_ss.at[index, m], io_rs.at[index, m], sib).start()
        store(buf.at[m], rows, 2 * index + m)

    def finish_input(m, r):
        at = pl.ds(r * S, S)
        ig_s[m, at, :] = gr1_s[m, at, :] + sum_input[m][r].end()
        if r == 1:
            send_rows(ig_s, ig_ref, 1, m)

    class Spread:
        def __init__(self, index, reduce, lanes):
            self.index, self.reduce, self.lanes = index, reduce, lanes
            ss, rs = gp_ss.at[index], gp_rs.at[index]

            def send(src, slot, rows, at, dev):
                piece = gf_ref.at[slot, rows, lanes]
                return Copy(piece if src is None else src, piece, ss.at[at], rs.at[at], dev)

            every, top, bottom = pl.ds(0, DZ), pl.ds(0, DZ // 2), pl.ds(DZ // 2, DZ // 2)
            self.mine = gf_s.at[:, lanes]
            self.cx = send(self.mine, b, every, 0, xdev)
            self.cy = send(self.mine, b, every, 1, ydev)
            self.fx, self.fy = send(None, bx, top, 2, ydev), send(None, by, bottom, 3, xdev)

        def start(self):
            def put_sum(value):
                gf_s[:, self.lanes] = value

            self.reduce.total(put_sum)
            self.cx.start()
            self.cy.start()
            store(self.mine, gf_ref.at[b, :, self.lanes], 4 + self.index)

        def mid(self):
            self.cx.wait_recv()
            self.fx.start()
            self.cy.wait_recv()
            self.fy.start()

    spread_down = Spread(0, reduce_down, pl.ds(2 * UB, UB))
    spread_expand = Spread(1, reduce_expand, pl.ds(0, 2 * UB))

    def finish_attn():
        def put_fin(value):
            fin_a[...] = value

        reduce_attn.total(put_fin)
        slot, rs = ga_ref.at[odd, c], gp_rs.at[2 + odd, c]
        copies = [raw(fin_a, slot, gp_ss.at[2, k], rs, (z, xor(b, k), half)) for k in (3, 1, 2)]
        cross = raw(fin_a, slot, gp_ss.at[2, 0], rs, sib)
        for copy in copies:
            copy.start()
        pl.when(c != half)(cross.start)

        local = pltpu.make_async_copy(fin_a, slot, st_sem.at[6])
        pl.when(c == half)(local.start)
        for parity in (0, 1):
            for core in (0, 1):
                own = jnp.logical_and(c == half, jnp.logical_and(odd == parity, c == core))
                rs = gp_rs.at[2 + parity, core]
                arrival = raw(fin_a, ga_ref.at[parity, core], gp_ss.at[2, 0], rs, sib)
                pl.when(jnp.logical_not(own))(arrival.wait_recv)
        pl.when(c != half)(cross.wait_send)
        pl.when(c == half)(local.wait)
        for copy in copies:
            copy.wait_send()

    def finish():
        @pl.when(c == half)
        def _():
            attn_column.sent()
            for index, (cross, _) in enumerate(attn_own):
                pl.when(c != index)(cross.wait_send)

        for index in (0, 1):
            pl.when(c == index)(functools.partial(attn_column.relayed, index))
        for column in (gu_column, down_column):
            column.sent()
            for index in range(len(column.pieces)):
                column.relayed(index)
        for item in (reduce_down, reduce_expand, reduce_attn):
            item.sent()
        for copy in started:
            copy.finish()
        for copy in stored:
            copy.wait()

    steps = [
        prepare,
        start_attn,
        gather_x[0][0].start,
        gather_x[0][1].start,
        gather_x[1][0].start,
        gather_x[1][1].start,
        constants,
        relay_out,
        gather_x[0][0].mid_x,
        gather_x[0][0].mid_y,
        gather_x[0][1].mid_x,
        gather_x[0][1].mid_y,
        relay_attn,
        gather_x[1][0].mid_x,
        gather_x[1][0].mid_y,
        gather_x[1][1].mid_x,
        gather_x[1][1].mid_y,
        share_attn,
        gu_column.send,
        lambda: project(0),
        lambda: attend(0, 0),
        lambda: attend(0, 1),
        lambda: gu_column.pass_on(0),
        sum_branch[0][0].mid_x,
        sum_branch[0][0].mid_y,
        lambda: project(1),
        lambda: attend(1, 0),
        sum_branch[0][1].mid_x,
        sum_branch[0][1].mid_y,
        lambda: gu_column.pass_on(1),
        down_column.send,
        lambda: first_norm(0, 0),
        lambda: attend(1, 1),
        sum_branch[1][0].mid_x,
        sum_branch[1][0].mid_y,
        lambda: first_norm(0, 1),
        lambda: take_weights(gu_column, feed_own[:2], share_gu),
        gather_first[0][0].mid_x,
        gather_first[0][0].mid_y,
        sum_branch[1][1].mid_x,
        sum_branch[1][1].mid_y,
        lambda: first_norm(1, 0),
        gather_first[0][1].mid_x,
        gather_first[0][1].mid_y,
        lambda: down_column.pass_on(0),
        lambda: feed_forward(0, 0),
        lambda: first_norm(1, 1),
        gather_first[1][0].mid_x,
        gather_first[1][0].mid_y,
        lambda: feed_forward(0, 1),
        lambda: take_weights(down_column, feed_own[2:], share_down),
        gather_first[1][1].mid_x,
        gather_first[1][1].mid_y,
        lambda: feed_forward(1, 0),
        lambda: feed_out(0, 0),
        lambda: feed_out(0, 1),
        lambda: feed_out(1, 0),
        lambda: feed_forward(1, 1),
        lambda: feed_out(1, 1),
        sum_feed[0][0].mid_x,
        sum_feed[0][0].mid_y,
        sum_feed[0][1].mid_x,
        sum_feed[0][1].mid_y,
        sum_feed[1][0].mid_x,
        sum_feed[1][0].mid_y,
        sum_feed[1][1].mid_x,
        sum_feed[1][1].mid_y,
        lambda: second_norm(0, 0),
        lambda: second_norm(0, 1),
        lambda: second_norm(1, 0),
        lambda: second_norm(1, 1),
        gather_feed[0][0].mid_x,
        gather_feed[0][0].mid_y,
        gather_feed[0][1].mid_x,
        gather_feed[0][1].mid_y,
        gather_feed[1][0].mid_x,
        gather_feed[1][0].mid_y,
        gather_feed[1][1].mid_x,
        gather_feed[1][1].mid_y,
        lambda: feed_backward(0, 0),
        lambda: feed_backward(0, 1),
        down_weights,
        sum_first[0][0].mid_x,
        sum_first[0][0].mid_y,
        reduce_down.swap.start,
        lambda: feed_backward(1, 0),
        sum_first[0][1].mid_x,
        sum_first[0][1].mid_y,
        lambda: feed_backward(1, 1),
        lambda: first_back(0, 0),
        reduce_down.join,
        sum_first[1][0].mid_x,
        sum_first[1][0].mid_y,
        lambda: expand_weights(0),
        lambda: expand_weights(1),
        sum_first[1][1].mid_x,
        sum_first[1][1].mid_y,
        lambda: first_back(0, 1),
        lambda: expand_weights(2),
        reduce_expand.swap.start,
        reduce_down.relay,
        gather_branch[0][0].mid_x,
        gather_branch[0][0].mid_y,
        lambda: first_back(1, 0),
        lambda: first_back(1, 1),
        early_start,
        reduce_expand.join,
        gather_branch[0][1].mid_x,
        gather_branch[0][1].mid_y,
        spread_down.start,
        lambda: early_sum.step(0),
        gather_branch[1][0].mid_x,
        gather_branch[1][0].mid_y,
        gather_branch[1][1].mid_x,
        gather_branch[1][1].mid_y,
        lambda: context_back(0),
        lambda: attend_back(0, 0),
        lambda: attend_back(0, 1),
        reduce_expand.relay,
        spread_down.mid,
        lambda: attend_back(0, 2),
        lambda: input_back(0, 0),
        lambda: input_back(0, 1),
        lambda: context_back(1),
        lambda: attend_back(1, 0),
        lambda: attend_back(1, 1),
        sum_input[0][0].mid_x,
        sum_input[0][0].mid_y,
        lambda: attend_back(1, 2),
        sum_input[0][1].mid_x,
        sum_input[0][1].mid_y,
        lambda: input_back(1, 0),
        late_sum.start,
        lambda: input_back(1, 1),
        lambda: finish_input(0, 0),
        attend_weights,
        sum_input[1][0].mid_x,
        sum_input[1][0].mid_y,
        lambda: finish_input(0, 1),
        lambda: early_sum.step(1),
        spread_expand.start,
        sum_input[1][1].mid_x,
        sum_input[1][1].mid_y,
        lambda: late_sum.step(0),
        reduce_attn.join,
        lambda: finish_input(1, 0),
        lambda: early_sum.step(2),
        lambda: late_sum.step(1),
        lambda: late_sum.step(2),
        reduce_attn.relay,
        spread_expand.mid,
        lambda: finish_input(1, 1),
        lambda: early_sum.step(3),
        lambda: late_sum.step(3),
        finish_attn,
        lambda: early_sum.step(4),
        lambda: late_sum.step(4),
        finish,
    ]
    for step in steps:
        step()


def result_kernel(
    ga_ref, gf_ref, early_ref, late_ref, out_in, ig_in,
    out_ref, ig_ref, pw_ref, pb_ref, ow_ref, ob_ref, g1_ref, s1_ref,
    ew_ref, eb_ref, dw_ref, db_ref, g2_ref, s2_ref,
    gf_in, out_buf, ig_buf, ew_out, dw_out, in_sems, out_sems,
):
    loads = [pltpu.make_async_copy(gf_ref.at[n], gf_in.at[n], in_sems.at[n]) for n in range(4)]
    loads.append(pltpu.make_async_copy(out_in, out_buf, in_sems.at[4]))
    loads.append(pltpu.make_async_copy(ig_in, ig_buf, in_sems.at[5]))
    stores = [
        pltpu.make_async_copy(src, dst, out_sems.at[n])
        for n, (src, dst) in enumerate(
            ((out_buf, out_ref), (ig_buf, ig_ref), (ew_out, ew_ref), (dw_out, dw_ref))
        )
    ]
    for copy in loads:
        copy.start()
    core = lax.axis_index("head")
    UB = gf_ref.shape[2] // 3
    HW = 3 * HEAD
    for n in range(4):
        loads[n].wait()
        for kind in (0, 1):
            ew_out[:, kind, n * UB : n * UB + UB] = gf_in[n, :, kind * UB : kind * UB + UB].astype(F32)
        dw_out[:, n * UB : n * UB + UB] = gf_in[n, :, 2 * UB : 3 * UB].astype(F32)
    stores[2].start()
    stores[3].start()
    for n in (0, 1):
        loads[4 + n].wait()
        stores[n].start()
    sides = [
        jnp.concatenate([ga_ref[parity, 0], ga_ref[parity, 1]], axis=1).astype(F32)
        for parity in (0, 1)
    ]
    for kind in range(4):
        cols = slice(kind * HW, kind * HW + HW)
        both = jnp.concatenate([sides[0][:, cols], sides[1][:, cols]], axis=1)
        if kind < 3:
            pw_ref[kind] = both
        else:
            ow_ref[...] = both
    D = early_ref.shape[1]
    for kind in (0, 1):
        first, second = late_ref[2 * kind : 2 * kind + 1], late_ref[2 * kind + 1 : 2 * kind + 2]
        pair = jnp.where(core == 0, first, second)
        pb_ref[kind : kind + 1, 0:HW] = pair[:, 0:HW]
        pb_ref[kind : kind + 1, HW : 2 * HW] = pair[:, D // 2 : D // 2 + HW]
        for h in (0, 1):
            low, high = 6 + 2 * kind + h, 10 + 2 * kind + h
            row = jnp.where(core == 0, early_ref[low : low + 1, :], early_ref[high : high + 1, :])
            eb_ref[kind : kind + 1, h * D : h * D + D] = row
    for row, ref in enumerate((ob_ref, g1_ref, s1_ref, db_ref, g2_ref, s2_ref)):
        ref[...] = early_ref[row : row + 1, :].reshape(D)
    for copy in stores:
        copy.wait()


def planes(
    layer_input,
    sequence_lengths,
    alibi_slopes,
    project_weight,
    project_bias,
    output_weight,
    output_bias,
    first_gain,
    first_shift,
    expand_weight,
    expand_bias,
    down_weight,
    down_bias,
    second_gain,
    second_shift,
    layer_cotangent,
):
    batches, tokens, width = layer_input.shape
    units = expand_weight.shape[2]
    shard = project_weight.shape[0]
    half_width = project_weight.shape[2]
    rows = 4 * tokens
    unit = units // 4
    vmem = pl.BlockSpec(memory_space=pltpu.VMEM)
    hbm = pl.BlockSpec(memory_space=pl.ANY)
    smem = pl.BlockSpec(memory_space=pltpu.SMEM)
    dma = pltpu.SemaphoreType.DMA
    full = pltpu.VMEM((8, tokens, width), BF)
    head = pltpu.VMEM((6, rows, HEAD), BF)
    own = pltpu.VMEM((2, tokens, width), F32)
    hidden = pltpu.VMEM((8, tokens, 2 * unit), BF)
    halves = pltpu.VMEM((4, 2, 2, tokens, width // 2), BF)
    shape = jax.ShapeDtypeStruct
    outs = pl.pallas_call(
        layer_kernel,
        out_shape=(
            shape((batches, tokens, width), BF),
            shape((batches, tokens, width), F32),
            shape((2, 2, shard, half_width), BF),
            shape((4, shard, 3 * unit), BF),
            shape((16, width), F32),
            shape((8, width), F32),
        ),
        in_specs=[vmem] * 4 + [hbm] * 2 + [smem] * 2 + [vmem] * 8,
        out_specs=(hbm,) * 4 + (vmem,) * 2,
        scratch_shapes=[
            full, full, full, full,
            pltpu.VMEM((width, width), BF),
            pltpu.VMEM((2, width, 2 * unit), BF),
            pltpu.VMEM((width, 2 * unit), BF),
            pltpu.VMEM((2, 16, units), F32),
            pltpu.VMEM((shard, width), BF),
            pltpu.VMEM((2, 8, tokens, width), BF),
            halves, halves, halves,
            head, head, head, head,
            pltpu.VMEM((6, rows, rows), BF),
            pltpu.VMEM((6, rows, HEAD), F32),
            pltpu.VMEM((8, tokens, 3 * HEAD), BF),
            pltpu.VMEM((8, tokens, 9 * HEAD), BF),
            pltpu.VMEM((3, rows, rows), BF),
            pltpu.VMEM((3, 3, rows, HEAD), BF),
            pltpu.VMEM((2, rows, rows), F32),
            hidden, hidden, hidden,
            pltpu.VMEM((2, 8, tokens, 2 * unit), BF),
            pltpu.VMEM((8, unit), F32),
            own, own,
            pltpu.VMEM((2, tokens, 1), F32),
            own, own,
            pltpu.VMEM((2, width, unit), BF),
            pltpu.VMEM((width, unit), BF),
            pltpu.VMEM((4, shard, unit), BF),
            pltpu.VMEM((2, width, 2 * unit), BF),
            pltpu.VMEM((width, 2 * unit), BF),
            pltpu.VMEM((4, shard, 2 * unit), BF),
            pltpu.VMEM((2, width, half_width), BF),
            pltpu.VMEM((width, half_width), BF),
            pltpu.VMEM((4, shard, half_width), BF),
            pltpu.VMEM((shard, half_width), BF),
            pltpu.VMEM((10, 16, width), F32),
            pltpu.VMEM((10, 8, width), F32),
            pltpu.VMEM((3, 8, 128), F32),
            pltpu.VMEM((2, tokens, width), BF),
            own,
            pltpu.VMEM((shard, 3 * unit), BF),
            pltpu.VMEM((shard, 2, unit), BF),
            pltpu.VMEM((2, shard, unit), BF),
            dma((2, 2, 4)), dma((2, 2, 4)),
            dma((2, 2, 6)), dma((2, 2, 6)),
            dma((2,)),
            dma((5, 2)), dma((5, 2)),
            dma((2, 4, 2)), dma((2, 4, 2)),
            dma((6,)),
            dma((3,)), dma((3,)),
            dma((3,)), dma((3,)),
            dma((3, 4)), dma((3, 4)),
            dma((3, 4)), dma((4, 4)),
            dma((5,)), dma((5,)),
            dma((5,)), dma((5,)),
            dma((2, 2)), dma((2, 2)),
            dma((7,)),
        ],
        compiler_params=pltpu.CompilerParams(
            collective_id=0, has_side_effects=True, vmem_limit_bytes=VMEM_BYTES
        ),
        name="encoder_layer",
    )(
        layer_input, layer_cotangent, jnp.transpose(project_weight, (1, 0, 2)), output_weight.T,
        expand_weight, down_weight.T, jnp.transpose(sequence_lengths, (2, 1, 0)), alibi_slopes,
        project_bias, expand_bias, output_bias, first_gain, first_shift, down_bias, second_gain, second_shift,
    )
    layer_output, input_gradient, attn, feed, early, late = outs
    vector = shape((width,), F32)
    results = pl.pallas_call(
        result_kernel,
        out_shape=(
            shape((batches, tokens, width), BF),
            shape((batches, tokens, width), F32),
            shape((3, shard, half_width), F32),
            shape(project_bias.shape, F32),
            shape((shard, half_width), F32),
            vector, vector, vector,
            shape(expand_weight.shape, F32),
            shape(expand_bias.shape, F32),
            shape((shard, units), F32),
            vector, vector, vector,
        ),
        in_specs=[vmem, hbm, vmem, vmem, hbm, hbm],
        out_specs=(hbm,) * 2 + (vmem,) * 6 + (hbm, vmem, hbm) + (vmem,) * 3,
        scratch_shapes=[
            pltpu.VMEM(feed.shape, BF),
            pltpu.VMEM(layer_output.shape, BF),
            pltpu.VMEM(input_gradient.shape, F32),
            pltpu.VMEM(expand_weight.shape, F32),
            pltpu.VMEM((shard, units), F32),
            dma((6,)), dma((4,)),
        ],
        compiler_params=pltpu.CompilerParams(vmem_limit_bytes=VMEM_BYTES),
        name="gradient_results",
    )(attn, feed, early, late, layer_output, input_gradient)
    results = list(results)
    results[2] = jnp.transpose(results[2], (1, 0, 2))
    results[4] = results[4].T
    results[10] = results[10].T
    return tuple(results)


def fits(mesh):
    shape = dict(mesh.shape)
    return shape["dp"] == 4 and shape["blk"] == 4 and shape["head"] == 2


def solution(mesh):
    in_specs = (
        P(None, ("dp", "blk"), None),
        P(None, "dp", None),
        P("head"),
        P("dp", None, "head"),
        P(None, "head"),
        P("head", "dp"),
        P(),
        P(),
        P(),
        P("dp", None, "head"),
        P(None, "head"),
        P("head", "dp"),
        P(),
        P(),
        P(),
        P(None, ("dp", "blk"), None),
    )
    out_specs = (
        P(None, ("dp", "blk"), None),
        P(None, ("dp", "blk"), None),
        P("dp", None, "head"),
        P(None, "head"),
        P("head", "dp"),
        P(),
        P(),
        P(),
        P("dp", None, "head"),
        P(None, "head"),
        P("head", "dp"),
        P(),
        P(),
        P(),
    )
    body = planes if fits(mesh) else general
    return jax.shard_map(body, mesh=mesh, in_specs=in_specs, out_specs=out_specs, check_vma=False)
```
